32 devices in a mesh: dp: 8 (over y, x, core), seq: 4 (over z).
Axes of the slice: x: 2, y: 2, z: 4, core: 2. Of those that a mesh axis runs over, the one named last changes fastest.
Arguments:
- patches_a: bfloat16 [8, 576, 768], P('dp', 'seq'), may hold values from -6 to 6
- class_a: bfloat16 [8, 768], P('dp'), may hold values from -6 to 6
- patches_b: bfloat16 [16, 224, 768], P('dp', 'seq'), may hold values from -6 to 6
- class_b: bfloat16 [16, 768], P('dp'), may hold values from -6 to 6
- count_a: int32 [8], P('dp'), may hold values from 288 to 576, as said below
- count_b: int32 [16], P('dp'), may hold values from 98 to 196, as said below
- index_a: int32 [577, 577], replicated, may hold values from 92 to 2303, as said below
- index_b: int32 [225, 225], replicated, may hold values from 92 to 2303, as said below
- cot_a: bfloat16 [8, 576, 768], P('dp', 'seq'), may hold values from -6 to 6
- cot_class_a: bfloat16 [8, 768], P('dp'), may hold values from -6 to 6
- cot_b: bfloat16 [16, 224, 768], P('dp', 'seq'), may hold values from -6 to 6
- cot_class_b: bfloat16 [16, 768], P('dp'), may hold values from -6 to 6
- qkv_weight: float32 [768, 2304], P(('dp', 'seq')), may hold values from -0.21875 to 0.21875
- qkv_momentum: float32 [768, 2304], P(('dp', 'seq')), may hold values from -256 to 256
- qkv_average: float32 [768, 2304], P(('dp', 'seq')), may hold values from -0.21875 to 0.21875
- out_weight: float32 [768, 768], P(('dp', 'seq')), may hold values from -1.75 to 1.75
- out_momentum: float32 [768, 768], P(('dp', 'seq')), may hold values from -56 to 56
- out_average: float32 [768, 768], P(('dp', 'seq')), may hold values from -1.75 to 1.75
- up_weight: float32 [768, 3072], P(('dp', 'seq')), may hold values from -0.21875 to 0.21875
- up_momentum: float32 [768, 3072], P(('dp', 'seq')), may hold values from -128 to 128
- up_average: float32 [768, 3072], P(('dp', 'seq')), may hold values from -0.21875 to 0.21875
- down_weight: float32 [3072, 768], P(('dp', 'seq')), may hold values from -0.109375 to 0.109375
- down_momentum: float32 [3072, 768], P(('dp', 'seq')), may hold values from -256 to 256
- down_average: float32 [3072, 768], P(('dp', 'seq')), may hold values from -0.109375 to 0.109375
- table_weight: float32 [2304, 12], P(('dp', 'seq')), may hold values from -5 to 5
- table_momentum: float32 [2304, 12], P(('dp', 'seq')), may hold values from -80 to 80
- table_average: float32 [2304, 12], P(('dp', 'seq')), may hold values from -5 to 5
- vector_weight: float32 [10752], P(('dp', 'seq')), may hold values from -0.7 to 1.5, as said below
- vector_momentum: float32 [10752], P(('dp', 'seq')), may hold values from -256 to 256
- vector_average: float32 [10752], P(('dp', 'seq')), may hold values from -0.7 to 1.5, as said below
Outputs:
- out_a: float32 [8, 576, 768], P('dp', 'seq')
- out_class_a: float32 [8, 768], P('dp')
- out_b: float32 [16, 224, 768], P('dp', 'seq')
- out_class_b: float32 [16, 768], P('dp')
- grad_a: float32 [8, 576, 768], P('dp', 'seq')
- grad_class_a: float32 [8, 768], P('dp')
- grad_b: float32 [16, 224, 768], P('dp', 'seq')
- grad_class_b: float32 [16, 768], P('dp')
- qkv_weight_new: float32 [768, 2304], P(('dp', 'seq'))
- qkv_momentum_new: float32 [768, 2304], P(('dp', 'seq'))
- qkv_average_new: float32 [768, 2304], P(('dp', 'seq'))
- out_weight_new: float32 [768, 768], P(('dp', 'seq'))
- out_momentum_new: float32 [768, 768], P(('dp', 'seq'))
- out_average_new: float32 [768, 768], P(('dp', 'seq'))
- up_weight_new: float32 [768, 3072], P(('dp', 'seq'))
- up_momentum_new: float32 [768, 3072], P(('dp', 'seq'))
- up_average_new: float32 [768, 3072], P(('dp', 'seq'))
- down_weight_new: float32 [3072, 768], P(('dp', 'seq'))
- down_momentum_new: float32 [3072, 768], P(('dp', 'seq'))
- down_average_new: float32 [3072, 768], P(('dp', 'seq'))
- table_weight_new: float32 [2304, 12], P(('dp', 'seq'))
- table_momentum_new: float32 [2304, 12], P(('dp', 'seq'))
- table_average_new: float32 [2304, 12], P(('dp', 'seq'))
- vector_weight_new: float32 [10752], P(('dp', 'seq'))
- vector_momentum_new: float32 [10752], P(('dp', 'seq'))
- vector_average_new: float32 [10752], P(('dp', 'seq'))
The draws below stay inside these ranges and needn't reach their ends.
Inputs may be any that keep to these rules, and one draw needn't show every extreme that they name: `count_a`: patches hold content up to the count, padding after it; at least one of all 384px images holds all 576. `count_b`: Likewise; at least one of all 224px images holds all 196. `index_a`: pairs of rows at the same offset on the patch grid name the same table row. `index_b`: pairs of patches at the same offset on the patch grid name the same table row, the one that index_a names for that offset; empty slots name rows too. `vector_weight`: gains and layer scales (g1, s1, g2, s2) lie within 0.5 to 1.5. `vector_average`: drawn as vector_weight.
All inputs are finite; a program needn't handle non-finite values.
Results may differ from the reference program's by a relative error of at most 0.013.
The reference program's roundings to bfloat16 on the way count: a program that leaves them out, or rounds other values in their place, can miss the bound.
Values may be sent and summed in bfloat16 or wider, within the bound.
No kernel may reach another device: no remote copies, remote signals or barrier semaphores. Data moves between devices by JAX's collectives and lax.ppermute only.
A program may use at most 192 MiB of HBM per device.

```python
import math
import jax
import jax.numpy as jnp
from jax import lax

D = 768
HEADS = 12
HEAD_DIM = 64
FF = 3072
SIDE_A = 24
SIDE_B = 14
TABLE = 2304
IMA = 1
IMB = 2
PAT_A = 576
PAT_B = 196
REAL_B = 49
BLK_B = 56
SLOT_B = 224
IMG_A = 8
IMG_B = 16
VEC = 10752
ROWS_ALL = 7768
N_DP = 8


def drawn_lengths(key, total_images, largest):
    first_key, second_key = jax.random.split(key)
    lengths_drawn = jax.random.randint(first_key, (total_images,), largest // 2, largest + 1)
    full_pick = jax.random.randint(second_key, (1,), 0, total_images)
    lengths_drawn = jnp.where(jnp.arange(total_images) == full_pick, largest, lengths_drawn)
    return lengths_drawn.astype(jnp.int32)


def draw_count_a(key, part):
    key = jax.random.fold_in(key, 21)
    return drawn_lengths(key, IMA * N_DP, PAT_A)


def draw_count_b(key, part):
    key = jax.random.fold_in(key, 22)
    return drawn_lengths(key, IMB * N_DP, PAT_B)


def relabel(key, grid_rows, grid_cols):
    reach_span = 2 * SIDE_A - 1
    offsets = reach_span * reach_span
    slot_count = grid_rows.shape[0]
    inner = (grid_rows[:, None] - grid_rows[None, :] + SIDE_A - 1) * reach_span + (grid_cols[:, None] - grid_cols[None, :] + SIDE_A - 1)
    top_row = jnp.full((1, slot_count), offsets, jnp.int32)
    left_col = jnp.full((slot_count, 1), offsets + 1, jnp.int32)
    corner = jnp.full((1, 1), offsets + 2, jnp.int32)
    raw_index = jnp.concatenate([jnp.concatenate([corner, top_row], axis=1), jnp.concatenate([left_col, inner.astype(jnp.int32)], axis=1)], axis=0)
    relabel_map = jax.random.permutation(key, offsets + 3).astype(jnp.int32) + (TABLE - offsets - 3)
    return relabel_map[raw_index].astype(jnp.int32)


def draw_index_a(key, part):
    patch_ids = jnp.arange(PAT_A, dtype=jnp.int32)
    return relabel(jax.random.fold_in(key, 5), patch_ids // SIDE_A, patch_ids % SIDE_A)


def draw_index_b(key, part):
    slot_ids = jnp.arange(SLOT_B, dtype=jnp.int32)
    patch_ids = jnp.minimum(slot_ids // BLK_B * REAL_B + slot_ids % BLK_B, PAT_B - 1)
    return relabel(jax.random.fold_in(key, 5), patch_ids // SIDE_B, patch_ids % SIDE_B)


def vector_law(key, gain_low, gain_high, shift_reach):
    first_key, second_key = jax.random.split(key)
    gains = jax.random.uniform(first_key, (VEC,), jnp.float32, gain_low, gain_high)
    shifts = jax.random.uniform(second_key, (VEC,), jnp.float32, -shift_reach, shift_reach)
    piece_of = jnp.arange(VEC) // D
    chosen = (piece_of == 0) | (piece_of == 5) | (piece_of == 6) | (piece_of == 9)
    return jnp.where(chosen, gains, shifts)


def draw_vector_weight(key, part):
    key = jax.random.fold_in(key, 31)
    return vector_law(key, 0.6, 1.4, 0.5)


def draw_vector_average(key, part):
    key = jax.random.fold_in(key, 32)
    return vector_law(key, 0.6, 1.4, 0.5)


def block_levels(rng, shape, cuts, low, high):
    def one(dim, blocks):
        heights = jax.random.uniform(jax.random.fold_in(jax.random.fold_in(rng, 6), dim), (blocks,), jnp.float32, low / len(cuts), high / len(cuts))
        return jnp.repeat(jnp.exp(heights), shape[dim] // blocks).reshape((-1,) + (1,) * (len(shape) - dim - 1))

    level = one(*cuts[0])
    for cut in cuts[1:]:
        level = level * one(*cut)
    return level


def bell_draw(own_key, shape, spread, bound, shards=(), held_as=jnp.bfloat16):
    values = spread * jax.random.normal(own_key, shape, jnp.float32)
    if shards:
        values = values * block_levels(own_key, shape, shards, -0.22, 0.18)
    return jnp.clip(values, -bound, bound).astype(held_as)


def setup_inputs(seed: int = 0) -> dict:
    streams_of = jax.random.split(jax.random.key(seed), 31)
    return {
        "patches_a": bell_draw(streams_of[0], (IMG_A, PAT_A, D), 1.0, 6.0, ((0, 8), (1, 4))),
        "class_a": bell_draw(streams_of[1], (IMG_A, D), 1.0, 6.0, ((0, 8),)),
        "patches_b": bell_draw(streams_of[2], (IMG_B, SLOT_B, D), 1.0, 6.0, ((0, 8), (1, 4))),
        "class_b": bell_draw(streams_of[3], (IMG_B, D), 1.0, 6.0, ((0, 8),)),
        "count_a": draw_count_a(jax.random.fold_in(streams_of[30], 71), 0),
        "count_b": draw_count_b(jax.random.fold_in(streams_of[30], 71), 0),
        "index_a": draw_index_a(jax.random.fold_in(streams_of[30], 71), 0),
        "index_b": draw_index_b(jax.random.fold_in(streams_of[30], 71), 0),
        "cot_a": bell_draw(streams_of[8], (IMG_A, PAT_A, D), 1.0, 6.0, ((0, 8), (1, 4))),
        "cot_class_a": bell_draw(streams_of[9], (IMG_A, D), 1.0, 6.0, ((0, 8),)),
        "cot_b": bell_draw(streams_of[10], (IMG_B, SLOT_B, D), 1.0, 6.0, ((0, 8), (1, 4))),
        "cot_class_b": bell_draw(streams_of[11], (IMG_B, D), 1.0, 6.0, ((0, 8),)),
        "qkv_weight": bell_draw(streams_of[12], (D, 3 * D), D ** -0.5, 0.21875, ((0, 32),), jnp.float32),
        "qkv_momentum": bell_draw(streams_of[13], (D, 3 * D), (0.5 * ROWS_ALL ** 0.5), 256.0, ((0, 32),), jnp.float32),
        "qkv_average": bell_draw(streams_of[14], (D, 3 * D), D ** -0.5, 0.21875, ((0, 32),), jnp.float32),
        "out_weight": bell_draw(streams_of[15], (D, D), (D // 64) ** -0.5, 1.75, ((0, 32),), jnp.float32),
        "out_momentum": bell_draw(streams_of[16], (D, D), (0.1 * ROWS_ALL ** 0.5), 56.0, ((0, 32),), jnp.float32),
        "out_average": bell_draw(streams_of[17], (D, D), (D // 64) ** -0.5, 1.75, ((0, 32),), jnp.float32),
        "up_weight": bell_draw(streams_of[18], (D, FF), D ** -0.5, 0.21875, ((0, 32),), jnp.float32),
        "up_momentum": bell_draw(streams_of[19], (D, FF), (0.25 * ROWS_ALL ** 0.5), 128.0, ((0, 32),), jnp.float32),
        "up_average": bell_draw(streams_of[20], (D, FF), D ** -0.5, 0.21875, ((0, 32),), jnp.float32),
        "down_weight": bell_draw(streams_of[21], (FF, D), FF ** -0.5, 0.109375, ((0, 32),), jnp.float32),
        "down_momentum": bell_draw(streams_of[22], (FF, D), (0.5 * ROWS_ALL ** 0.5), 256.0, ((0, 32),), jnp.float32),
        "down_average": bell_draw(streams_of[23], (FF, D), FF ** -0.5, 0.109375, ((0, 32),), jnp.float32),
        "table_weight": bell_draw(streams_of[24], (TABLE, HEADS), 1.0, 5.0, ((0, 32),), jnp.float32),
        "table_momentum": bell_draw(streams_of[25], (TABLE, HEADS), (3 * (N_DP * (IMA + IMB)) ** 0.5), 80.0, ((0, 32),), jnp.float32),
        "table_average": bell_draw(streams_of[26], (TABLE, HEADS), 1.0, 5.0, ((0, 32),), jnp.float32),
        "vector_weight": draw_vector_weight(jax.random.fold_in(streams_of[30], 71), 0),
        "vector_momentum": bell_draw(streams_of[28], (VEC,), (0.5 * ROWS_ALL ** 0.5), 256.0, ((0, 32),), jnp.float32),
        "vector_average": draw_vector_average(jax.random.fold_in(streams_of[30], 71), 0),
    }


@jax.custom_vjp
def low(v):
    return lax.optimization_barrier(v.astype(jnp.bfloat16)).astype(jnp.float32)

@jax.custom_vjp
def low_back(v):
    return v

def low_keep(v):
    return (low(v), None)

def low_pass(kept, grad):
    return (grad,)

def back_keep(v):
    return (v, None)

def back_low(kept, grad):
    return (low(grad),)
low.defvjp(low_keep, low_pass)
low_back.defvjp(back_keep, back_low)
EPS = 1e-06
NEG = -1e+30
MOMENTUM_DECAY = 0.5
AVERAGE_KEEP = 0.5
ROOT_HALF = 0.7071067811865476
step_rates = (0.04, 1.6, 0.08, 0.02, 3.0, 0.6)

def product(left, right):
    return jnp.dot(left, right, precision=lax.Precision.HIGHEST, preferred_element_type=jnp.float32)

def layer_norm(values, gain, shift):
    center = values - lax.optimization_barrier(jnp.mean(values, axis=-1, keepdims=True))
    return center * lax.rsqrt(lax.optimization_barrier(jnp.mean(center * center, axis=-1, keepdims=True)) + EPS) * gain + shift

def split_vector(vector):
    return [vector[piece * D:(piece + 1) * D] for piece in range(10)] + [vector[10 * D:]]

def split_heads(values):
    return values.reshape(values.shape[:-1] + (HEADS, HEAD_DIM))

def layer(params, tokens, key_live, bias_full):
    w_qkv, w_out, w_up, w_down, table_w, vector = params
    parts = split_vector(vector)
    n_img, length = (tokens.shape[0], tokens.shape[1])
    normed = low(layer_norm(tokens, parts[0], parts[1]))
    joined = product(normed.reshape(-1, D), w_qkv).reshape(n_img, length, 3 * D)
    queries = low(low_back((joined[..., :D] + parts[2]) * (1.0 / math.sqrt(HEAD_DIM))))
    key_rows = low(low_back(joined[..., D:2 * D]))
    value_rows = low(low_back(joined[..., 2 * D:] + parts[3]))
    scores = jnp.einsum('nqhd,nkhd->nhqk', split_heads(queries), split_heads(key_rows), precision=lax.Precision.HIGHEST) + bias_full[None]
    scores = low_back(jnp.where(key_live[:, None, None, :], scores, NEG))
    row_max = lax.optimization_barrier(jnp.max(scores, axis=-1, keepdims=True))
    exp_rows = jnp.exp(scores - row_max)
    probs = low(exp_rows / lax.optimization_barrier(jnp.sum(exp_rows, axis=-1, keepdims=True)))
    mixed = jnp.einsum('nhqk,nkhd->nqhd', probs, split_heads(value_rows), precision=lax.Precision.HIGHEST)
    mixed = low(low_back(mixed.reshape(n_img, length, D)))
    branch = low_back(product(mixed.reshape(-1, D), w_out).reshape(n_img, length, D) + parts[4])
    residual = tokens + parts[5] * branch
    normed_two = low(layer_norm(residual, parts[6], parts[7]))
    hidden = low_back(product(normed_two.reshape(-1, D), w_up).reshape(n_img, length, FF) + parts[10])
    gelu_out = low(0.5 * hidden * (1.0 + lax.erf(hidden * ROOT_HALF)))
    second = low_back(product(gelu_out.reshape(-1, FF), w_down).reshape(n_img, length, D) + parts[8])
    return residual + parts[9] * second

def run_group(params, patches, classes, live, index):
    bias_full = jnp.transpose(params[4][index], (2, 0, 1))

    def one_batch(item):
        patch_rows, class_rows, live_rows = item
        tokens = jnp.concatenate([class_rows[:, None, :], patch_rows], axis=1)
        key_live = jnp.concatenate([jnp.ones_like(live_rows[:, :1]), live_rows], axis=1)
        result = layer(params, tokens, key_live, bias_full)
        return (result[:, 1:], result[:, 0])
    return lax.map(jax.checkpoint(one_batch), (patches, classes, live))

def nesterov(master, moment, average, grad, step_rate):
    moment_new = MOMENTUM_DECAY * moment + grad
    master_new = master - step_rate * (grad + MOMENTUM_DECAY * moment_new)
    return (master_new, moment_new, AVERAGE_KEEP * average + (1.0 - AVERAGE_KEEP) * master_new)

def reference(patches_a, class_a, patches_b, class_b, count_a, count_b, index_a, index_b, cot_a, cot_class_a, cot_b, cot_class_b, qkv_weight, qkv_momentum, qkv_average, out_weight, out_momentum, out_average, up_weight, up_momentum, up_average, down_weight, down_momentum, down_average, table_weight, table_momentum, table_average, vector_weight, vector_momentum, vector_average):
    masters = (qkv_weight, out_weight, up_weight, down_weight, table_weight, vector_weight)
    params = tuple((master.astype(jnp.bfloat16).astype(jnp.float32) for master in masters))
    slots_a = jnp.arange(PAT_A, dtype=jnp.int32)
    live_a = (slots_a[None, :] < count_a[:, None]).reshape(N_DP, IMA, PAT_A)
    slots_b = jnp.arange(SLOT_B, dtype=jnp.int32)
    in_block = slots_b % BLK_B
    patch_b = slots_b // BLK_B * REAL_B + in_block
    live_b = ((in_block < REAL_B)[None, :] & (patch_b[None, :] < count_b[:, None])).reshape(N_DP, IMB, SLOT_B)
    rows_a = patches_a.astype(jnp.float32).reshape(N_DP, IMA, PAT_A, D)
    heads_a = class_a.astype(jnp.float32).reshape(N_DP, IMA, D)
    rows_b = patches_b.astype(jnp.float32).reshape(N_DP, IMB, SLOT_B, D)
    heads_b = class_b.astype(jnp.float32).reshape(N_DP, IMB, D)

    def forward(params, rows_a, heads_a, rows_b, heads_b):
        return (run_group(params, rows_a, heads_a, live_a, index_a), run_group(params, rows_b, heads_b, live_b, index_b))
    primal, pull_back = jax.vjp(forward, params, rows_a, heads_a, rows_b, heads_b)
    cot_rows_a = cot_a.astype(jnp.float32).reshape(N_DP, IMA, PAT_A, D) * live_a[..., None]
    cot_heads_a = cot_class_a.astype(jnp.float32).reshape(N_DP, IMA, D)
    cot_rows_b = cot_b.astype(jnp.float32).reshape(N_DP, IMB, SLOT_B, D) * live_b[..., None]
    cot_heads_b = cot_class_b.astype(jnp.float32).reshape(N_DP, IMB, D)
    grads = pull_back(((cot_rows_a, cot_heads_a), (cot_rows_b, cot_heads_b)))
    weight_grads = grads[0]
    states = ((qkv_weight, qkv_momentum, qkv_average), (out_weight, out_momentum, out_average), (up_weight, up_momentum, up_average), (down_weight, down_momentum, down_average), (table_weight, table_momentum, table_average), (vector_weight, vector_momentum, vector_average))
    updated = [nesterov(state[0], state[1], state[2], grad_w, rate_c / math.sqrt(ROWS_ALL)) for state, grad_w, rate_c in zip(states, weight_grads, step_rates)]
    return (primal[0][0].reshape(IMG_A, PAT_A, D), primal[0][1].reshape(IMG_A, D), primal[1][0].reshape(IMG_B, SLOT_B, D), primal[1][1].reshape(IMG_B, D), grads[1].reshape(IMG_A, PAT_A, D), grads[2].reshape(IMG_A, D), grads[3].reshape(IMG_B, SLOT_B, D), grads[4].reshape(IMG_B, D), updated[0][0], updated[0][1], updated[0][2], updated[1][0], updated[1][1], updated[1][2], updated[2][0], updated[2][1], updated[2][2], updated[3][0], updated[3][1], updated[3][2], updated[4][0], updated[4][1], updated[4][2], updated[5][0], updated[5][1], updated[5][2])
```

```python
import functools
import math

import jax
import jax.numpy as jnp
from jax import lax
from jax.experimental import pallas as pl
from jax.experimental.pallas import tpu as pltpu
from jax.sharding import Mesh
from jax.sharding import PartitionSpec as P

F32 = jnp.float32
BF16 = jnp.bfloat16
D = 768
HEADS = 12
HEAD_DIM = 64
FF = 3072
IMA = 1
IMB = 2
SIDE_A = 24
SIDE_B = 14
PAT_A = 576
PAT_B = 196
SLOT_B = 224
BLK_A = 144
BLK_B = 56
REAL_B = 49
TABLE = 2304
EPS = 1e-06
NEG = -1e30
ROOT_HALF = 0.7071067811865476
ROOT_TAU = 0.3989422804014327
STEP_RATES = (0.04, 1.6, 0.08, 0.02, 3.0, 0.6)

QA = 160
QB = 64
NQ = QA + IMB * QB
KA = 640
KB = 256
NK = KA + IMB * KB
BLOCK = BLK_A + IMB * QB
GROUPS = BLK_A // SIDE_A
CHUNK = 256
REACH = 29
SPAN = 2 * SIDE_A - 1
STRIP = 768
VMEM = 56 << 20
AXES = ("d0", "d1", "c", "zh", "zl")


def lookup_kernel(table_ref, index_ref, out_ref):
    rows, lanes = index_ref.shape
    heads, entries = table_ref.shape

    def eight_rows(at, carry):
        start = pl.multiple_of(at * 8, 8)
        for col in range(lanes // 128):
            ids = index_ref[pl.ds(start, 8), col * 128 : (col + 1) * 128]
            low = ids & 127
            high = ids >> 7
            found = [jnp.zeros((8, 128), F32) for _ in range(heads)]
            for chunk in range(entries // 128):
                here = high == chunk
                for head in range(heads):
                    row = jnp.broadcast_to(
                        table_ref[head : head + 1, chunk * 128 : (chunk + 1) * 128], (8, 128)
                    )
                    got = jnp.take_along_axis(row, low, axis=1)
                    found[head] = jnp.where(here, got, found[head])
            for head in range(heads):
                out_ref[head, pl.ds(start, 8), col * 128 : (col + 1) * 128] = found[head]
        return carry

    lax.fori_loop(0, rows // 8, eight_rows, 0)


def lookup(table_t, ids):
    return pl.pallas_call(
        lookup_kernel,
        out_shape=jax.ShapeDtypeStruct((table_t.shape[0],) + ids.shape, F32),
        compiler_params=pltpu.CompilerParams(vmem_limit_bytes=VMEM),
        cost_estimate=pl.CostEstimate(flops=20_000_000, bytes_accessed=2_000_000, transcendentals=0),
    )(table_t, ids)


def dot_last(left, right):
    return lax.dot_general(left, right, (((1,), (1,)), ((), ())), preferred_element_type=F32)


def dot_first(left, right):
    return lax.dot_general(left, right, (((0,), (0,)), ((), ())), preferred_element_type=F32)


def dot_plain(left, right):
    return jnp.dot(left, right, preferred_element_type=F32)


def unit_of(values):
    center = values - jnp.mean(values, axis=-1, keepdims=True)
    inv_std = lax.rsqrt(jnp.mean(center * center, axis=-1, keepdims=True) + EPS)
    return center * inv_std, inv_std


def norm_back(grad_in, unit_rows, inv_std, gain):
    d_unit = grad_in * gain
    return inv_std * (
        d_unit
        - jnp.mean(d_unit, axis=-1, keepdims=True)
        - unit_rows * jnp.mean(d_unit * unit_rows, axis=-1, keepdims=True)
    )


def col_sum(values):
    return jnp.sum(values, axis=0, keepdims=True)


class Piece:
    def __init__(self, blocks, rows, cols, order, other, col0, src=0, first=0, base=0):
        self.blocks, self.rows, self.cols = blocks, rows, cols
        self.order, self.other, self.col0 = order, other, col0
        self.src, self.first, self.base = src, first, base

    def part(self, ref, k):
        return ref.at[self.first + k, :, self.src : self.src + self.cols]

    def row(self, pos, k):
        if self.order is None:
            return 0
        near, far = k % 2, (k + self.base) // 2
        dy, dx = (near, far) if self.order == "x" else (far, near)
        y = 1 - pos[0] if dy else pos[0]
        x = 1 - pos[1] if dx else pos[1]
        c = 1 - pos[2] if self.other else pos[2]
        return pl.multiple_of(((y * 2 + x) * 2 + c) * self.rows, self.rows)


def copies_in(pos, pieces, refs, dest, sems):
    made = []
    for piece, ref in zip(pieces, refs):
        for k in range(piece.blocks):
            spot = dest.at[pl.ds(piece.row(pos, k), piece.rows), piece.col0 : piece.col0 + piece.cols]
            made.append(pltpu.make_async_copy(piece.part(ref, k), spot, sems.at[len(made)]))
    return made


def copies_out(pos, pieces, refs, source, sems):
    made = []
    for piece, ref in zip(pieces, refs):
        for k in range(piece.blocks):
            spot = source.at[pl.ds(piece.row(pos, k), piece.rows), piece.col0 : piece.col0 + piece.cols]
            made.append(pltpu.make_async_copy(spot, piece.part(ref, k), sems.at[len(made)]))
    return made


def piece_count(pieces):
    return sum(piece.blocks for piece in pieces)


def shift_perm(size, shift):
    return [(at, (at + shift) % size) for at in range(size)]


def swap(value, axis):
    return lax.ppermute(value, axis, [(0, 1), (1, 0)])


def hold(value, *after):
    return lax.optimization_barrier((value, *after))[0]


def small_grid():
    return lax.axis_size("d0") == 2 and lax.axis_size("d1") == 2 and lax.axis_size("c") == 2


def gather_axis(value, axis):
    size = lax.axis_size(axis)
    if size == 1:
        return value[None]
    if size > 4:
        return lax.all_gather(value, axis, axis=0)
    me = lax.axis_index(axis)
    pieces = [value] + [lax.ppermute(value, axis, shift_perm(size, s)) for s in range(1, size)]
    ordered = []
    for at in range(size):
        chosen = pieces[0]
        for s in range(1, size):
            chosen = jnp.where((me - at) % size == s, pieces[s], chosen)
        ordered.append(chosen)
    return jnp.stack(ordered)


def scatter_axis(value, axis):
    size = lax.axis_size(axis)
    if size == 1:
        return value[0].astype(F32)
    if size > 4:
        return lax.psum_scatter(value, axis, scatter_dimension=0).astype(F32)
    me = lax.axis_index(axis)
    total = lax.dynamic_index_in_dim(value, me, 0, keepdims=False).astype(F32)
    for s in range(1, size):
        outgoing = lax.dynamic_index_in_dim(value, (me + s) % size, 0, keepdims=False)
        total = total + lax.ppermute(outgoing.astype(BF16), axis, shift_perm(size, s)).astype(F32)
    return total


def halves_of(cols, order):
    if order == "split":
        return [("x", 0, cols // 2), ("y", cols // 2, cols)]
    return [(order, 0, cols)]


def gather_whole(block):
    rows, cols = block.shape
    for axis in ("c", "d1", "d0"):
        block = gather_axis(block, axis)
    return block.reshape(1, -1, cols)


def weight_pieces(turn, rows, cols, col0=0, src=0, pairs=False):
    if not small_grid():
        return [Piece(1, rows * lax.axis_size(AXES[:3]), cols, None, 0, col0, src)]
    if pairs:
        return [Piece(2, rows, cols, turn, other, col0, src, 0, far) for other in (0, 1) for far in (0, 2)]
    return [Piece(4, rows, cols, turn, other, col0, src) for other in (0, 1)]


def small_part(arrays, start):
    if not small_grid():
        tail = arrays[0][0, :, start:]
    else:
        tail = jnp.stack([each[..., start:] for each in arrays])
        tail = tail.reshape(2, 2, 2, *tail.shape[2:])
        for at, axis in enumerate(("c", "d0", "d1")):
            tail = jnp.where(lax.axis_index(axis) == 0, tail, jnp.flip(tail, at))
        tail = jnp.moveaxis(tail, 0, 2)
    return tail.reshape(lax.axis_size(AXES), -1)


def grad_pieces(rows, cols, order):
    if not small_grid():
        return [Piece(1, rows, stop - start, None, 0, start) for _, start, stop in halves_of(cols, order)]
    return [
        Piece(4, rows // 8, stop - start, turn, other, start)
        for turn, start, stop in halves_of(cols, order)
        for other in (0, 1)
    ]


def wide(value):
    return value.astype(F32)


def far_part(own, core):
    return (wide(own[2:]) + wide(core[2:])).astype(BF16)


def near_part(own, core, far):
    return (wide(own[1]) + wide(core[1]) + wide(far[1])).astype(BF16)


def block_sum(own, core, far, near):
    return wide(own[0]) + wide(core[0]) + wide(far[0]) + wide(near)


def whole_grid_sum(whole):
    value = whole[0]
    sizes = [lax.axis_size(axis) for axis in AXES]
    value = value.reshape(*sizes[:3], -1, value.shape[-1])
    for axis in AXES[:3]:
        value = scatter_axis(value, axis)
        if axis != "c":
            value = value.astype(BF16)
    return value


def project_kernel(pieces, pos_ref, pair_ref, two_ref, xl_ref, vec_ref, *refs):
    w_refs = refs[: len(pieces)]
    q_ref, k_ref, v_ref, na_ref, nl_ref, xa_ref, w, sems = refs[len(pieces) :]
    copies = copies_in([pos_ref[at] for at in range(3)], pieces, w_refs, w, sems)
    for copy in copies:
        copy.start()
    for at in range(4):
        mine = pos_ref[3] % 2 == at % 2
        rows = jnp.where(mine, pair_ref[at // 2], two_ref[at // 2])
        xa_ref[at * BLK_A : (at + 1) * BLK_A] = rows[:BLK_A]
        for i in range(IMB):
            start = KA + i * KB + at * QB
            xa_ref[start : start + QB] = rows[BLK_A + i * QB : BLK_A + (i + 1) * QB]
    xa_ref[PAT_A : PAT_A + 16] = xl_ref[BLK_A:QA]
    xa_ref[PAT_A + 16 : KA] = jnp.zeros((KA - PAT_A - 16, D), BF16)
    gain, shift = vec_ref[0:1], vec_ref[1:2]
    nl_ref[...] = (unit_of(wide(xl_ref[...]))[0] * gain + shift).astype(BF16)

    @pl.loop(0, NK // 128)
    def _(at):
        rows = pl.ds(pl.multiple_of(at * 128, 128), 128)
        na_ref[rows] = (unit_of(wide(xa_ref[rows]))[0] * gain + shift).astype(BF16)

    for copy in copies:
        copy.wait()
    queries = dot_plain(nl_ref[...], w[:, :D]) + vec_ref[2:3]
    q_ref[...] = (queries * (1.0 / math.sqrt(HEAD_DIM))).astype(BF16)

    @pl.loop(0, NK // 384)
    def _(at):
        rows = pl.ds(pl.multiple_of(at * 384, 128), 384)
        k_ref[rows] = dot_plain(na_ref[rows], w[:, D : 2 * D]).astype(BF16)
        v_ref[rows] = (dot_plain(na_ref[rows], w[:, 2 * D :]) + vec_ref[3:4]).astype(BF16)


VSPEC = pl.BlockSpec(memory_space=pltpu.VMEM)
SSPEC = pl.BlockSpec(memory_space=pltpu.SMEM)
ANYSPEC = pl.BlockSpec(memory_space=pl.ANY)


def params():
    return pltpu.CompilerParams(vmem_limit_bytes=VMEM)


def cost(flops, moved):
    return pl.CostEstimate(flops=int(flops), bytes_accessed=int(moved), transcendentals=0)


def project(pos, x_pair, x_two, x_loc, vec, arrays, pieces):
    return pl.pallas_call(
        functools.partial(project_kernel, pieces),
        in_specs=[SSPEC] + [VSPEC] * 4 + [ANYSPEC] * len(arrays),
        out_specs=[VSPEC] * 6,
        out_shape=[
            jax.ShapeDtypeStruct((NQ, D), BF16),
            jax.ShapeDtypeStruct((NK, D), BF16),
            jax.ShapeDtypeStruct((NK, D), BF16),
            jax.ShapeDtypeStruct((NK, D), BF16),
            jax.ShapeDtypeStruct((NQ, D), BF16),
            jax.ShapeDtypeStruct((NK, D), BF16),
        ],
        scratch_shapes=[pltpu.VMEM((D, 3 * D), BF16), pltpu.SemaphoreType.DMA((piece_count(pieces),))],
        compiler_params=params(),
        cost_estimate=cost(2 * D * D * (NQ + 2 * NK), 12e6),
        name="project",
    )(pos, x_pair, x_two, x_loc, vec, *arrays)


def softmax_rows(scores):
    top = jnp.max(scores, axis=-1, keepdims=True)
    grown = jnp.exp(scores - top)
    return grown * (1.0 / jnp.sum(grown, axis=-1, keepdims=True))


def attend_kernel(cnt_ref, q_ref, k_ref, v_ref, col_ref, strip_ref, bias_ref, o_ref, pa_ref, pb_ref):
    lane = lax.broadcasted_iota(jnp.int32, (1, 128), 1)
    lane_a = lax.broadcasted_iota(jnp.int32, (1, KA), 1)
    lane_b = lax.broadcasted_iota(jnp.int32, (1, KB), 1)
    row_a = lax.broadcasted_iota(jnp.int32, (QA, 1), 0)
    live_a = ((lane_a < PAT_A) & (lane_a < cnt_ref[0])) | (lane_a == PAT_A)
    spot = lane_b % QB
    live_b = [
        ((spot < REAL_B) & (lane_b // QB * REAL_B + spot < cnt_ref[1 + i])) | (lane_b == BLK_B)
        for i in range(IMB)
    ]
    mixed = []
    for t in range(2):
        mine = (lane < HEAD_DIM) if t == 0 else (lane >= HEAD_DIM)
        queries = jnp.where(mine, q_ref[...], jnp.zeros((), BF16))
        strip = strip_ref[t][:SIDE_A]
        class_row = strip_ref[t][SIDE_A:, :KA]
        bias_b = bias_ref[t]
        parts = []
        for r in range(GROUPS):
            off = (GROUPS - 1 - r) * SIDE_A
            moved = strip if off == 0 else pltpu.roll(strip, STRIP - off, 1)
            parts.append(moved[:, :KA])
        parts += [class_row] * 2
        bias = jnp.concatenate(parts, axis=0)
        bias = jnp.where((lane_a == PAT_A) & (row_a < BLK_A), col_ref[0][:, t : t + 1], bias)
        scores = dot_last(queries[:QA], k_ref[:KA]) + bias
        probs = softmax_rows(jnp.where(live_a, scores, NEG))
        pa_ref[t] = probs
        outs = [dot_plain(probs.astype(BF16), v_ref[:KA])]
        for i in range(IMB):
            q_at = QA + i * QB
            k_at = KA + i * KB
            scores = dot_last(queries[q_at : q_at + QB], k_ref[k_at : k_at + KB]) + bias_b
            probs = softmax_rows(jnp.where(live_b[i], scores, NEG))
            pb_ref[t, i] = probs
            outs.append(dot_plain(probs.astype(BF16), v_ref[k_at : k_at + KB]))
        mixed.append(jnp.concatenate(outs, axis=0))
    o_ref[...] = jnp.where(lane < HEAD_DIM, mixed[0], mixed[1]).astype(BF16)


def attend(counts, queries, keys, values, cols, strip, bias_b):
    pairs = HEADS // 2
    return pl.pallas_call(
        attend_kernel,
        grid=(pairs,),
        in_specs=[
            SSPEC,
            pl.BlockSpec((NQ, 128), lambda p: (0, p)),
            pl.BlockSpec((NK, 128), lambda p: (0, p)),
            pl.BlockSpec((NK, 128), lambda p: (0, p)),
            pl.BlockSpec((1, QA, 128), lambda p: (p, 0, 0)),
        ]
        + [pl.BlockSpec((2, 32, STRIP), lambda p: (p, 0, 0)), pl.BlockSpec((2, QB, KB), lambda p: (p, 0, 0))],
        out_specs=[
            pl.BlockSpec((NQ, 128), lambda p: (0, p)),
            pl.BlockSpec((2, QA, KA), lambda p: (p, 0, 0)),
            pl.BlockSpec((2, IMB, QB, KB), lambda p: (p, 0, 0, 0)),
        ],
        out_shape=[
            jax.ShapeDtypeStruct((NQ, D), BF16),
            jax.ShapeDtypeStruct((HEADS, QA, KA), F32),
            jax.ShapeDtypeStruct((HEADS, IMB, QB, KB), F32),
        ],
        compiler_params=params(),
        cost_estimate=cost(4 * HEADS * 128 * (QA * KA + IMB * QB * KB), 30e6),
        name="attend",
    )(counts, queries, keys, values, cols, strip, bias_b)


def orders_b(odd):
    new_row = lax.broadcasted_iota(jnp.int32, (QB, QB), 0)
    old_row = lax.broadcasted_iota(jnp.int32, (QB, QB), 1)
    inside = new_row % 8
    slot = (new_row // 8 - odd) * 7 + 6 - inside
    order = (inside < 7) & (slot >= 0) & (slot < REAL_B) & (slot == old_row) & (new_row // 8 - odd >= 0)
    old_col = lax.broadcasted_iota(jnp.int32, (KB, KB), 0)
    new_col = lax.broadcasted_iota(jnp.int32, (KB, KB), 1)
    spread = (new_col < PAT_B) & (old_col == new_col // REAL_B * QB + new_col % REAL_B)
    return jnp.where(order, 1.0, 0.0).astype(BF16), jnp.where(spread, 1.0, 0.0).astype(BF16)


def strips_b(laid):
    pieces = []
    for r in range(4):
        off = (3 - r) * SIDE_B
        piece = laid[r * 16 : (r + 1) * 16]
        pieces.append(piece if off == 0 else pltpu.roll(piece, off, 1))
    return pieces


def fold_strip(strip, side):
    even = lax.broadcasted_iota(jnp.int32, (1, strip.shape[1]), 1) // side % 2 == 0
    return [
        pltpu.roll(part, 0, 1, stride=1, stride_axis=0)
        for part in (jnp.where(even, strip, 0.0), jnp.where(even, 0.0, strip))
    ]


def fold_strip_b(strip):
    even = lax.broadcasted_iota(jnp.int32, (1, KB), 1) // SIDE_B % 2 == 0
    return [
        (
            pltpu.roll(part[:8], 7, 1, stride=1, stride_axis=0),
            pltpu.roll(part[8:], 0, 1, stride=1, stride_axis=0),
        )
        for part in (jnp.where(even, strip, 0.0), jnp.where(even, 0.0, strip))
    ]


def row_weights(first):
    row = lax.broadcasted_iota(jnp.int32, (NQ, 1), 0)
    is_class = (row == BLK_A) | ((row >= QA) & ((row - QA) % QB == BLK_B))
    return jnp.where(is_class, first, 1.0)


def attend_back_kernel(place_ref, do_ref, q_ref, k_ref, v_ref, pa_ref, pb_ref, dq_ref, dk_ref, dv_ref, g_ref):
    lane = lax.broadcasted_iota(jnp.int32, (1, 128), 1)
    lane_a = lax.broadcasted_iota(jnp.int32, (1, KA), 1)
    low = lane < HEAD_DIM
    place = place_ref[0]
    odd = place % 2
    weight = row_weights(jnp.where(place == 0, 1.0, 0.0))
    new_row = lax.broadcasted_iota(jnp.int32, (BLK_A, QA), 0)
    old_row = lax.broadcasted_iota(jnp.int32, (BLK_A, QA), 1)
    turned = old_row == new_row // SIDE_A * SIDE_A + (SIDE_A - 1 - new_row % SIDE_A)
    turned = jnp.where(turned, 1.0, 0.0).astype(BF16)
    order, spread = orders_b(odd)
    pick_a = lax.broadcasted_iota(jnp.int32, (8, KA), 1) == PAT_A
    pick_a = jnp.where(pick_a, 1.0, 0.0).astype(BF16)
    pick_b = lax.broadcasted_iota(jnp.int32, (8, KB), 1) == BLK_B
    pick_b = jnp.where(pick_b, 1.0, 0.0).astype(BF16)
    lane_q = lax.broadcasted_iota(jnp.int32, (1, QA), 1)
    d_out = do_ref[...]
    d_out_w = (wide(d_out) * weight).astype(BF16)
    q_all = q_ref[...]
    dq_parts, dk_parts, dv_parts = [], [], []
    for t in range(2):
        mine = low if t == 0 else jnp.logical_not(low)
        d_mine = jnp.where(mine, d_out, jnp.zeros((), BF16))

        def one(q_at, q_len, k_at, k_len, probs):
            d_probs = dot_last(d_mine[q_at : q_at + q_len], v_ref[k_at : k_at + k_len])
            delta = jnp.sum(probs * d_probs, axis=-1, keepdims=True)
            d_wide = probs * (d_probs - delta)
            d_low = d_wide.astype(BF16)
            d_query = dot_plain(d_low, k_ref[k_at : k_at + k_len])
            d_w = (wide(d_low) * weight[q_at : q_at + q_len]).astype(BF16)
            d_key = dot_first(d_w, q_all[q_at : q_at + q_len])
            d_value = dot_first(probs.astype(BF16), d_out_w[q_at : q_at + q_len])
            return d_query, d_key, d_value, d_w

        d_query, d_key, d_value, d_w = one(0, QA, 0, KA, pa_ref[t])
        dqs, dks, dvs = [d_query], [d_key], [d_value]
        flipped = jnp.where(lane_a < PAT_A, dot_plain(turned, d_w), 0.0)
        flipped = jnp.concatenate([flipped, jnp.zeros((BLK_A, STRIP - KA), F32)], axis=1)
        strip = None
        for r in range(GROUPS):
            off = (GROUPS - 1 - r) * SIDE_A
            piece = flipped[r * SIDE_A : (r + 1) * SIDE_A]
            piece = piece if off == 0 else pltpu.roll(piece, off, 1)
            strip = piece if strip is None else strip + piece
        fold = [col_sum(part) for part in fold_strip(strip, SIDE_A)]
        row_a = wide(d_w[BLK_A : BLK_A + 16])[:1]
        col_a = jnp.where(lane_q < BLK_A, dot_last(pick_a, d_w)[:1], 0.0)
        moved, row_b, col_b = None, None, None
        for i in range(IMB):
            d_query, d_key, d_value, d_w = one(QA + i * QB, QB, KA + i * KB, KB, pb_ref[t, i])
            dqs.append(d_query)
            dks.append(d_key)
            dvs.append(d_value)
            laid = dot_plain(dot_plain(order, d_w).astype(BF16), spread)
            row = wide(d_w[BLK_B - 8 : BLK_B + 8])[8:9]
            col = jnp.where(lane_q[:, :QB] < BLK_B, dot_last(pick_b, d_w)[:1], 0.0)
            moved = laid if i == 0 else moved + laid
            row_b = row if i == 0 else row_b + row
            col_b = col if i == 0 else col_b + col
        strip = None
        for piece in strips_b(moved):
            strip = piece if strip is None else strip + piece
        fold_b = [col_sum(left + right) for left, right in fold_strip_b(strip)]
        g_ref[t, 0:1] = fold[0]
        g_ref[t, 1:2] = fold[1]
        g_ref[t, 2:3, 0:KB] = fold_b[0]
        g_ref[t, 2:3, KB : 2 * KB] = fold_b[1]
        g_ref[t, 2:3, 2 * KB :] = row_b
        g_ref[t, 3:4, 0:KA] = row_a
        g_ref[t, 3:4, KA:] = jnp.concatenate([col_b, jnp.zeros((1, 128 - QB), F32)], axis=1)
        g_ref[t, 4:5, 0:256] = jnp.concatenate([col_a, jnp.zeros((1, 256 - QA), F32)], axis=1)
        g_ref[t, 4:5, 256:] = jnp.zeros((1, STRIP - 256), F32)
        g_ref[t, 5:8] = jnp.zeros((3, STRIP), F32)
        dq_parts.append(jnp.concatenate(dqs, axis=0))
        dk_parts.append(jnp.concatenate(dks, axis=0))
        dv_parts.append(jnp.concatenate(dvs, axis=0))
    d_query = jnp.where(low, dq_parts[0], dq_parts[1]).astype(BF16)
    dq_ref[...] = (wide(d_query) * (1.0 / math.sqrt(HEAD_DIM))).astype(BF16)
    dk_ref[...] = jnp.where(low, dk_parts[0], dk_parts[1]).astype(BF16)
    dv_ref[...] = jnp.where(low, dv_parts[0], dv_parts[1]).astype(BF16)


def attend_back(place, part, d_mixed, queries, keys, values, probs_a, probs_b):
    pairs = HEADS // 4
    base = part * pairs
    return pl.pallas_call(
        attend_back_kernel,
        grid=(pairs,),
        in_specs=[
            SSPEC,
            pl.BlockSpec((NQ, 128), lambda p: (0, base + p)),
            pl.BlockSpec((NQ, 128), lambda p: (0, base + p)),
            pl.BlockSpec((NK, 128), lambda p: (0, base + p)),
            pl.BlockSpec((NK, 128), lambda p: (0, base + p)),
            pl.BlockSpec((2, QA, KA), lambda p: (base + p, 0, 0)),
            pl.BlockSpec((2, IMB, QB, KB), lambda p: (base + p, 0, 0, 0)),
        ],
        out_specs=[
            pl.BlockSpec((NQ, 128), lambda p: (0, p)),
            pl.BlockSpec((NK, 128), lambda p: (0, p)),
            pl.BlockSpec((NK, 128), lambda p: (0, p)),
            pl.BlockSpec((2, 8, STRIP), lambda p: (p, 0, 0)),
        ],
        out_shape=[
            jax.ShapeDtypeStruct((NQ, D // 2), BF16),
            jax.ShapeDtypeStruct((NK, D // 2), BF16),
            jax.ShapeDtypeStruct((NK, D // 2), BF16),
            jax.ShapeDtypeStruct((HEADS // 2, 8, STRIP), F32),
        ],
        compiler_params=params(),
        cost_estimate=cost(6 * HEADS * 128 * (QA * KA + IMB * QB * KB), 15e6),
        name="attend_back",
    )(place, d_mixed, queries, keys, values, probs_a, probs_b)


def table_kernel(g0_ref, g1_ref, ids_ref, out_ref):
    rows = lax.broadcasted_iota(jnp.int32, (CHUNK, STRIP), 0)
    split = []
    for at in range(5):
        values = jnp.concatenate([g0_ref[:, at], g1_ref[:, at]], axis=0)
        top = values.astype(BF16)
        rest = values - wide(top)
        middle = rest.astype(BF16)
        bottom = (rest - wide(middle)).astype(BF16)
        pad = jnp.zeros((4, STRIP), F32)
        stacked = []
        for part in (top, middle, bottom):
            stacked += [wide(part), pad]
        split.append(jnp.concatenate(stacked, axis=0).astype(BF16))

    for step in range(TABLE // CHUNK):
        total = jnp.zeros((48, CHUNK), F32)
        for at in range(5):
            hot = jnp.where(rows + step * CHUNK == ids_ref[at : at + 1], 1.0, 0.0).astype(BF16)
            total = total + dot_last(split[at], hot)
        out_ref[:, step * CHUNK : (step + 1) * CHUNK] = total[:16] + total[16:32] + total[32:]


def table_grad(first, second, ids):
    return pl.pallas_call(
        table_kernel,
        in_specs=[VSPEC] * 3,
        out_specs=VSPEC,
        out_shape=jax.ShapeDtypeStruct((16, TABLE), F32),
        compiler_params=params(),
        cost_estimate=cost(2 * 48 * TABLE * 5 * STRIP, 2e6),
        name="table_grad",
    )(first, second, ids)


def flip_rows(count, size):
    new_row = lax.broadcasted_iota(jnp.int32, (count, count), 0)
    old_row = lax.broadcasted_iota(jnp.int32, (count, count), 1)
    turned = old_row == new_row // size * size + (size - 1 - new_row % size)
    return jnp.where(turned, 1.0, 0.0).astype(BF16)


def ids_kernel(place_ref, ia_ref, ib_ref, a_ref, b_ref, f_ref):
    place = place_ref[0]

    def through(matrix, ids):
        high = (ids // 64).astype(F32).astype(BF16)
        low = (ids % 64).astype(F32).astype(BF16)
        return 64.0 * dot_plain(matrix, high) + dot_plain(matrix, low)

    def column(ids, at):
        pick = lax.broadcasted_iota(jnp.int32, (8, ids.shape[1]), 1) == at
        pick = jnp.where(pick, 1.0, 0.0).astype(BF16)
        high = (ids // 64).astype(F32).astype(BF16)
        low = (ids % 64).astype(F32).astype(BF16)
        return (64.0 * dot_last(pick, high) + dot_last(pick, low))[:1].astype(jnp.int32)

    def fill(row, width):
        return jnp.concatenate([row, jnp.zeros((row.shape[0], width - row.shape[1]), jnp.int32)], axis=1)

    top = (GROUPS - 1) * SIDE_A
    for at in range(4):

        @pl.when(place == at)
        def _():
            rows_a = ia_ref[1 + BLK_A * at : 1 + BLK_A * (at + 1), :]
            last, first = rows_a[top:, 1 : 1 + top], rows_a[:SIDE_A, 1:]
            a_ref[:SIDE_A] = fill(jnp.concatenate([last, first], axis=1), STRIP)
            f_ref[4:5] = fill(column(rows_a, 0), STRIP)
            rows_b = jnp.concatenate(
                [ib_ref[1 + BLK_B * at : 1 + BLK_B * (at + 1), :], ib_ref[0:1, :], jnp.zeros((7, SLOT_B + 1), jnp.int32)],
                axis=0,
            )
            parts = []
            for k in range(4):
                parts += [rows_b[:, 1 + k * BLK_B : 1 + (k + 1) * BLK_B], rows_b[:, :1], jnp.zeros((QB, 7), jnp.int32)]
            b_ref[...] = jnp.concatenate(parts, axis=1)
            f_ref[3:4, KA:] = fill(column(rows_b, 0)[:, :BLK_B], 128)

    class_row = jnp.concatenate([ia_ref[0:1, 1:], ia_ref[0:1, :1]], axis=1)
    a_ref[SIDE_A : SIDE_A + 1] = fill(class_row, STRIP)
    a_ref[SIDE_A + 1 : SIDE_A + 2] = f_ref[4:5]
    a_ref[SIDE_A + 2 :] = jnp.zeros((6, STRIP), jnp.int32)
    f_ref[3:4, :KA] = fill(class_row, KA)
    f_ref[2:3, 2 * KB :] = b_ref[BLK_B : BLK_B + 1]
    f_ref[5:8] = jnp.zeros((3, STRIP), jnp.int32)
    turned = through(flip_rows(SIDE_A, SIDE_A), a_ref[:SIDE_A])
    lane = lax.broadcasted_iota(jnp.int32, (1, STRIP), 1)
    turned = jnp.where(lane < REACH * SIDE_A, turned, 0.0)
    for at, part in enumerate(fold_strip(turned, SIDE_A)):
        f_ref[at : at + 1] = jnp.max(part, axis=0, keepdims=True).astype(jnp.int32)
    order, spread = orders_b(place % 2)
    laid = through(order, b_ref[...]).astype(jnp.int32)
    high = (laid // 64).astype(F32).astype(BF16)
    low = (laid % 64).astype(F32).astype(BF16)
    laid = 64.0 * dot_plain(high, spread) + dot_plain(low, spread)
    strip = None
    for piece in strips_b(laid):
        strip = piece if strip is None else jnp.maximum(strip, piece)
    for at, (left, right) in enumerate(fold_strip_b(strip)):
        found = jnp.max(jnp.maximum(left, right), axis=0, keepdims=True)
        f_ref[2:3, at * KB : (at + 1) * KB] = found.astype(jnp.int32)


def all_ids(pos, index_a, index_b):
    return pl.pallas_call(
        ids_kernel,
        in_specs=[SSPEC, VSPEC, VSPEC],
        out_specs=[VSPEC] * 3,
        out_shape=[jax.ShapeDtypeStruct(shape, jnp.int32) for shape in ((32, STRIP), (QB, KB), (8, STRIP))],
        compiler_params=params(),
        cost_estimate=cost(1e8, 6e6),
        name="ids",
    )(pos[3:], index_a, index_b)


def feed_kernel(meta, pos_ref, cnt_ref, mixed_ref, x_ref, cot_ref, vec_ref, b1_ref, *refs):
    (p_out, p_up, p_down), (q_out, q_up, q_down) = meta
    refs = list(refs)

    def take(count):
        taken = refs[:count]
        del refs[:count]
        return taken

    wo_refs, wu_refs, wd_refs = take(len(p_out)), take(len(p_up)), take(len(p_down))
    fa_ref, fca_ref, fb_ref, fcb_ref, dres_ref, dmix_ref, gv_ref, gb_ref = take(8)
    go_refs, gu_refs, gd_refs = take(len(q_out)), take(len(q_up)), take(len(q_down))
    wo, wu, wd, go, gu, gd, norm, gelu, slope, dsec, dsec_w, acc, sem_o, sem_u, sem_d = refs
    pos = [pos_ref[at] for at in range(3)]
    loads = [copies_in(pos, *each) for each in ((p_out, wo_refs, wo, sem_o), (p_up, wu_refs, wu, sem_u), (p_down, wd_refs, wd, sem_d))]
    for group in loads:
        for copy in group:
            copy.start()

    def piece(at):
        return vec_ref[at : at + 1]

    place = pos_ref[3]
    weight = row_weights(jnp.where(place == 0, 1.0, 0.0))
    row = lax.broadcasted_iota(jnp.int32, (NQ, 1), 0)
    slot = (row - QA) % QB
    count_b = jnp.where(row < QA + QB, cnt_ref[1], cnt_ref[2])
    live_a = ((row < BLK_A) & (place * BLK_A + row < cnt_ref[0])) | (row == BLK_A)
    live_b = ((slot < REAL_B) & (place * REAL_B + slot < count_b)) | (slot == BLK_B)
    live = jnp.where(((row < QA) & live_a) | ((row >= QA) & live_b), 1.0, 0.0)

    for copy in loads[0]:
        copy.wait()
    branch = dot_plain(mixed_ref[...], wo[...]) + piece(4)
    resid = wide(x_ref[...]) + piece(5) * branch
    unit, inv_std = unit_of(resid)
    norm[...] = (unit * piece(6) + piece(7)).astype(BF16)
    for copy in loads[1]:
        copy.wait()

    @pl.loop(0, FF // CHUNK)
    def _(at):
        cols = pl.ds(pl.multiple_of(at * CHUNK, CHUNK), CHUNK)
        hidden = dot_plain(norm[...], wu[:, cols]) + b1_ref[pl.ds(at, 1), :]
        gate = 0.5 * (1.0 + lax.erf(hidden * ROOT_HALF))
        gelu[:, cols] = (hidden * gate).astype(BF16)
        slope[:, cols] = gate + hidden * ROOT_TAU * jnp.exp(-0.5 * hidden * hidden)

    for copy in loads[2]:
        copy.wait()
    second = dot_plain(gelu[...], wd[...]) + piece(8)
    final = resid + piece(9) * second
    fa_ref[0] = final[:BLK_A]
    fca_ref[...] = final[BLK_A : BLK_A + 1]
    d_final = wide(cot_ref[...]) * live
    for i in range(IMB):
        fb_ref[i] = final[QA + i * QB : QA + i * QB + BLK_B]
        fcb_ref[i : i + 1] = final[QA + i * QB + BLK_B : QA + i * QB + BLK_B + 1]
    gv_ref[5:6] = col_sum(d_final * second * weight)
    d_second = (piece(9) * d_final).astype(BF16)
    dsec[...] = d_second
    d_second_w = wide(d_second) * weight
    gv_ref[4:5] = col_sum(d_second_w)
    dsec_w[...] = d_second_w.astype(BF16)
    acc[...] = jnp.zeros((NQ, D), F32)

    @pl.loop(0, FF // CHUNK)
    def _(at):
        cols = pl.ds(pl.multiple_of(at * CHUNK, CHUNK), CHUNK)
        d_gelu = dot_last(dsec[...], wd[cols, :])
        d_hidden = (d_gelu * slope[:, cols]).astype(BF16)
        d_hidden_w = wide(d_hidden) * weight
        gb_ref[pl.ds(at, 1), :] = col_sum(d_hidden_w)
        gd[cols, :] = dot_first(gelu[:, cols], dsec_w[...]).astype(BF16)
        gu[:, cols] = dot_first(norm[...], d_hidden_w.astype(BF16)).astype(BF16)
        acc[...] += dot_last(d_hidden, wu[:, cols])

    stores = copies_out(pos, q_down, gd_refs, gd, sem_d) + copies_out(pos, q_up, gu_refs, gu, sem_u)
    for copy in stores:
        copy.start()
    d_normed = acc[...]
    d_normed_w = d_normed * weight
    gv_ref[2:3] = col_sum(d_normed_w * unit)
    gv_ref[3:4] = col_sum(d_normed_w)
    d_resid = d_final + norm_back(d_normed, unit, inv_std, piece(6))
    dres_ref[...] = d_resid
    gv_ref[1:2] = col_sum(d_resid * branch * weight)
    d_branch = (piece(5) * d_resid).astype(BF16)
    d_branch_w = wide(d_branch) * weight
    gv_ref[0:1] = col_sum(d_branch_w)
    gv_ref[6:8] = jnp.zeros((2, D), F32)
    go[...] = dot_first(mixed_ref[...], d_branch_w.astype(BF16)).astype(BF16)
    last = copies_out(pos, q_out, go_refs, go, sem_o)
    for copy in last:
        copy.start()
    dmix_ref[...] = dot_last(d_branch, wo[...]).astype(BF16)
    for copy in stores + last:
        copy.wait()


def feed(pos, counts, mixed, x_loc, cot, vec, b1, weights, orders):
    (a_out, p_out), (a_up, p_up), (a_down, p_down) = weights
    q_out = grad_pieces(D, D, orders[0])
    q_up = grad_pieces(D, FF, orders[1])
    q_down = grad_pieces(FF, D, orders[2])
    grads = q_out + q_up + q_down
    shapes = [
        jax.ShapeDtypeStruct((IMA, BLK_A, D), F32),
        jax.ShapeDtypeStruct((IMA, D), F32),
        jax.ShapeDtypeStruct((IMB, BLK_B, D), F32),
        jax.ShapeDtypeStruct((IMB, D), F32),
        jax.ShapeDtypeStruct((NQ, D), F32),
        jax.ShapeDtypeStruct((NQ, D), BF16),
        jax.ShapeDtypeStruct((8, D), F32),
        jax.ShapeDtypeStruct((FF // CHUNK, CHUNK), F32),
    ]
    outs = pl.pallas_call(
        functools.partial(feed_kernel, ((p_out, p_up, p_down), (q_out, q_up, q_down))),
        in_specs=[SSPEC] * 2 + [VSPEC] * 5 + [ANYSPEC] * (len(a_out) + len(a_up) + len(a_down)),
        out_specs=[VSPEC] * 8 + [ANYSPEC] * len(grads),
        out_shape=shapes + [jax.ShapeDtypeStruct((p.blocks, p.rows, p.cols), BF16) for p in grads],
        scratch_shapes=[
            pltpu.VMEM((D, D), BF16),
            pltpu.VMEM((D, FF), BF16),
            pltpu.VMEM((FF, D), BF16),
            pltpu.VMEM((D, D), BF16),
            pltpu.VMEM((D, FF), BF16),
            pltpu.VMEM((FF, D), BF16),
            pltpu.VMEM((NQ, D), BF16),
            pltpu.VMEM((NQ, FF), BF16),
            pltpu.VMEM((NQ, FF), F32),
            pltpu.VMEM((NQ, D), BF16),
            pltpu.VMEM((NQ, D), BF16),
            pltpu.VMEM((NQ, D), F32),
            pltpu.SemaphoreType.DMA((max(piece_count(p_out), piece_count(q_out)),)),
            pltpu.SemaphoreType.DMA((max(piece_count(p_up), piece_count(q_up)),)),
            pltpu.SemaphoreType.DMA((max(piece_count(p_down), piece_count(q_down)),)),
        ],
        compiler_params=params(),
        cost_estimate=cost(6 * NQ * D * (D + 2 * FF), 30e6),
        name="feed",
    )(pos, counts, mixed, x_loc, cot, vec, b1, *a_out, *a_up, *a_down)
    plain, rest = outs[:8], list(outs[8:])
    g_out = [rest.pop(0) for _ in q_out]
    g_up = [rest.pop(0) for _ in q_up]
    g_down = [rest.pop(0) for _ in q_down]
    return plain, g_out, g_up, g_down


def back_kernel(p_qkv, q_qkv, q_out, pos_ref, dq0_ref, dk0_ref, dv0_ref, dq1_ref, dk1_ref, dv1_ref, na_ref, nl_ref, xa_ref, xl_ref, *refs):
    refs = list(refs)

    def take(count):
        taken = refs[:count]
        del refs[:count]
        return taken

    w_refs, o_refs = take(len(p_qkv)), take(len(q_out))
    local_ref, keep_ref, send_ref, gv_ref = take(4)
    g_refs = take(2 if small_grid() else len(q_qkv))
    w, g, rows_all, sums, sem_w, sem_g, sem_o = refs
    pos = [pos_ref[at] for at in range(3)]
    place = pos_ref[3]
    loads = copies_in(pos, p_qkv, w_refs, w, sem_w)
    for copy in loads:
        copy.start()
    targets = [g_refs[at % 2] if small_grid() else g_refs[at] for at in range(len(q_qkv))]
    passed = []
    for piece, source, ref in zip(q_out, o_refs, targets):
        for k in range(piece.blocks):
            passed.append(pltpu.make_async_copy(source.at[k], piece.part(ref, k), sem_o.at[len(passed)]))
            passed[-1].start()
    weight = row_weights(jnp.where(place == 0, 1.0, 0.0))
    d_query = jnp.concatenate([dq0_ref[...], dq1_ref[...]], axis=1)
    d_query_w = wide(d_query) * weight
    gv_ref[2:3] = col_sum(d_query_w)
    g[:, :D] = dot_first(nl_ref[...], d_query_w.astype(BF16)).astype(BF16)

    half = D // 2
    for at, (dk_ref, dv_ref) in enumerate(((dk0_ref, dv0_ref), (dk1_ref, dv1_ref))):
        g[:, D + at * half : D + (at + 1) * half] = dot_first(na_ref[...], dk_ref[...]).astype(BF16)
        g[:, 2 * D + at * half : 2 * D + (at + 1) * half] = dot_first(na_ref[...], dv_ref[...]).astype(BF16)

    stores = copies_out(pos, q_qkv, targets, g, sem_g)
    for copy in stores:
        copy.start()
    for copy in loads:
        copy.wait()
    sums[...] = jnp.zeros((8, D), F32)

    @pl.loop(0, NK // 384)
    def _(at):
        rows = pl.ds(pl.multiple_of(at * 384, 128), 384)
        d_key = jnp.concatenate([dk0_ref[rows], dk1_ref[rows]], axis=1)
        d_value = jnp.concatenate([dv0_ref[rows], dv1_ref[rows]], axis=1)
        d_norm = dot_last(d_key, w[:, D : 2 * D]) + dot_last(d_value, w[:, 2 * D :])
        rows_all[rows] = d_norm
        unit = unit_of(wide(xa_ref[rows]))[0]
        sums[0:1] += col_sum(d_norm * unit)
        sums[1:2] += col_sum(d_norm)
        sums[2:3] += col_sum(wide(d_value))

    d_local = dot_last(d_query, w[:, :D])
    d_local_w = d_local * weight
    unit = unit_of(wide(xl_ref[...]))[0]
    gv_ref[0:1] = sums[0:1] + col_sum(d_local_w * unit)
    gv_ref[1:2] = sums[1:2] + col_sum(d_local_w)
    gv_ref[3:4] = sums[2:3]
    gv_ref[4:8] = jnp.zeros((4, D), F32)
    class_a = rows_all[PAT_A : PAT_A + 8][:1]
    class_b = [rows_all[KA + i * KB + BLK_B : KA + i * KB + BLK_B + 8][:1] for i in range(IMB)]
    row_b = lax.broadcasted_iota(jnp.int32, (QB, 1), 0)

    zh, zl = place // 2, place % 2

    def block_of(at):
        part_a = rows_all[pl.ds(pl.multiple_of(at * BLK_A, BLK_A), BLK_A)]
        parts = [part_a]
        for i in range(IMB):
            part = rows_all[pl.ds(pl.multiple_of(KA + i * KB + at * QB, QB), QB)]
            part = jnp.where(row_b == BLK_B, class_b[i], part)
            part = jnp.where(row_b == BLK_B + 1, class_a, part) if i == 0 else part
            parts.append(part)
        return parts

    for step in (0, 1):
        high = zh if step == 0 else 1 - zh
        send_ref[step] = jnp.concatenate(block_of(high * 2 + 1 - zl), axis=0).astype(BF16)
    keep_ref[...] = jnp.concatenate(block_of((1 - zh) * 2 + zl), axis=0)
    own = block_of(place)
    local_ref[:BLK_A] = own[0] + d_local[:BLK_A]
    local_ref[BLK_A : BLK_A + 16] = jnp.concatenate(
        [own[1][BLK_B + 1 : BLK_B + 2] + d_local[BLK_A : BLK_A + 1], jnp.zeros((15, D), F32)], axis=0
    )
    for i in range(IMB):
        at = QA + i * QB
        local_ref[at : at + QB] = own[1 + i] + d_local[at : at + QB]
    for copy in stores + passed:
        copy.wait()


def back(pos, first, second, normed_all, normed_loc, x_all, x_loc, arrays, pieces, g_out):
    q_qkv, q_out = grad_pieces(D, 3 * D, "split"), grad_pieces(D, D, "split")
    width = q_qkv[0].cols
    joint = [(1, D, 2 * D)] * 2
    if small_grid():
        joint = [(8, D // 8, 2 * D)] * 2
        for at in range(4):
            q_qkv[at].first = q_out[at].first = at // 2 * 4
    for piece in q_out:
        piece.src = width
    shapes = [((NQ, D), F32), ((BLOCK, D), F32), ((2, BLOCK, D), BF16), ((8, D), F32)]
    outs = pl.pallas_call(
        functools.partial(back_kernel, pieces, q_qkv, q_out),
        in_specs=[SSPEC] + [VSPEC] * 10 + [ANYSPEC] * len(arrays) + [VSPEC] * len(g_out),
        out_specs=[VSPEC] * 4 + [ANYSPEC] * 2,
        out_shape=[jax.ShapeDtypeStruct(*each) for each in shapes]
        + [jax.ShapeDtypeStruct(shape, BF16) for shape in joint],
        scratch_shapes=[
            pltpu.VMEM((D, 3 * D), BF16),
            pltpu.VMEM((D, 3 * D), BF16),
            pltpu.VMEM((NK, D), F32),
            pltpu.VMEM((8, D), F32),
            pltpu.SemaphoreType.DMA((piece_count(pieces),)),
            pltpu.SemaphoreType.DMA((piece_count(q_qkv),)),
            pltpu.SemaphoreType.DMA((piece_count(q_out),)),
        ],
        compiler_params=params(),
        cost_estimate=cost(4 * D * D * (NQ + 2 * NK), 20e6),
        name="back",
    )(pos, *first, *second, normed_all, normed_loc, x_all, x_loc, *arrays, *g_out)
    return outs[:4], list(outs[4:])


def finish_kernel(dres_ref, local_ref, r1_ref, r2_ref, x_ref, vec_ref, ga_ref, gca_ref, gb_ref, gcb_ref):
    gain = vec_ref[0:1]

    def rows_of(at, count, got_at):
        grad = local_ref[at : at + count]
        grad = grad + wide(r1_ref[0, got_at : got_at + count]) + wide(r2_ref[got_at : got_at + count])
        unit, inv_std = unit_of(wide(x_ref[at : at + count]))
        return dres_ref[at : at + count] + norm_back(grad, unit, inv_std, gain)

    ga_ref[0] = rows_of(0, BLK_A, 0)
    for i in range(IMB):
        at = QA + i * QB
        rows = rows_of(at, QB, BLK_A + i * QB)
        gb_ref[i] = rows[:BLK_B]
        gcb_ref[i : i + 1] = rows[BLK_B : BLK_B + 1]
    grad = local_ref[BLK_A : BLK_A + 16]
    spot = BLK_A + 48
    grad = grad + wide(r1_ref[0, spot : spot + 16])[9:10] + wide(r2_ref[spot : spot + 16])[9:10]
    unit, inv_std = unit_of(wide(x_ref[BLK_A : BLK_A + 16]))
    rows = dres_ref[BLK_A : BLK_A + 16] + norm_back(grad, unit, inv_std, gain)
    gca_ref[...] = rows[:1]


def finish(d_resid, local, got, x_loc, vec):
    return pl.pallas_call(
        finish_kernel,
        in_specs=[VSPEC] * 6,
        out_specs=[VSPEC] * 4,
        out_shape=[
            jax.ShapeDtypeStruct((IMA, BLK_A, D), F32),
            jax.ShapeDtypeStruct((IMA, D), F32),
            jax.ShapeDtypeStruct((IMB, BLK_B, D), F32),
            jax.ShapeDtypeStruct((IMB, D), F32),
        ],
        compiler_params=params(),
        cost_estimate=cost(1e6, 6e6),
        name="finish",
    )(d_resid, local, *got, x_loc, vec)


def pad_to(values, width):
    return jnp.pad(values, ((0, width - values.shape[0]),))


def nesterov(master, moment, average, grad_w, step_rate):
    moment_new = 0.5 * moment + grad_w
    master_new = master - step_rate * (grad_w + 0.5 * moment_new)
    return (master_new, moment_new, 0.5 * average + 0.5 * master_new)


def pair_up(value, other, axis):
    first = lax.axis_index(axis) == 0
    return jnp.stack([jnp.where(first, value, other), jnp.where(first, other, value)])


def across(mine, other):
    first = lax.axis_index("zl") == 0
    return jnp.stack([jnp.where(first, mine, other), jnp.where(first, other, mine)], axis=1)


def zl_parts(block):
    cut = block.reshape(2, 2, block.shape[0] // 4, block.shape[1])
    zl = lax.axis_index("zl")
    send = lax.dynamic_index_in_dim(cut, 1 - zl, 1, keepdims=False).astype(BF16)
    return send, lax.dynamic_index_in_dim(cut, zl, 1, keepdims=False)


def zh_parts(kept, got):
    zh = lax.axis_index("zh")
    both = kept + wide(got)
    send = lax.dynamic_index_in_dim(both, 1 - zh, 0, keepdims=False).astype(BF16)
    return send, lax.dynamic_index_in_dim(both, zh, 0, keepdims=False)


def sum_z(block):
    send, kept = zl_parts(block)
    send, kept = zh_parts(kept, swap(send, "zl"))
    return kept + wide(swap(send, "zh"))


def tick(*values):
    return lax.optimization_barrier(values)


def pack_kernel(xa_ref, xca_ref, xb_ref, xcb_ref, ca_ref, cca_ref, cb_ref, ccb_ref, x_ref, cot_ref, send_ref):
    def lay(rows_a, class_a, rows_b, class_b):
        zero = jnp.zeros((16, D), F32)
        parts = [wide(rows_a[0]), wide(class_a[...]), zero[: QA - BLK_A - 1]]
        for i in range(IMB):
            parts += [wide(rows_b[i]), wide(class_b[i : i + 1]), zero[: QB - BLK_B - 1]]
        return jnp.concatenate(parts, axis=0).astype(BF16)

    rows = lay(xa_ref, xca_ref, xb_ref, xcb_ref)
    x_ref[...] = rows
    send_ref[:BLK_A] = rows[:BLK_A]
    send_ref[BLK_A:] = rows[QA:]
    cot_ref[...] = lay(ca_ref, cca_ref, cb_ref, ccb_ref)


def pack(*rows):
    return pl.pallas_call(
        pack_kernel,
        in_specs=[VSPEC] * 8,
        out_specs=[VSPEC] * 3,
        out_shape=[jax.ShapeDtypeStruct((count, D), BF16) for count in (NQ, NQ, BLOCK)],
        compiler_params=params(),
        cost_estimate=cost(1e6, 2e6),
        name="pack",
    )(*rows)


LEFT = 3 * D // 2 + D // 2


def body(
    patches_a, class_a, patches_b, class_b, count_a, count_b, index_a, index_b,
    cot_a, cot_class_a, cot_b, cot_class_b,
    qkv_weight, qkv_momentum, qkv_average, out_weight, out_momentum, out_average,
    up_weight, up_momentum, up_average, down_weight, down_momentum, down_average,
    table_weight, table_momentum, table_average, vector_weight, vector_momentum, vector_average,
):
    zh, zl = lax.axis_index("zh"), lax.axis_index("zl")
    place = zh * 2 + zl
    devices = lax.axis_size(AXES)
    n0, n1, nc = [lax.axis_size(axis) for axis in AXES[:3]]
    pos = jnp.stack([lax.axis_index("d0"), lax.axis_index("d1"), lax.axis_index("c"), place]).astype(jnp.int32)
    counts = jnp.concatenate([count_a, count_b, jnp.zeros((1,), jnp.int32)])

    grid = small_grid()
    t_rows, v_len = table_weight.shape[0], vector_weight.shape[0]
    small = jnp.concatenate([table_weight.reshape(-1), vector_weight])
    small = pad_to(small, qkv_weight.shape[0] * 128).reshape(-1, 128)
    half, part = 3 * D // 2, D // 2
    qkv = jnp.concatenate(
        [qkv_weight[:, :half], out_weight[:, :part], qkv_weight[:, half:], out_weight[:, part:], small], axis=1
    ).astype(BF16)

    q_one = swap(qkv, "zh")
    up, down = up_weight.astype(BF16), down_weight.astype(BF16)
    x_loc, cot, message = pack(patches_a, class_a, patches_b, class_b, cot_a, cot_class_a, cot_b, cot_class_b)
    q_one, up, down, x_loc, cot, message = tick(q_one, up, down, x_loc, cot, message)

    q_pair, up = tick(pair_up(qkv, q_one, "zh"), up)
    q_two, u_one = swap(q_pair, "zl"), swap(up, "zh")
    q_two, u_one = tick(q_two, u_one)

    q_block = across(q_pair, q_two).reshape(-1, qkv.shape[1])
    left, right = q_block[:, :LEFT], q_block[:, LEFT:]
    u_pair = pair_up(up, u_one, "zh")
    left, right, u_pair, down, index_a, index_b = tick(left, right, u_pair, down, index_a, index_b)
    if grid:
        l_one, r_one = swap(left, "d0"), swap(right, "d1")
    u_two, d_one = swap(u_pair, "zl"), swap(down, "zh")
    ids = all_ids(pos, index_a, index_b)
    if grid:
        l_one, r_one, u_two, d_one, ids = tick(l_one, r_one, u_two, d_one, ids)
        l_two, r_two = jnp.stack([left, l_one]), jnp.stack([right, r_one])
    else:
        u_two, d_one, ids = tick(u_two, d_one, ids)
        l_two, r_two = left, right
    d_pair = pair_up(down, d_one, "zh")
    l_two, r_two, d_pair, message = tick(l_two, r_two, d_pair, message)
    if grid:
        l_far, r_far = swap(l_two, "d1"), swap(r_two, "d0")
    d_two, x_one = swap(d_pair, "zl"), swap(message, "zh")
    u_block = across(u_pair, u_two).reshape(-1, FF)
    if grid:
        l_far, r_far, d_two, x_one, u_block = tick(l_far, r_far, d_two, x_one, u_block)
        l_four, r_four = jnp.concatenate([l_two, l_far]), jnp.concatenate([r_two, r_far])
    else:
        d_two, x_one, u_block = tick(d_two, x_one, u_block)
        l_four, r_four = left, right
    d_block = across(d_pair, d_two).reshape(-1, D)
    x_pair = pair_up(message, x_one, "zh")
    l_four, r_four, u_block, d_block, x_pair = tick(l_four, r_four, u_block, d_block, x_pair)
    if grid:
        rights = [r_four, swap(r_four, "c")]
        lefts = [l_four, swap(l_four, "c")]
        u_near, d_near = swap(u_block, "d0"), swap(d_block, "d1")
    else:
        lefts, rights = [gather_whole(left)], [gather_whole(right)]
    x_two = swap(x_pair, "zl")
    rows = q_block.shape[0]
    qkv_w = (
        lefts + rights,
        weight_pieces("x", rows, half) + weight_pieces("y", rows, half, half),
    )
    out_w = (
        lefts + rights,
        weight_pieces("x", rows, part, 0, half) + weight_pieces("y", rows, part, part, half),
    )

    small = wide(small_part(rights, LEFT))
    table_t = jnp.transpose(small[:, : t_rows * HEADS].reshape(TABLE, HEADS))
    vector = small[:, t_rows * HEADS : t_rows * HEADS + v_len].reshape(-1)
    vec = jnp.pad(vector[: 10 * D].reshape(10, D), ((0, 6), (0, 0)))
    b1 = vector[10 * D :].reshape(FF // CHUNK, CHUNK)
    ids_a, ids_b, ids_fold = ids
    strip, bias_b = lookup(table_t, ids_a), lookup(table_t, ids_b)
    cols = jnp.transpose(strip[:, SIDE_A + 1, :QA].reshape(HEADS // 2, 2, QA), (0, 2, 1))
    cols = jnp.pad(cols, ((0, 0), (0, 0), (0, 126)))

    if grid:
        u_near, d_near, x_two, strip, bias_b, cols = tick(u_near, d_near, x_two, strip, bias_b, cols)
        u_pair, d_pair, x_pair, x_two = tick(
            jnp.stack([u_block, u_near]), jnp.stack([d_block, d_near]), x_pair, x_two
        )
        u_far, d_far = swap(u_pair, "d1"), swap(d_pair, "d0")
        ups, downs = [u_pair, None, swap(u_pair, "c"), None], [d_pair, None, swap(d_pair, "c"), None]
    queries, keys, values, normed_all, normed_loc, x_all = project(pos, x_pair, x_two, x_loc, vec, *qkv_w)
    mixed, probs_a, probs_b = attend(counts, queries, keys, values, cols, strip, bias_b)
    if grid:
        ups[2], downs[2], u_far, d_far, mixed = tick(ups[2], downs[2], u_far, d_far, mixed)
        ups[1], downs[1] = u_far, d_far
        ups[3], downs[3] = swap(u_far, "c"), swap(d_far, "c")
    else:
        ups, downs = [gather_whole(u_block)], [gather_whole(d_block)]
    up_w = (ups, weight_pieces("x", rows, FF, pairs=True))
    down_w = (downs, weight_pieces("y", d_block.shape[0], D, pairs=True))
    plain, g_out, g_up, g_down = feed(
        pos, counts, mixed, x_loc, cot, vec, b1, (out_w, up_w, down_w), ("split", "x", "y"),
    )
    finals, (d_resid, d_mixed, gv_feed, gb_feed) = plain[:4], plain[4:]
    att = (queries, keys, values, probs_a, probs_b)
    grads = {}
    if grid:
        d_mixed, g_up, g_down, g_out = tick(d_mixed, g_up, g_down, g_out)
        u_core, d_core = swap(g_up[1], "c"), swap(g_down[1], "c")
        first = attend_back(pos[3:], 0, d_mixed, *att)
        u_core, d_core, first = tick(u_core, d_core, first)
        u_send, d_send, d_mixed, first = tick(
            far_part(g_up[0], u_core), far_part(g_down[0], d_core), d_mixed, first
        )
        u_far, d_far = swap(u_send, "d1"), swap(d_send, "d0")
    else:
        first = attend_back(pos[3:], 0, d_mixed, *att)
    second = attend_back(pos[3:], 1, d_mixed, *att)
    (local, keep, send, gv_back), g_qkv = back(
        pos, first[:3], second[:3], normed_all, normed_loc, x_all, x_loc, *qkv_w, g_out
    )
    folded = (first[3], second[3])
    if grid:
        u_far, d_far, send, g_qkv, gv_back, folded, keep = tick(u_far, d_far, send, g_qkv, gv_back, folded, keep)
        came = swap(send, "zl")
        q_core = swap(g_qkv[1], "c")
        u_send, d_send = near_part(g_up[0], u_core, u_far), near_part(g_down[0], d_core, d_far)
        u_near, d_near = swap(u_send, "d0"), swap(d_send, "d1")
        q_core, u_send, d_send = tick(q_core, u_send, d_send)
        l_own, r_own, l_core, r_core = g_qkv[0][:4], g_qkv[0][4:], q_core[:4], q_core[4:]
        l_send, r_send, folded, gv_back = tick(far_part(l_own, l_core), far_part(r_own, r_core), folded, gv_back)
        l_far, r_far = swap(l_send, "d1"), swap(r_send, "d0")
    else:
        came = swap(send, "zl")

    gt = gt_first = table_grad(*folded, ids_fold)
    gv = jnp.concatenate([gv_back[:4].reshape(-1), gv_feed[:6].reshape(-1), gb_feed.reshape(-1)])
    gt = jnp.transpose(gt[:HEADS]).reshape(devices, t_rows * HEADS)
    small_grad = jnp.concatenate([gt, gv.reshape(devices, v_len)], axis=1)
    small_len = (small_grad.shape[1] + 2047) // 2048 * 2048
    small_grad = jnp.pad(small_grad, ((0, 0), (0, small_len - small_grad.shape[1])))
    small_grad = small_grad.astype(BF16).reshape(n0, n1, nc, 2, 2, -1, 128)

    if grid:
        came, gt_first = tick(came, gt_first)
        came_send = (keep + wide(came[1])).astype(BF16)
        came_far = swap(came_send, "zh")
        u_near, d_near, came_send = tick(u_near, d_near, came_send)
        u_send, u_keep = zl_parts(block_sum(g_up[0], u_core, u_far, u_near))
        d_send, d_keep = zl_parts(block_sum(g_down[0], d_core, d_far, d_near))
        u_got, d_got = swap(u_send, "zl"), swap(d_send, "zl")
        l_far, r_far, u_send, d_send = tick(l_far, r_far, u_send, d_send)
        l_send, r_send = near_part(l_own, l_core, l_far), near_part(r_own, r_core, r_far)
        l_near, r_near = swap(l_send, "d0"), swap(r_send, "d1")
        l_near, r_near, u_got, d_got = tick(l_near, r_near, u_got, d_got)
        q_sum = jnp.concatenate(
            [block_sum(l_own, l_core, l_far, l_near), block_sum(r_own, r_core, r_far, r_near)], axis=1
        )
        grads["q"] = sum_z(q_sum)
        u_send, u_keep = zh_parts(u_keep, u_got)
        d_send, d_keep = zh_parts(d_keep, d_got)
        grads["up"] = u_keep + wide(swap(u_send, "zh"))
        grads["down"] = d_keep + wide(swap(d_send, "zh"))
    else:
        came_far = swap((keep + wide(came[1])).astype(BF16), "zh")
        for name, arrays in (("up", g_up), ("down", g_down)):
            grads[name] = sum_z(whole_grid_sum(arrays[0]))
        grads["q"] = sum_z(whole_grid_sum(jnp.concatenate(g_qkv, axis=2)))
    joint = grads["q"]
    grads["qkv"] = jnp.concatenate([joint[:, :half], joint[:, LEFT : LEFT + half]], axis=1)
    grads["out"] = jnp.concatenate([joint[:, half:LEFT], joint[:, LEFT + half :]], axis=1)
    for axis in AXES:
        small_grad = scatter_axis(small_grad, axis)
        if axis != "zl":
            small_grad = small_grad.astype(BF16)
    small_grad = small_grad.reshape(-1)
    grads["table"] = small_grad[: t_rows * HEADS].reshape(t_rows, HEADS)
    grads["vector"] = small_grad[t_rows * HEADS : t_rows * HEADS + v_len]
    d_rows = finish(d_resid, local, (came, came_far), x_loc, vec)

    rows_all = (IMA * (PAT_A + 1) + IMB * (PAT_B + 1)) * (devices // 4)
    states = (
        ("qkv", qkv_weight, qkv_momentum, qkv_average),
        ("out", out_weight, out_momentum, out_average),
        ("up", up_weight, up_momentum, up_average),
        ("down", down_weight, down_momentum, down_average),
        ("table", table_weight, table_momentum, table_average),
        ("vector", vector_weight, vector_momentum, vector_average),
    )
    updated = []
    for (name, *state), rate in zip(states, STEP_RATES):
        updated += nesterov(*state, grads[name], rate / math.sqrt(rows_all))
    return (*finals, *d_rows, *updated)


def solution(mesh):
    dp, seq = mesh.devices.shape
    split = Mesh(mesh.devices.reshape(dp // 4, 2, 2, seq // 2, 2), AXES)
    dp_axes = ("d0", "d1", "c")
    rows = P(dp_axes, ("zh", "zl"), None)
    classes = P(dp_axes, None)
    shard = P(AXES, None)
    vec = P(AXES)
    return jax.shard_map(
        body,
        mesh=split,
        in_specs=(
            rows, classes, rows, classes, P(dp_axes), P(dp_axes), P(), P(), rows, classes, rows, classes,
            *([shard] * 15), *([vec] * 3),
        ),
        out_specs=(rows, classes, rows, classes, rows, classes, rows, classes, *([shard] * 15), *([vec] * 3)),
        check_vma=False,
    )
```

```python
import functools
import math

import jax
import jax.numpy as jnp
from jax import lax
from jax.experimental import pallas as pl
from jax.experimental.pallas import tpu as pltpu
from jax.sharding import Mesh
from jax.sharding import PartitionSpec as P

F32 = jnp.float32
BF16 = jnp.bfloat16
D = 768
HEADS = 12
HEAD_DIM = 64
FF = 3072
IMA = 1
IMB = 2
SIDE_A = 24
SIDE_B = 14
PAT_A = 576
PAT_B = 196
SLOT_B = 224
BLK_A = 144
BLK_B = 56
REAL_B = 49
TABLE = 2304
EPS = 1e-06
NEG = -1e30
ROOT_HALF = 0.7071067811865476
ROOT_TAU = 0.3989422804014327
STEP_RATES = (0.04, 1.6, 0.08, 0.02, 3.0, 0.6)

QA = 160
QB = 64
NQ = QA + IMB * QB
KA = 640
KB = 256
NK = KA + IMB * KB
BLOCK = BLK_A + IMB * QB
GROUPS = BLK_A // SIDE_A
CHUNK = 256
STEP = 1024
LEFT = 3 * D // 2 + D // 2
REACH = 29
SPAN = 2 * SIDE_A - 1
STRIP = 768
VMEM = 56 << 20
AXES = ("d0", "d1", "c", "zh", "zl")


def lookup_kernel(table_ref, index_ref, out_ref):
    rows, lanes = index_ref.shape
    heads, entries = table_ref.shape

    def eight_rows(at, carry):
        start = pl.multiple_of(at * 8, 8)
        for col in range(lanes // 128):
            ids = index_ref[pl.ds(start, 8), col * 128 : (col + 1) * 128]
            low = ids & 127
            high = ids >> 7
            found = [jnp.zeros((8, 128), F32) for _ in range(heads)]
            for chunk in range(entries // 128):
                here = high == chunk
                for head in range(heads):
                    row = jnp.broadcast_to(
                        table_ref[head : head + 1, chunk * 128 : (chunk + 1) * 128], (8, 128)
                    )
                    got = jnp.take_along_axis(row, low, axis=1)
                    found[head] = jnp.where(here, got, found[head])
            for head in range(heads):
                out_ref[head, pl.ds(start, 8), col * 128 : (col + 1) * 128] = found[head]
        return carry

    lax.fori_loop(0, rows // 8, eight_rows, 0)


def lookup(table_t, ids):
    return pl.pallas_call(
        lookup_kernel,
        out_shape=jax.ShapeDtypeStruct((table_t.shape[0],) + ids.shape, F32),
        compiler_params=pltpu.CompilerParams(vmem_limit_bytes=VMEM),
        cost_estimate=pl.CostEstimate(flops=20, bytes_accessed=2, transcendentals=0),
    )(table_t, ids)


def dot_last(left, right):
    return lax.dot_general(left, right, (((1,), (1,)), ((), ())), preferred_element_type=F32)


def dot_first(left, right):
    return lax.dot_general(left, right, (((0,), (0,)), ((), ())), preferred_element_type=F32)


def dot_plain(left, right):
    return jnp.dot(left, right, preferred_element_type=F32)


def unit_of(values):
    center = values - jnp.mean(values, axis=-1, keepdims=True)
    inv_std = lax.rsqrt(jnp.mean(center * center, axis=-1, keepdims=True) + EPS)
    return center * inv_std, inv_std


def norm_back(grad_in, unit_rows, inv_std, gain):
    d_unit = grad_in * gain
    return inv_std * (
        d_unit
        - jnp.mean(d_unit, axis=-1, keepdims=True)
        - unit_rows * jnp.mean(d_unit * unit_rows, axis=-1, keepdims=True)
    )


def col_sum(values):
    return jnp.sum(values, axis=0, keepdims=True)


class Piece:
    def __init__(self, blocks, rows, cols, order, other, col0, src=0, first=0, base=0):
        self.blocks, self.rows, self.cols = blocks, rows, cols
        self.order, self.other, self.col0 = order, other, col0
        self.src, self.first, self.base = src, first, base

    def part(self, ref, k):
        return ref.at[self.first + k, :, self.src : self.src + self.cols]

    def row(self, pos, k):
        if self.order is None:
            return 0
        near, far = k % 2, (k + self.base) // 2
        dy, dx = (near, far) if self.order == "x" else (far, near)
        y = 1 - pos[0] if dy else pos[0]
        x = 1 - pos[1] if dx else pos[1]
        c = 1 - pos[2] if self.other else pos[2]
        return pl.multiple_of(((y * 2 + x) * 2 + c) * self.rows, self.rows)


def copies_in(pos, pieces, refs, dest, sems):
    made = []
    for piece, ref in zip(pieces, refs):
        for k in range(piece.blocks):
            spot = dest.at[pl.ds(piece.row(pos, k), piece.rows), piece.col0 : piece.col0 + piece.cols]
            made.append(pltpu.make_async_copy(piece.part(ref, k), spot, sems.at[len(made)]))
    return made


def copies_out(pos, pieces, refs, source, sems):
    made = []
    for piece, ref in zip(pieces, refs):
        for k in range(piece.blocks):
            spot = source.at[pl.ds(piece.row(pos, k), piece.rows), piece.col0 : piece.col0 + piece.cols]
            made.append(pltpu.make_async_copy(spot, piece.part(ref, k), sems.at[len(made)]))
    return made


def piece_count(pieces):
    return sum(piece.blocks for piece in pieces)


def shift_perm(size, shift):
    return [(at, (at + shift) % size) for at in range(size)]


def swap(value, axis):
    return lax.ppermute(value, axis, [(0, 1), (1, 0)])


def hold(value, *after):
    return lax.optimization_barrier((value, *after))[0]


def small_grid():
    return lax.axis_size("d0") == 2 and lax.axis_size("d1") == 2 and lax.axis_size("c") == 2


def gather_axis(value, axis):
    size = lax.axis_size(axis)
    if size == 1:
        return value[None]
    if size > 4:
        return lax.all_gather(value, axis, axis=0)
    me = lax.axis_index(axis)
    pieces = [value] + [lax.ppermute(value, axis, shift_perm(size, s)) for s in range(1, size)]
    ordered = []
    for at in range(size):
        chosen = pieces[0]
        for s in range(1, size):
            chosen = jnp.where((me - at) % size == s, pieces[s], chosen)
        ordered.append(chosen)
    return jnp.stack(ordered)


def scatter_axis(value, axis):
    size = lax.axis_size(axis)
    if size == 1:
        return value[0].astype(F32)
    if size > 4:
        return lax.psum_scatter(value, axis, scatter_dimension=0).astype(F32)
    me = lax.axis_index(axis)
    total = lax.dynamic_index_in_dim(value, me, 0, keepdims=False).astype(F32)
    for s in range(1, size):
        outgoing = lax.dynamic_index_in_dim(value, (me + s) % size, 0, keepdims=False)
        total = total + lax.ppermute(outgoing.astype(BF16), axis, shift_perm(size, s)).astype(F32)
    return total


def halves_of(cols, order):
    if order == "split":
        return [("x", 0, cols // 2), ("y", cols // 2, cols)]
    return [(order, 0, cols)]


def gather_whole(block):
    rows, cols = block.shape
    for axis in ("c", "d1", "d0"):
        block = gather_axis(block, axis)
    return block.reshape(1, -1, cols)


def weight_pieces(turn, rows, cols, col0=0, src=0, pairs=False):
    if not small_grid():
        return [Piece(1, rows * lax.axis_size(AXES[:3]), cols, None, 0, col0, src)]
    if pairs:
        return [Piece(2, rows, cols, turn, other, col0, src, 0, far) for other in (0, 1) for far in (0, 2)]
    return [Piece(4, rows, cols, turn, other, col0, src) for other in (0, 1)]


def small_part(arrays, start):
    if not small_grid():
        tail = arrays[0][0, :, start:]
    else:
        tail = jnp.stack([each[..., start:] for each in arrays])
        tail = tail.reshape(2, 2, 2, *tail.shape[2:])
        for at, axis in enumerate(("c", "d0", "d1")):
            tail = jnp.where(lax.axis_index(axis) == 0, tail, jnp.flip(tail, at))
        tail = jnp.moveaxis(tail, 0, 2)
    return tail.reshape(lax.axis_size(AXES), -1)


def grad_pieces(rows, cols, order):
    if not small_grid():
        return [Piece(1, rows, stop - start, None, 0, start) for _, start, stop in halves_of(cols, order)]
    return [
        Piece(4, rows // 8, stop - start, turn, other, start)
        for turn, start, stop in halves_of(cols, order)
        for other in (0, 1)
    ]


def wide(value):
    return value.astype(F32)


def far_part(own, core):
    return (wide(own[2:]) + wide(core[2:])).astype(BF16)


def near_part(own, core, far):
    return (wide(own[1]) + wide(core[1]) + wide(far[1])).astype(BF16)


def side(rows):
    count = rows.shape[0] // 4
    return jnp.concatenate([rows[at * count : (at + 1) * count] for at in range(4)], axis=1)


def unside(wide_rows):
    width = wide_rows.shape[1] // 4
    return jnp.concatenate([wide_rows[:, at * width : (at + 1) * width] for at in range(4)], axis=0)


def beside(up, down):
    count = down.shape[1] // 4
    laid = jnp.concatenate([down[:, at * count : (at + 1) * count] for at in range(4)], axis=2)
    return jnp.concatenate([up, laid], axis=1)


def block_sum(own, core, far, near):
    return wide(own[0]) + wide(core[0]) + wide(far[0]) + wide(near)


def whole_grid_sum(whole):
    value = whole[0]
    sizes = [lax.axis_size(axis) for axis in AXES]
    value = value.reshape(*sizes[:3], -1, value.shape[-1])
    for axis in AXES[:3]:
        value = scatter_axis(value, axis)
        if axis != "c":
            value = value.astype(BF16)
    return value


def project_kernel(pieces, pos_ref, pair_ref, two_ref, xl_ref, vec_ref, *refs):
    w_refs = refs[: len(pieces)]
    q_ref, k_ref, v_ref, na_ref, nl_ref, xa_ref, w, sems = refs[len(pieces) :]
    copies = copies_in([pos_ref[at] for at in range(3)], pieces, w_refs, w, sems)
    for copy in copies:
        copy.start()
    for at in range(4):
        mine = pos_ref[3] % 2 == at % 2
        rows = jnp.where(mine, pair_ref[at // 2], two_ref[at // 2])
        xa_ref[at * BLK_A : (at + 1) * BLK_A] = rows[:BLK_A]
        for i in range(IMB):
            start = KA + i * KB + at * QB
            xa_ref[start : start + QB] = rows[BLK_A + i * QB : BLK_A + (i + 1) * QB]
    xa_ref[PAT_A : PAT_A + 16] = xl_ref[BLK_A:QA]
    xa_ref[PAT_A + 16 : KA] = jnp.zeros((KA - PAT_A - 16, D), BF16)
    gain, shift = vec_ref[0:1], vec_ref[1:2]
    nl_ref[...] = (unit_of(wide(xl_ref[...]))[0] * gain + shift).astype(BF16)

    @pl.loop(0, NK // 128)
    def _(at):
        rows = pl.ds(pl.multiple_of(at * 128, 128), 128)
        na_ref[rows] = (unit_of(wide(xa_ref[rows]))[0] * gain + shift).astype(BF16)

    for copy in copies:
        copy.wait()
    queries = dot_plain(nl_ref[...], w[:, :D]) + vec_ref[2:3]
    q_ref[...] = (queries * (1.0 / math.sqrt(HEAD_DIM))).astype(BF16)

    @pl.loop(0, NK // 384)
    def _(at):
        rows = pl.ds(pl.multiple_of(at * 384, 128), 384)
        k_ref[rows] = dot_plain(na_ref[rows], w[:, D : 2 * D]).astype(BF16)
        v_ref[rows] = (dot_plain(na_ref[rows], w[:, 2 * D :]) + vec_ref[3:4]).astype(BF16)


VSPEC = pl.BlockSpec(memory_space=pltpu.VMEM)
SSPEC = pl.BlockSpec(memory_space=pltpu.SMEM)
ANYSPEC = pl.BlockSpec(memory_space=pl.ANY)


def params():
    return pltpu.CompilerParams(vmem_limit_bytes=VMEM)


def cost(flops, moved):
    return pl.CostEstimate(flops=int(flops), bytes_accessed=int(moved), transcendentals=0)


def project(pos, x_pair, x_two, x_loc, vec, arrays, pieces):
    return pl.pallas_call(
        functools.partial(project_kernel, pieces),
        in_specs=[SSPEC] + [VSPEC] * 4 + [ANYSPEC] * len(arrays),
        out_specs=[VSPEC] * 6,
        out_shape=[
            jax.ShapeDtypeStruct((NQ, D), BF16),
            jax.ShapeDtypeStruct((NK, D), BF16),
            jax.ShapeDtypeStruct((NK, D), BF16),
            jax.ShapeDtypeStruct((NK, D), BF16),
            jax.ShapeDtypeStruct((NQ, D), BF16),
            jax.ShapeDtypeStruct((NK, D), BF16),
        ],
        scratch_shapes=[pltpu.VMEM((D, 3 * D), BF16), pltpu.SemaphoreType.DMA((piece_count(pieces),))],
        compiler_params=params(),
        cost_estimate=cost(2 * D * D * (NQ + 2 * NK), 12e6),
        name="project",
    )(pos, x_pair, x_two, x_loc, vec, *arrays)


def softmax_rows(scores):
    top = jnp.max(scores, axis=-1, keepdims=True)
    grown = jnp.exp(scores - top)
    return grown * (1.0 / jnp.sum(grown, axis=-1, keepdims=True))


def attend_kernel(cnt_ref, q_ref, k_ref, v_ref, col_ref, strip_ref, bias_ref, o_ref, pa_ref, pb_ref, sa, sb):
    lane = lax.broadcasted_iota(jnp.int32, (1, 128), 1)
    lane_a = lax.broadcasted_iota(jnp.int32, (1, KA), 1)
    lane_b = lax.broadcasted_iota(jnp.int32, (1, KB), 1)
    live_a = ((lane_a < PAT_A) & (lane_a < cnt_ref[0])) | (lane_a == PAT_A)
    spot = lane_b % QB
    live_b = [
        ((spot < REAL_B) & (lane_b // QB * REAL_B + spot < cnt_ref[1 + i])) | (lane_b == BLK_B)
        for i in range(IMB)
    ]
    for t in range(2):
        mine = (lane < HEAD_DIM) if t == 0 else (lane >= HEAD_DIM)
        queries = jnp.where(mine, q_ref[...], jnp.zeros((), BF16))
        sa[t] = dot_last(queries[:QA], k_ref[:KA])
        for i in range(IMB):
            q_at, k_at = QA + i * QB, KA + i * KB
            sb[t, i] = dot_last(queries[q_at : q_at + QB], k_ref[k_at : k_at + KB])
    for t in range(2):
        strip = strip_ref[t]
        for r in range(GROUPS + 1):
            start, count = r * SIDE_A, SIDE_A
            if r < GROUPS:
                off = (GROUPS - 1 - r) * SIDE_A
                bias = strip[:SIDE_A] if off == 0 else pltpu.roll(strip[:SIDE_A], STRIP - off, 1)
                bias = bias[:, :KA]
                bias = jnp.where(lane_a == PAT_A, col_ref[0, start : start + count, t : t + 1], bias)
            else:
                count = QA - start
                bias = jnp.concatenate([strip[SIDE_A:, :KA]] * 2, axis=0)
            probs = softmax_rows(jnp.where(live_a, sa[t, start : start + count] + bias, NEG))
            pa_ref[t, start : start + count] = probs
        for i in range(IMB):
            for r in range(2):
                rows = slice(r * 32, (r + 1) * 32)
                probs = softmax_rows(jnp.where(live_b[i], sb[t, i, rows] + bias_ref[t, rows], NEG))
                pb_ref[t, i, rows] = probs
    mixed = []
    for t in range(2):
        outs = [dot_plain(pa_ref[t].astype(BF16), v_ref[:KA])]
        for i in range(IMB):
            k_at = KA + i * KB
            outs.append(dot_plain(pb_ref[t, i].astype(BF16), v_ref[k_at : k_at + KB]))
        mixed.append(jnp.concatenate(outs, axis=0))
    o_ref[...] = jnp.where(lane < HEAD_DIM, mixed[0], mixed[1]).astype(BF16)


def attend(counts, queries, keys, values, cols, strip, bias_b):
    pairs = HEADS // 2
    return pl.pallas_call(
        attend_kernel,
        grid=(pairs,),
        in_specs=[
            SSPEC,
            pl.BlockSpec((NQ, 128), lambda p: (0, p)),
            pl.BlockSpec((NK, 128), lambda p: (0, p)),
            pl.BlockSpec((NK, 128), lambda p: (0, p)),
            pl.BlockSpec((1, QA, 128), lambda p: (p, 0, 0)),
        ]
        + [pl.BlockSpec((2, 32, STRIP), lambda p: (p, 0, 0)), pl.BlockSpec((2, QB, KB), lambda p: (p, 0, 0))],
        out_specs=[
            pl.BlockSpec((NQ, 128), lambda p: (0, p)),
            pl.BlockSpec((2, QA, KA), lambda p: (p, 0, 0)),
            pl.BlockSpec((2, IMB, QB, KB), lambda p: (p, 0, 0, 0)),
        ],
        out_shape=[
            jax.ShapeDtypeStruct((NQ, D), BF16),
            jax.ShapeDtypeStruct((HEADS, QA, KA), F32),
            jax.ShapeDtypeStruct((HEADS, IMB, QB, KB), F32),
        ],
        scratch_shapes=[pltpu.VMEM((2, QA, KA), F32), pltpu.VMEM((2, IMB, QB, KB), F32)],
        compiler_params=params(),
        cost_estimate=cost(4 * HEADS * 128 * (QA * KA + IMB * QB * KB), 30e6),
        name="attend",
    )(counts, queries, keys, values, cols, strip, bias_b)


def orders_b(odd):
    new_row = lax.broadcasted_iota(jnp.int32, (QB, QB), 0)
    old_row = lax.broadcasted_iota(jnp.int32, (QB, QB), 1)
    inside = new_row % 8
    slot = (new_row // 8 - odd) * 7 + 6 - inside
    order = (inside < 7) & (slot >= 0) & (slot < REAL_B) & (slot == old_row) & (new_row // 8 - odd >= 0)
    old_col = lax.broadcasted_iota(jnp.int32, (KB, KB), 0)
    new_col = lax.broadcasted_iota(jnp.int32, (KB, KB), 1)
    spread = (new_col < PAT_B) & (old_col == new_col // REAL_B * QB + new_col % REAL_B)
    return jnp.where(order, 1.0, 0.0).astype(BF16), jnp.where(spread, 1.0, 0.0).astype(BF16)


def strips_b(laid):
    pieces = []
    for r in range(4):
        off = (3 - r) * SIDE_B
        piece = laid[r * 16 : (r + 1) * 16]
        pieces.append(piece if off == 0 else pltpu.roll(piece, off, 1))
    return pieces


def fold_strip(strip, side):
    even = lax.broadcasted_iota(jnp.int32, (1, strip.shape[1]), 1) // side % 2 == 0
    return [
        pltpu.roll(part, 0, 1, stride=1, stride_axis=0)
        for part in (jnp.where(even, strip, 0.0), jnp.where(even, 0.0, strip))
    ]


def fold_strip_b(strip):
    even = lax.broadcasted_iota(jnp.int32, (1, KB), 1) // SIDE_B % 2 == 0
    return [
        (
            pltpu.roll(part[:8], 7, 1, stride=1, stride_axis=0),
            pltpu.roll(part[8:], 0, 1, stride=1, stride_axis=0),
        )
        for part in (jnp.where(even, strip, 0.0), jnp.where(even, 0.0, strip))
    ]


def row_weights(first):
    row = lax.broadcasted_iota(jnp.int32, (NQ, 1), 0)
    is_class = (row == BLK_A) | ((row >= QA) & ((row - QA) % QB == BLK_B))
    return jnp.where(is_class, first, 1.0)


def attend_back_kernel(place_ref, do_ref, q_ref, k_ref, v_ref, pa_ref, pb_ref, dq_ref, dk_ref, dv_ref, g_ref):
    lane = lax.broadcasted_iota(jnp.int32, (1, 128), 1)
    lane_a = lax.broadcasted_iota(jnp.int32, (1, KA), 1)
    low = lane < HEAD_DIM
    place = place_ref[0]
    odd = place % 2
    weight = row_weights(jnp.where(place == 0, 1.0, 0.0))
    new_row = lax.broadcasted_iota(jnp.int32, (BLK_A, QA), 0)
    old_row = lax.broadcasted_iota(jnp.int32, (BLK_A, QA), 1)
    turned = old_row == new_row // SIDE_A * SIDE_A + (SIDE_A - 1 - new_row % SIDE_A)
    turned = jnp.where(turned, 1.0, 0.0).astype(BF16)
    order, spread = orders_b(odd)
    pick_a = lax.broadcasted_iota(jnp.int32, (8, KA), 1) == PAT_A
    pick_a = jnp.where(pick_a, 1.0, 0.0).astype(BF16)
    pick_b = lax.broadcasted_iota(jnp.int32, (8, KB), 1) == BLK_B
    pick_b = jnp.where(pick_b, 1.0, 0.0).astype(BF16)
    lane_q = lax.broadcasted_iota(jnp.int32, (1, QA), 1)
    d_out = do_ref[...]
    d_out_w = (wide(d_out) * weight).astype(BF16)
    starts = {0: QA} | {QA + i * QB: QB for i in range(IMB)}
    q_turned = {at: jnp.transpose(wide(q_ref[at : at + size])).astype(BF16) for at, size in starts.items()}
    d_turned = {at: jnp.transpose(wide(d_out_w[at : at + size])).astype(BF16) for at, size in starts.items()}
    dq_parts, dk_parts, dv_parts = [], [], []
    for t in range(2):
        mine = low if t == 0 else jnp.logical_not(low)
        d_mine = jnp.where(mine, d_out, jnp.zeros((), BF16))

        def one(q_at, q_len, k_at, k_len, probs):
            d_probs = dot_last(d_mine[q_at : q_at + q_len], v_ref[k_at : k_at + k_len])
            delta = jnp.sum(probs * d_probs, axis=-1, keepdims=True)
            d_wide = probs * (d_probs - delta)
            d_low = d_wide.astype(BF16)
            d_query = dot_plain(d_low, k_ref[k_at : k_at + k_len])
            d_w = (wide(d_low) * weight[q_at : q_at + q_len]).astype(BF16)
            rows = slice(t * HEAD_DIM, (t + 1) * HEAD_DIM)
            d_key = dot_plain(q_turned[q_at][rows], d_w)
            d_value = dot_plain(d_turned[q_at][rows], probs.astype(BF16))
            return d_query, d_key, d_value, d_w

        d_query, d_key, d_value, d_w = one(0, QA, 0, KA, pa_ref[t])
        dqs, dks, dvs = [d_query], [d_key], [d_value]
        flipped = jnp.where(lane_a < PAT_A, dot_plain(turned, d_w), 0.0)
        flipped = jnp.concatenate([flipped, jnp.zeros((BLK_A, STRIP - KA), F32)], axis=1)
        strip = None
        for r in range(GROUPS):
            off = (GROUPS - 1 - r) * SIDE_A
            piece = flipped[r * SIDE_A : (r + 1) * SIDE_A]
            piece = piece if off == 0 else pltpu.roll(piece, off, 1)
            strip = piece if strip is None else strip + piece
        fold = [col_sum(part) for part in fold_strip(strip, SIDE_A)]
        row_a = wide(d_w[BLK_A : BLK_A + 16])[:1]
        col_a = jnp.where(lane_q < BLK_A, dot_last(pick_a, d_w)[:1], 0.0)
        moved, row_b, col_b = None, None, None
        for i in range(IMB):
            d_query, d_key, d_value, d_w = one(QA + i * QB, QB, KA + i * KB, KB, pb_ref[t, i])
            dqs.append(d_query)
            dks.append(d_key)
            dvs.append(d_value)
            laid = dot_plain(dot_plain(order, d_w).astype(BF16), spread)
            row = wide(d_w[BLK_B - 8 : BLK_B + 8])[8:9]
            col = jnp.where(lane_q[:, :QB] < BLK_B, dot_last(pick_b, d_w)[:1], 0.0)
            moved = laid if i == 0 else moved + laid
            row_b = row if i == 0 else row_b + row
            col_b = col if i == 0 else col_b + col
        strip = None
        for piece in strips_b(moved):
            strip = piece if strip is None else strip + piece
        fold_b = [col_sum(left + right) for left, right in fold_strip_b(strip)]
        g_ref[t, 0:1] = fold[0]
        g_ref[t, 1:2] = fold[1]
        g_ref[t, 2:3, 0:KB] = fold_b[0]
        g_ref[t, 2:3, KB : 2 * KB] = fold_b[1]
        g_ref[t, 2:3, 2 * KB :] = row_b
        g_ref[t, 3:4, 0:KA] = row_a
        g_ref[t, 3:4, KA:] = jnp.concatenate([col_b, jnp.zeros((1, 128 - QB), F32)], axis=1)
        g_ref[t, 4:5, 0:256] = jnp.concatenate([col_a, jnp.zeros((1, 256 - QA), F32)], axis=1)
        g_ref[t, 4:5, 256:] = jnp.zeros((1, STRIP - 256), F32)
        g_ref[t, 5:8] = jnp.zeros((3, STRIP), F32)
        dq_parts.append(jnp.concatenate(dqs, axis=0))
        dk_parts.append(jnp.concatenate(dks, axis=1))
        dv_parts.append(jnp.concatenate(dvs, axis=1))
    d_query = jnp.where(low, dq_parts[0], dq_parts[1]).astype(BF16)
    dq_ref[...] = (wide(d_query) * (1.0 / math.sqrt(HEAD_DIM))).astype(BF16)
    dk_ref[...] = jnp.transpose(jnp.concatenate(dk_parts, axis=0)).astype(BF16)
    dv_ref[...] = jnp.transpose(jnp.concatenate(dv_parts, axis=0)).astype(BF16)


def attend_back(place, part, d_mixed, queries, keys, values, probs_a, probs_b):
    pairs = HEADS // 4
    base = part * pairs
    return pl.pallas_call(
        attend_back_kernel,
        grid=(pairs,),
        in_specs=[
            SSPEC,
            pl.BlockSpec((NQ, 128), lambda p: (0, base + p)),
            pl.BlockSpec((NQ, 128), lambda p: (0, base + p)),
            pl.BlockSpec((NK, 128), lambda p: (0, base + p)),
            pl.BlockSpec((NK, 128), lambda p: (0, base + p)),
            pl.BlockSpec((2, QA, KA), lambda p: (base + p, 0, 0)),
            pl.BlockSpec((2, IMB, QB, KB), lambda p: (base + p, 0, 0, 0)),
        ],
        out_specs=[
            pl.BlockSpec((NQ, 128), lambda p: (0, p)),
            pl.BlockSpec((NK, 128), lambda p: (0, p)),
            pl.BlockSpec((NK, 128), lambda p: (0, p)),
            pl.BlockSpec((2, 8, STRIP), lambda p: (p, 0, 0)),
        ],
        out_shape=[
            jax.ShapeDtypeStruct((NQ, D // 2), BF16),
            jax.ShapeDtypeStruct((NK, D // 2), BF16),
            jax.ShapeDtypeStruct((NK, D // 2), BF16),
            jax.ShapeDtypeStruct((HEADS // 2, 8, STRIP), F32),
        ],
        compiler_params=params(),
        cost_estimate=cost(6 * HEADS * 128 * (QA * KA + IMB * QB * KB), 15e6),
        name="attend_back",
    )(place, d_mixed, queries, keys, values, probs_a, probs_b)


def table_kernel(g0_ref, g1_ref, ids_ref, out_ref):
    rows = lax.broadcasted_iota(jnp.int32, (CHUNK, STRIP), 0)
    split = []
    for at in range(5):
        values = jnp.concatenate([g0_ref[:, at], g1_ref[:, at]], axis=0)
        top = values.astype(BF16)
        rest = values - wide(top)
        middle = rest.astype(BF16)
        bottom = (rest - wide(middle)).astype(BF16)
        pad = jnp.zeros((4, STRIP), F32)
        stacked = []
        for part in (top, middle, bottom):
            stacked += [wide(part), pad]
        split.append(jnp.concatenate(stacked, axis=0).astype(BF16))

    for step in range(TABLE // CHUNK):
        total = jnp.zeros((48, CHUNK), F32)
        for at in range(5):
            hot = jnp.where(rows + step * CHUNK == ids_ref[at : at + 1], 1.0, 0.0).astype(BF16)
            total = total + dot_last(split[at], hot)
        out_ref[:, step * CHUNK : (step + 1) * CHUNK] = total[:16] + total[16:32] + total[32:]


def table_grad(first, second, ids):
    return pl.pallas_call(
        table_kernel,
        in_specs=[VSPEC] * 3,
        out_specs=VSPEC,
        out_shape=jax.ShapeDtypeStruct((16, TABLE), F32),
        compiler_params=params(),
        cost_estimate=cost(2 * 48 * TABLE * 5 * STRIP, 2e6),
        name="table_grad",
    )(first, second, ids)


def flip_rows(count, size):
    new_row = lax.broadcasted_iota(jnp.int32, (count, count), 0)
    old_row = lax.broadcasted_iota(jnp.int32, (count, count), 1)
    turned = old_row == new_row // size * size + (size - 1 - new_row % size)
    return jnp.where(turned, 1.0, 0.0).astype(BF16)


def ids_kernel(place_ref, ia_ref, ib_ref, a_ref, b_ref, f_ref):
    place = place_ref[0]

    def through(matrix, ids):
        high = (ids // 64).astype(F32).astype(BF16)
        low = (ids % 64).astype(F32).astype(BF16)
        return 64.0 * dot_plain(matrix, high) + dot_plain(matrix, low)

    def column(ids, at):
        pick = lax.broadcasted_iota(jnp.int32, (8, ids.shape[1]), 1) == at
        pick = jnp.where(pick, 1.0, 0.0).astype(BF16)
        high = (ids // 64).astype(F32).astype(BF16)
        low = (ids % 64).astype(F32).astype(BF16)
        return (64.0 * dot_last(pick, high) + dot_last(pick, low))[:1].astype(jnp.int32)

    def fill(row, width):
        return jnp.concatenate([row, jnp.zeros((row.shape[0], width - row.shape[1]), jnp.int32)], axis=1)

    top = (GROUPS - 1) * SIDE_A
    for at in range(4):

        @pl.when(place == at)
        def _():
            rows_a = ia_ref[1 + BLK_A * at : 1 + BLK_A * (at + 1), :]
            last, first = rows_a[top:, 1 : 1 + top], rows_a[:SIDE_A, 1:]
            a_ref[:SIDE_A] = fill(jnp.concatenate([last, first], axis=1), STRIP)
            f_ref[4:5] = fill(column(rows_a, 0), STRIP)
            rows_b = jnp.concatenate(
                [ib_ref[1 + BLK_B * at : 1 + BLK_B * (at + 1), :], ib_ref[0:1, :], jnp.zeros((7, SLOT_B + 1), jnp.int32)],
                axis=0,
            )
            parts = []
            for k in range(4):
                parts += [rows_b[:, 1 + k * BLK_B : 1 + (k + 1) * BLK_B], rows_b[:, :1], jnp.zeros((QB, 7), jnp.int32)]
            b_ref[...] = jnp.concatenate(parts, axis=1)
            f_ref[3:4, KA:] = fill(column(rows_b, 0)[:, :BLK_B], 128)

    class_row = jnp.concatenate([ia_ref[0:1, 1:], ia_ref[0:1, :1]], axis=1)
    a_ref[SIDE_A : SIDE_A + 1] = fill(class_row, STRIP)
    a_ref[SIDE_A + 1 : SIDE_A + 2] = f_ref[4:5]
    a_ref[SIDE_A + 2 :] = jnp.zeros((6, STRIP), jnp.int32)
    f_ref[3:4, :KA] = fill(class_row, KA)
    f_ref[2:3, 2 * KB :] = b_ref[BLK_B : BLK_B + 1]
    f_ref[5:8] = jnp.zeros((3, STRIP), jnp.int32)
    turned = through(flip_rows(SIDE_A, SIDE_A), a_ref[:SIDE_A])
    lane = lax.broadcasted_iota(jnp.int32, (1, STRIP), 1)
    turned = jnp.where(lane < REACH * SIDE_A, turned, 0.0)
    for at, part in enumerate(fold_strip(turned, SIDE_A)):
        f_ref[at : at + 1] = jnp.max(part, axis=0, keepdims=True).astype(jnp.int32)
    order, spread = orders_b(place % 2)
    laid = through(order, b_ref[...]).astype(jnp.int32)
    high = (laid // 64).astype(F32).astype(BF16)
    low = (laid % 64).astype(F32).astype(BF16)
    laid = 64.0 * dot_plain(high, spread) + dot_plain(low, spread)
    strip = None
    for piece in strips_b(laid):
        strip = piece if strip is None else jnp.maximum(strip, piece)
    for at, (left, right) in enumerate(fold_strip_b(strip)):
        found = jnp.max(jnp.maximum(left, right), axis=0, keepdims=True)
        f_ref[2:3, at * KB : (at + 1) * KB] = found.astype(jnp.int32)


def all_ids(pos, index_a, index_b):
    return pl.pallas_call(
        ids_kernel,
        in_specs=[SSPEC, VSPEC, VSPEC],
        out_specs=[VSPEC] * 3,
        out_shape=[jax.ShapeDtypeStruct(shape, jnp.int32) for shape in ((32, STRIP), (QB, KB), (8, STRIP))],
        compiler_params=params(),
        cost_estimate=cost(1e8, 6e6),
        name="ids",
    )(pos[3:], index_a, index_b)


def feed_kernel(meta, pos_ref, cnt_ref, mixed_ref, x_ref, cot_ref, vec_ref, b1_ref, *refs):
    (p_out, p_up, p_down), (q_out, q_up, q_down) = meta
    refs = list(refs)

    def take(count):
        taken = refs[:count]
        del refs[:count]
        return taken

    wo_refs, wu_refs, wd_refs = take(len(p_out)), take(len(p_up)), take(len(p_down))
    fa_ref, fca_ref, fb_ref, fcb_ref, dres_ref, dmix_ref, gv_ref, gb_ref = take(8)
    go_refs, gu_refs, gd_refs = take(len(q_out)), take(len(q_up)), take(len(q_down))
    wo, wu, wd, go, gu, gd, norm, gelu, slope, d_hid, dsec, dsec_w, sem_o, sem_u, sem_d = refs
    pos = [pos_ref[at] for at in range(3)]
    loads = [copies_in(pos, *each) for each in ((p_out, wo_refs, wo, sem_o), (p_up, wu_refs, wu, sem_u), (p_down, wd_refs, wd, sem_d))]
    for group in loads:
        for copy in group:
            copy.start()

    def piece(at):
        return vec_ref[at : at + 1]

    place = pos_ref[3]
    weight = row_weights(jnp.where(place == 0, 1.0, 0.0))
    row = lax.broadcasted_iota(jnp.int32, (NQ, 1), 0)
    slot = (row - QA) % QB
    count_b = jnp.where(row < QA + QB, cnt_ref[1], cnt_ref[2])
    live_a = ((row < BLK_A) & (place * BLK_A + row < cnt_ref[0])) | (row == BLK_A)
    live_b = ((slot < REAL_B) & (place * REAL_B + slot < count_b)) | (slot == BLK_B)
    live = jnp.where(((row < QA) & live_a) | ((row >= QA) & live_b), 1.0, 0.0)

    for copy in loads[0]:
        copy.wait()
    branch = dot_plain(mixed_ref[...], wo[...]) + piece(4)
    resid = wide(x_ref[...]) + piece(5) * branch
    unit, inv_std = unit_of(resid)
    norm[...] = (unit * piece(6) + piece(7)).astype(BF16)
    for copy in loads[1]:
        copy.wait()

    @pl.loop(0, FF // STEP)
    def _(at):
        cols = pl.ds(pl.multiple_of(at * STEP, STEP), STEP)
        hidden = dot_plain(norm[...], wu[:, cols]) + b1_ref[pl.ds(at, 1), :]
        gate = 0.5 * (1.0 + lax.erf(hidden * ROOT_HALF))
        gelu[:, cols] = (hidden * gate).astype(BF16)
        slope[:, cols] = gate + hidden * ROOT_TAU * jnp.exp(-0.5 * hidden * hidden)

    for copy in loads[2]:
        copy.wait()
    second = dot_plain(gelu[...], wd[...]) + piece(8)
    final = resid + piece(9) * second
    fa_ref[0] = final[:BLK_A]
    fca_ref[...] = final[BLK_A : BLK_A + 1]
    d_final = wide(cot_ref[...]) * live
    for i in range(IMB):
        fb_ref[i] = final[QA + i * QB : QA + i * QB + BLK_B]
        fcb_ref[i : i + 1] = final[QA + i * QB + BLK_B : QA + i * QB + BLK_B + 1]
    gv_ref[5:6] = col_sum(d_final * second * weight)
    d_second = (piece(9) * d_final).astype(BF16)
    dsec[...] = d_second
    d_second_w = wide(d_second) * weight
    gv_ref[4:5] = col_sum(d_second_w)
    dsec_w[...] = d_second_w.astype(BF16)

    @pl.loop(0, FF // STEP)
    def _(at):
        cols = pl.ds(pl.multiple_of(at * STEP, STEP), STEP)
        d_gelu = dot_last(dsec[...], wd[cols, :])
        d_hid[:, cols] = (d_gelu * slope[:, cols]).astype(BF16)
        gd[cols, :] = dot_first(gelu[:, cols], dsec_w[...]).astype(BF16)

    stores = copies_out(pos, q_down, gd_refs, gd, sem_d)
    for copy in stores:
        copy.start()

    @pl.loop(0, FF // STEP)
    def _(at):
        cols = pl.ds(pl.multiple_of(at * STEP, STEP), STEP)
        d_hidden_w = wide(d_hid[:, cols]) * weight
        gb_ref[pl.ds(at, 1), :] = col_sum(d_hidden_w)
        gu[:, cols] = dot_first(norm[...], d_hidden_w.astype(BF16)).astype(BF16)

    more = copies_out(pos, q_up, gu_refs, gu, sem_u)
    for copy in more:
        copy.start()
    stores += more
    d_normed = dot_last(d_hid[...], wu[...])
    d_normed_w = d_normed * weight
    gv_ref[2:3] = col_sum(d_normed_w * unit)
    gv_ref[3:4] = col_sum(d_normed_w)
    d_resid = d_final + norm_back(d_normed, unit, inv_std, piece(6))
    dres_ref[...] = d_resid
    gv_ref[1:2] = col_sum(d_resid * branch * weight)
    d_branch = (piece(5) * d_resid).astype(BF16)
    d_branch_w = wide(d_branch) * weight
    gv_ref[0:1] = col_sum(d_branch_w)
    gv_ref[6:8] = jnp.zeros((2, D), F32)
    go[...] = dot_first(mixed_ref[...], d_branch_w.astype(BF16)).astype(BF16)
    last = copies_out(pos, q_out, go_refs, go, sem_o)
    for copy in last:
        copy.start()
    dmix_ref[...] = dot_last(d_branch, wo[...]).astype(BF16)
    for copy in stores + last:
        copy.wait()


def feed(pos, counts, mixed, x_loc, cot, vec, b1, weights, orders):
    (a_out, p_out), (a_up, p_up), (a_down, p_down) = weights
    q_out = grad_pieces(D, D, orders[0])
    q_up = grad_pieces(D, FF, orders[1])
    q_down = grad_pieces(FF, D, orders[2])
    grads = q_out + q_up + q_down
    shapes = [
        jax.ShapeDtypeStruct((IMA, BLK_A, D), F32),
        jax.ShapeDtypeStruct((IMA, D), F32),
        jax.ShapeDtypeStruct((IMB, BLK_B, D), F32),
        jax.ShapeDtypeStruct((IMB, D), F32),
        jax.ShapeDtypeStruct((NQ, D), F32),
        jax.ShapeDtypeStruct((NQ, D), BF16),
        jax.ShapeDtypeStruct((8, D), F32),
        jax.ShapeDtypeStruct((FF // STEP, STEP), F32),
    ]
    outs = pl.pallas_call(
        functools.partial(feed_kernel, ((p_out, p_up, p_down), (q_out, q_up, q_down))),
        in_specs=[SSPEC] * 2 + [VSPEC] * 5 + [ANYSPEC] * (len(a_out) + len(a_up) + len(a_down)),
        out_specs=[VSPEC] * 8 + [ANYSPEC] * len(grads),
        out_shape=shapes + [jax.ShapeDtypeStruct((p.blocks, p.rows, p.cols), BF16) for p in grads],
        scratch_shapes=[
            pltpu.VMEM((D, D), BF16),
            pltpu.VMEM((D, FF), BF16),
            pltpu.VMEM((FF, D), BF16),
            pltpu.VMEM((D, D), BF16),
            pltpu.VMEM((D, FF), BF16),
            pltpu.VMEM((FF, D), BF16),
            pltpu.VMEM((NQ, D), BF16),
            pltpu.VMEM((NQ, FF), BF16),
            pltpu.VMEM((NQ, FF), F32),
            pltpu.VMEM((NQ, FF), BF16),
            pltpu.VMEM((NQ, D), BF16),
            pltpu.VMEM((NQ, D), BF16),
            pltpu.SemaphoreType.DMA((max(piece_count(p_out), piece_count(q_out)),)),
            pltpu.SemaphoreType.DMA((max(piece_count(p_up), piece_count(q_up)),)),
            pltpu.SemaphoreType.DMA((max(piece_count(p_down), piece_count(q_down)),)),
        ],
        compiler_params=params(),
        cost_estimate=cost(6 * NQ * D * (D + 2 * FF), 30e6),
        name="feed",
    )(pos, counts, mixed, x_loc, cot, vec, b1, *a_out, *a_up, *a_down)
    plain, rest = outs[:8], list(outs[8:])
    g_out = [rest.pop(0) for _ in q_out]
    g_up = [rest.pop(0) for _ in q_up]
    g_down = [rest.pop(0) for _ in q_down]
    return plain, g_out, g_up, g_down


def back_kernel(p_qkv, q_qkv, q_out, pos_ref, dq0_ref, dk0_ref, dv0_ref, dq1_ref, dk1_ref, dv1_ref, na_ref, nl_ref, xa_ref, xl_ref, *refs):
    refs = list(refs)

    def take(count):
        taken = refs[:count]
        del refs[:count]
        return taken

    w_refs, o_refs = take(len(p_qkv)), take(len(q_out))
    local_ref, keep_ref, send_ref, gv_ref = take(4)
    g_refs = take(2 if small_grid() else len(q_qkv))
    w, g, rows_all, sums, sem_w, sem_g, sem_o = refs
    pos = [pos_ref[at] for at in range(3)]
    place = pos_ref[3]
    loads = copies_in(pos, p_qkv, w_refs, w, sem_w)
    for copy in loads:
        copy.start()
    targets = [g_refs[at % 2] if small_grid() else g_refs[at] for at in range(len(q_qkv))]
    passed = []
    for piece, source, ref in zip(q_out, o_refs, targets):
        for k in range(piece.blocks):
            passed.append(pltpu.make_async_copy(source.at[k], piece.part(ref, k), sem_o.at[len(passed)]))
            passed[-1].start()
    weight = row_weights(jnp.where(place == 0, 1.0, 0.0))
    d_query = jnp.concatenate([dq0_ref[...], dq1_ref[...]], axis=1)
    d_query_w = wide(d_query) * weight
    gv_ref[2:3] = col_sum(d_query_w)
    g[:, :D] = dot_first(nl_ref[...], d_query_w.astype(BF16)).astype(BF16)

    half = D // 2
    for at, (dk_ref, dv_ref) in enumerate(((dk0_ref, dv0_ref), (dk1_ref, dv1_ref))):
        g[:, D + at * half : D + (at + 1) * half] = dot_first(na_ref[...], dk_ref[...]).astype(BF16)
        g[:, 2 * D + at * half : 2 * D + (at + 1) * half] = dot_first(na_ref[...], dv_ref[...]).astype(BF16)

    stores = copies_out(pos, q_qkv, targets, g, sem_g)
    for copy in stores:
        copy.start()
    for copy in loads:
        copy.wait()
    sums[...] = jnp.zeros((8, D), F32)

    @pl.loop(0, NK // 384)
    def _(at):
        rows = pl.ds(pl.multiple_of(at * 384, 128), 384)
        d_key = jnp.concatenate([dk0_ref[rows], dk1_ref[rows]], axis=1)
        d_value = jnp.concatenate([dv0_ref[rows], dv1_ref[rows]], axis=1)
        d_norm = dot_last(d_key, w[:, D : 2 * D]) + dot_last(d_value, w[:, 2 * D :])
        rows_all[rows] = d_norm
        unit = unit_of(wide(xa_ref[rows]))[0]
        sums[0:1] += col_sum(d_norm * unit)
        sums[1:2] += col_sum(d_norm)
        sums[2:3] += col_sum(wide(d_value))

    d_local = dot_last(d_query, w[:, :D])
    d_local_w = d_local * weight
    unit = unit_of(wide(xl_ref[...]))[0]
    gv_ref[0:1] = sums[0:1] + col_sum(d_local_w * unit)
    gv_ref[1:2] = sums[1:2] + col_sum(d_local_w)
    gv_ref[3:4] = sums[2:3]
    gv_ref[4:8] = jnp.zeros((4, D), F32)
    class_a = rows_all[PAT_A : PAT_A + 8][:1]
    class_b = [rows_all[KA + i * KB + BLK_B : KA + i * KB + BLK_B + 8][:1] for i in range(IMB)]
    row_b = lax.broadcasted_iota(jnp.int32, (QB, 1), 0)

    zh, zl = place // 2, place % 2

    def block_of(at):
        part_a = rows_all[pl.ds(pl.multiple_of(at * BLK_A, BLK_A), BLK_A)]
        parts = [part_a]
        for i in range(IMB):
            part = rows_all[pl.ds(pl.multiple_of(KA + i * KB + at * QB, QB), QB)]
            part = jnp.where(row_b == BLK_B, class_b[i], part)
            part = jnp.where(row_b == BLK_B + 1, class_a, part) if i == 0 else part
            parts.append(part)
        return parts

    for step in (0, 1):
        high = zh if step == 0 else 1 - zh
        send_ref[step] = jnp.concatenate(block_of(high * 2 + 1 - zl), axis=0).astype(BF16)
    keep_ref[...] = jnp.concatenate(block_of((1 - zh) * 2 + zl), axis=0)
    own = block_of(place)
    local_ref[:BLK_A] = own[0] + d_local[:BLK_A]
    local_ref[BLK_A : BLK_A + 16] = jnp.concatenate(
        [own[1][BLK_B + 1 : BLK_B + 2] + d_local[BLK_A : BLK_A + 1], jnp.zeros((15, D), F32)], axis=0
    )
    for i in range(IMB):
        at = QA + i * QB
        local_ref[at : at + QB] = own[1 + i] + d_local[at : at + QB]
    for copy in stores + passed:
        copy.wait()


def back(pos, first, second, normed_all, normed_loc, x_all, x_loc, arrays, pieces, g_out):
    q_qkv, q_out = grad_pieces(D, 3 * D, "split"), grad_pieces(D, D, "split")
    width = q_qkv[0].cols
    joint = [(1, D, 2 * D)] * 2
    if small_grid():
        joint = [(8, D // 8, 2 * D)] * 2
        for at in range(4):
            q_qkv[at].first = q_out[at].first = at // 2 * 4
    for piece in q_out:
        piece.src = width
    shapes = [((NQ, D), F32), ((BLOCK, D), F32), ((2, BLOCK, D), BF16), ((8, D), F32)]
    outs = pl.pallas_call(
        functools.partial(back_kernel, pieces, q_qkv, q_out),
        in_specs=[SSPEC] + [VSPEC] * 10 + [ANYSPEC] * len(arrays) + [VSPEC] * len(g_out),
        out_specs=[VSPEC] * 4 + [ANYSPEC] * 2,
        out_shape=[jax.ShapeDtypeStruct(*each) for each in shapes]
        + [jax.ShapeDtypeStruct(shape, BF16) for shape in joint],
        scratch_shapes=[
            pltpu.VMEM((D, 3 * D), BF16),
            pltpu.VMEM((D, 3 * D), BF16),
            pltpu.VMEM((NK, D), F32),
            pltpu.VMEM((8, D), F32),
            pltpu.SemaphoreType.DMA((piece_count(pieces),)),
            pltpu.SemaphoreType.DMA((piece_count(q_qkv),)),
            pltpu.SemaphoreType.DMA((piece_count(q_out),)),
        ],
        compiler_params=params(),
        cost_estimate=cost(4 * D * D * (NQ + 2 * NK), 20e6),
        name="back",
    )(pos, *first, *second, normed_all, normed_loc, x_all, x_loc, *arrays, *g_out)
    return outs[:4], list(outs[4:])


def finish_kernel(dres_ref, local_ref, r1_ref, r2_ref, x_ref, vec_ref, ga_ref, gca_ref, gb_ref, gcb_ref):
    gain = vec_ref[0:1]

    def rows_of(at, count, got_at):
        grad = local_ref[at : at + count]
        grad = grad + wide(r1_ref[0, got_at : got_at + count]) + wide(r2_ref[got_at : got_at + count])
        unit, inv_std = unit_of(wide(x_ref[at : at + count]))
        return dres_ref[at : at + count] + norm_back(grad, unit, inv_std, gain)

    ga_ref[0] = rows_of(0, BLK_A, 0)
    for i in range(IMB):
        at = QA + i * QB
        rows = rows_of(at, QB, BLK_A + i * QB)
        gb_ref[i] = rows[:BLK_B]
        gcb_ref[i : i + 1] = rows[BLK_B : BLK_B + 1]
    grad = local_ref[BLK_A : BLK_A + 16]
    spot = BLK_A + 48
    grad = grad + wide(r1_ref[0, spot : spot + 16])[9:10] + wide(r2_ref[spot : spot + 16])[9:10]
    unit, inv_std = unit_of(wide(x_ref[BLK_A : BLK_A + 16]))
    rows = dres_ref[BLK_A : BLK_A + 16] + norm_back(grad, unit, inv_std, gain)
    gca_ref[...] = rows[:1]


def finish(d_resid, local, got, x_loc, vec):
    return pl.pallas_call(
        finish_kernel,
        in_specs=[VSPEC] * 6,
        out_specs=[VSPEC] * 4,
        out_shape=[
            jax.ShapeDtypeStruct((IMA, BLK_A, D), F32),
            jax.ShapeDtypeStruct((IMA, D), F32),
            jax.ShapeDtypeStruct((IMB, BLK_B, D), F32),
            jax.ShapeDtypeStruct((IMB, D), F32),
        ],
        compiler_params=params(),
        cost_estimate=cost(1e6, 6e6),
        name="finish",
    )(d_resid, local, *got, x_loc, vec)


def add_kernel(counts, *refs):
    ins, outs = refs[: sum(counts)], refs[sum(counts) :]
    at = 0
    for count, out in zip(counts, outs):
        total = wide(ins[at][...])
        for ref in ins[at + 1 : at + count]:
            total = total + wide(ref[...])
        out[...] = total.astype(BF16)
        at += count


def add_blocks(*groups):
    steps = 3
    specs, arrays, outs, shapes = [], [], [], []
    for group in groups:
        for array, first, count in group:
            rows, cols = array.shape[1:]
            specs.append(
                pl.BlockSpec((count, rows, cols // steps), lambda i, at=first // count: (at, 0, i))
            )
            arrays.append(array)
        outs.append(pl.BlockSpec((count, rows, cols // steps), lambda i: (0, 0, i)))
        shapes.append(jax.ShapeDtypeStruct((count, rows, cols), BF16))
    return pl.pallas_call(
        functools.partial(add_kernel, [len(group) for group in groups]),
        grid=(steps,),
        in_specs=specs,
        out_specs=outs,
        out_shape=shapes,
        compiler_params=params(),
        cost_estimate=cost(1, 1),
        name="add_blocks",
    )(*arrays)


def split_kernel(counts, zl_ref, *refs):
    ins, (send, kept) = refs[: sum(counts)], refs[sum(counts) :]
    first = zl_ref[0] == 0
    sums, at = [], 0
    for count in counts:
        total = wide(ins[at][0])
        for ref in ins[at + 1 : at + count]:
            total = total + wide(ref[0])
        sums.append(total)
        at += count
    groups = []
    for z in range(4):
        parts = []
        for total in sums:
            rows = total.shape[0] // 4
            part = total[z * rows : (z + 1) * rows]
            if rows > 24:
                part = jnp.concatenate([part[at : at + 24] for at in range(0, rows, 24)], axis=1)
            parts.append(part)
        axis = 1 if sums[0].shape == sums[1].shape else 0
        groups.append(jnp.concatenate(parts, axis=axis))
    for zh in range(2):
        one, two = groups[2 * zh], groups[2 * zh + 1]
        send[zh] = jnp.where(first, two, one).astype(BF16)
        kept[zh] = jnp.where(first, one, two)


def split_blocks(zl, rows, *groups):
    specs, arrays = [], []
    for group in groups:
        for array, first in group:
            specs.append(pl.BlockSpec((1,) + array.shape[1:], lambda i, at=first: (at, 0, 0)))
            arrays.append(array)
    shape = (2, rows, FF)
    return pl.pallas_call(
        functools.partial(split_kernel, [len(group) for group in groups]),
        grid=(1,),
        in_specs=[SSPEC] + specs,
        out_specs=[pl.BlockSpec(shape, lambda i: (0, 0, 0))] * 2,
        out_shape=[jax.ShapeDtypeStruct(shape, BF16), jax.ShapeDtypeStruct(shape, F32)],
        compiler_params=params(),
        cost_estimate=cost(1, 1),
        name="split_blocks",
    )(zl[None], *arrays)


def half_kernel(zh_ref, kept_ref, got_ref, send, keep):
    zh = zh_ref[0]
    send[...] = (kept_ref[1 - zh] + wide(got_ref[1 - zh])).astype(BF16)
    keep[...] = kept_ref[zh] + wide(got_ref[zh])


def half_blocks(zh, kept, got):
    return pl.pallas_call(
        half_kernel,
        in_specs=[SSPEC, VSPEC, VSPEC],
        out_specs=[VSPEC] * 2,
        out_shape=[jax.ShapeDtypeStruct(kept.shape[1:], BF16), jax.ShapeDtypeStruct(kept.shape[1:], F32)],
        compiler_params=params(),
        cost_estimate=cost(1, 1),
        name="half_blocks",
    )(zh[None], kept, got)


def pad_to(values, width):
    return jnp.pad(values, ((0, width - values.shape[0]),))


def nesterov(master, moment, average, grad_w, step_rate):
    moment_new = 0.5 * moment + grad_w
    master_new = master - step_rate * (grad_w + 0.5 * moment_new)
    return (master_new, moment_new, 0.5 * average + 0.5 * master_new)


def pair_up(value, other, axis):
    first = lax.axis_index(axis) == 0
    return jnp.stack([jnp.where(first, value, other), jnp.where(first, other, value)])


def across(mine, other):
    first = lax.axis_index("zl") == 0
    return jnp.stack([jnp.where(first, mine, other), jnp.where(first, other, mine)], axis=1)


def zl_parts(block):
    cut = block.reshape(2, 2, block.shape[0] // 4, block.shape[1])
    zl = lax.axis_index("zl")
    send = lax.dynamic_index_in_dim(cut, 1 - zl, 1, keepdims=False).astype(BF16)
    return send, lax.dynamic_index_in_dim(cut, zl, 1, keepdims=False)


def zh_parts(kept, got):
    zh = lax.axis_index("zh")
    both = kept + wide(got)
    send = lax.dynamic_index_in_dim(both, 1 - zh, 0, keepdims=False).astype(BF16)
    return send, lax.dynamic_index_in_dim(both, zh, 0, keepdims=False)


def sum_z(block):
    send, kept = zl_parts(block)
    send, kept = zh_parts(kept, swap(send, "zl"))
    return kept + wide(swap(send, "zh"))


def tick(*values):
    return lax.optimization_barrier(values)


def pack_kernel(xa_ref, xca_ref, xb_ref, xcb_ref, ca_ref, cca_ref, cb_ref, ccb_ref, x_ref, cot_ref, send_ref):
    def lay(rows_a, class_a, rows_b, class_b):
        zero = jnp.zeros((16, D), F32)
        parts = [wide(rows_a[0]), wide(class_a[...]), zero[: QA - BLK_A - 1]]
        for i in range(IMB):
            parts += [wide(rows_b[i]), wide(class_b[i : i + 1]), zero[: QB - BLK_B - 1]]
        return jnp.concatenate(parts, axis=0).astype(BF16)

    rows = lay(xa_ref, xca_ref, xb_ref, xcb_ref)
    x_ref[...] = rows
    send_ref[:BLK_A] = rows[:BLK_A]
    send_ref[BLK_A:] = rows[QA:]
    cot_ref[...] = lay(ca_ref, cca_ref, cb_ref, ccb_ref)


def pack(*rows):
    return pl.pallas_call(
        pack_kernel,
        in_specs=[VSPEC] * 8,
        out_specs=[VSPEC] * 3,
        out_shape=[jax.ShapeDtypeStruct((count, D), BF16) for count in (NQ, NQ, BLOCK)],
        compiler_params=params(),
        cost_estimate=cost(1e6, 2e6),
        name="pack",
    )(*rows)


LEFT = 3 * D // 2 + D // 2


def body(
    patches_a, class_a, patches_b, class_b, count_a, count_b, index_a, index_b,
    cot_a, cot_class_a, cot_b, cot_class_b,
    qkv_weight, qkv_momentum, qkv_average, out_weight, out_momentum, out_average,
    up_weight, up_momentum, up_average, down_weight, down_momentum, down_average,
    table_weight, table_momentum, table_average, vector_weight, vector_momentum, vector_average,
):
    zh, zl = lax.axis_index("zh"), lax.axis_index("zl")
    place = zh * 2 + zl
    devices = lax.axis_size(AXES)
    n0, n1, nc = [lax.axis_size(axis) for axis in AXES[:3]]
    pos = jnp.stack([lax.axis_index("d0"), lax.axis_index("d1"), lax.axis_index("c"), place]).astype(jnp.int32)
    counts = jnp.concatenate([count_a, count_b, jnp.zeros((1,), jnp.int32)])

    grid = small_grid()
    t_rows, v_len = table_weight.shape[0], vector_weight.shape[0]
    small = jnp.concatenate([table_weight.reshape(-1), vector_weight])
    small = pad_to(small, qkv_weight.shape[0] * 128).reshape(-1, 128)
    half, part = 3 * D // 2, D // 2
    qkv = jnp.concatenate(
        [qkv_weight[:, :half], out_weight[:, :part], qkv_weight[:, half:], out_weight[:, part:], small], axis=1
    ).astype(BF16)

    q_one = swap(qkv, "zh")
    up, down = up_weight.astype(BF16), down_weight.astype(BF16)
    x_loc, cot, message = pack(patches_a, class_a, patches_b, class_b, cot_a, cot_class_a, cot_b, cot_class_b)
    q_one, up, down, x_loc, cot, message = tick(q_one, up, down, x_loc, cot, message)

    q_pair, up = tick(pair_up(qkv, q_one, "zh"), up)
    q_two, u_one = swap(q_pair, "zl"), swap(up, "zh")
    q_two, u_one = tick(q_two, u_one)

    q_block = across(q_pair, q_two).reshape(-1, qkv.shape[1])
    left, right = q_block[:, :LEFT], q_block[:, LEFT:]
    u_pair = pair_up(up, u_one, "zh")
    left, right, u_pair, down, index_a, index_b = tick(left, right, u_pair, down, index_a, index_b)
    if grid:
        l_one, r_one = swap(left, "d0"), swap(right, "d1")
    u_two, d_one = swap(u_pair, "zl"), swap(down, "zh")
    ids = all_ids(pos, index_a, index_b)
    if grid:
        l_one, r_one, u_two, d_one, ids = tick(l_one, r_one, u_two, d_one, ids)
        l_two, r_two = jnp.stack([left, l_one]), jnp.stack([right, r_one])
    else:
        u_two, d_one, ids = tick(u_two, d_one, ids)
        l_two, r_two = left, right
    d_pair = pair_up(down, d_one, "zh")
    l_two, r_two, d_pair, message = tick(l_two, r_two, d_pair, message)
    if grid:
        l_far, r_far = swap(l_two, "d1"), swap(r_two, "d0")
    d_two, x_one = swap(d_pair, "zl"), swap(message, "zh")
    u_block = across(u_pair, u_two).reshape(-1, FF)
    if grid:
        l_far, r_far, d_two, x_one, u_block = tick(l_far, r_far, d_two, x_one, u_block)
        l_four, r_four = jnp.concatenate([l_two, l_far]), jnp.concatenate([r_two, r_far])
    else:
        d_two, x_one, u_block = tick(d_two, x_one, u_block)
        l_four, r_four = left, right
    d_block = across(d_pair, d_two).reshape(-1, D)
    x_pair = pair_up(message, x_one, "zh")
    l_four, r_four, u_block, d_block, x_pair = tick(l_four, r_four, u_block, d_block, x_pair)
    if grid:
        rights = [r_four, swap(r_four, "c")]
        lefts = [l_four, swap(l_four, "c")]
        u_near, d_near = swap(u_block, "d0"), swap(d_block, "d1")
    else:
        lefts, rights = [gather_whole(left)], [gather_whole(right)]
    x_two = swap(x_pair, "zl")
    rows = q_block.shape[0]
    qkv_w = (
        lefts + rights,
        weight_pieces("x", rows, half) + weight_pieces("y", rows, half, half),
    )
    out_w = (
        lefts + rights,
        weight_pieces("x", rows, part, 0, half) + weight_pieces("y", rows, part, part, half),
    )

    small = wide(small_part(rights, LEFT))
    table_t = jnp.transpose(small[:, : t_rows * HEADS].reshape(TABLE, HEADS))
    vector = small[:, t_rows * HEADS : t_rows * HEADS + v_len].reshape(-1)
    vec = jnp.pad(vector[: 10 * D].reshape(10, D), ((0, 6), (0, 0)))
    b1 = vector[10 * D :].reshape(FF // STEP, STEP)
    ids_a, ids_b, ids_fold = ids
    strip = lookup(table_t, ids_a)
    cols = jnp.transpose(strip[:, SIDE_A + 1, :QA].reshape(HEADS // 2, 2, QA), (0, 2, 1))
    cols = jnp.pad(cols, ((0, 0), (0, 0), (0, 126)))

    if grid:
        u_near, d_near, strip, cols = tick(u_near, d_near, strip, cols)
        u_pair, d_pair, table_t = tick(jnp.stack([u_block, u_near]), jnp.stack([d_block, d_near]), table_t)
        u_far, d_far = swap(u_pair, "d1"), swap(d_pair, "d0")
        ups, downs = [u_pair, None, swap(u_pair, "c"), None], [d_pair, None, swap(d_pair, "c"), None]
    bias_b = lookup(table_t, ids_b)
    if grid:
        x_two, bias_b = tick(x_two, bias_b)
    queries, keys, values, normed_all, normed_loc, x_all = project(pos, x_pair, x_two, x_loc, vec, *qkv_w)
    mixed, probs_a, probs_b = attend(counts, queries, keys, values, cols, strip, bias_b)
    if grid:
        ups[2], downs[2], u_far, d_far, mixed = tick(ups[2], downs[2], u_far, d_far, mixed)
        ups[1], downs[1] = u_far, d_far
        ups[3], downs[3] = swap(u_far, "c"), swap(d_far, "c")
    else:
        ups, downs = [gather_whole(u_block)], [gather_whole(d_block)]
    up_w = (ups, weight_pieces("x", rows, FF, pairs=True))
    down_w = (downs, weight_pieces("y", d_block.shape[0], D, pairs=True))
    plain, g_out, g_up, g_down = feed(
        pos, counts, mixed, x_loc, cot, vec, b1, (out_w, up_w, down_w), ("split", "x", "y"),
    )
    finals, (d_resid, d_mixed, gv_feed, gb_feed) = plain[:4], plain[4:]
    att = (queries, keys, values, probs_a, probs_b)
    grads = {}
    if grid:
        d_mixed, g_up, g_down, g_out = tick(d_mixed, g_up, g_down, g_out)
        u_core, d_core = swap(g_up[1], "c"), swap(g_down[1], "c")
        first = attend_back(pos[3:], 0, d_mixed, *att)
        u_core, d_core, first = tick(u_core, d_core, first)
        u_send, d_send, d_mixed, first = tick(
            far_part(g_up[0], u_core), far_part(g_down[0], d_core), d_mixed, first
        )
        u_far, d_far = swap(u_send, "d1"), swap(d_send, "d0")
    else:
        first = attend_back(pos[3:], 0, d_mixed, *att)
    second = attend_back(pos[3:], 1, d_mixed, *att)
    (local, keep, send, gv_back), g_qkv = back(
        pos, first[:3], second[:3], normed_all, normed_loc, x_all, x_loc, *qkv_w, g_out
    )
    folded = (first[3], second[3])
    if grid:
        u_far, d_far, send, g_qkv, gv_back, folded, keep = tick(u_far, d_far, send, g_qkv, gv_back, folded, keep)
        came = swap(send, "zl")
        q_core = swap(g_qkv[1], "c")
        u_send, d_send = near_part(g_up[0], u_core, u_far), near_part(g_down[0], d_core, d_far)
        u_near, d_near = swap(u_send, "d0"), swap(d_send, "d1")
        q_core, u_send, d_send = tick(q_core, u_send, d_send)
        l_own, r_own, l_core, r_core = g_qkv[0][:4], g_qkv[0][4:], q_core[:4], q_core[4:]
        l_send, r_send, folded, gv_back = tick(far_part(l_own, l_core), far_part(r_own, r_core), folded, gv_back)
        l_far, r_far = swap(l_send, "d1"), swap(r_send, "d0")
    else:
        came = swap(send, "zl")

    gt = gt_first = table_grad(*folded, ids_fold)
    gv = jnp.concatenate([gv_back[:4].reshape(-1), gv_feed[:6].reshape(-1), gb_feed.reshape(-1)])
    gt = jnp.transpose(gt[:HEADS]).reshape(devices, t_rows * HEADS)
    small_grad = jnp.concatenate([gt, gv.reshape(devices, v_len)], axis=1)
    small_len = (small_grad.shape[1] + 2047) // 2048 * 2048
    small_grad = jnp.pad(small_grad, ((0, 0), (0, small_len - small_grad.shape[1])))
    small_grad = small_grad.astype(BF16).reshape(n0, n1, nc, 2, 2, -1, 128)

    if grid:
        came, gt_first = tick(came, gt_first)
        came_send = (keep + wide(came[1])).astype(BF16)
        came_far = swap(came_send, "zh")
        u_near, d_near, came_send, small_grad = tick(u_near, d_near, came_send, small_grad)
        send, kept = split_blocks(
            zl, 48,
            [(g_up[0], 0), (u_core, 0), (u_far, 0), (u_near[None], 0)],
            [(g_down[0], 0), (d_core, 0), (d_far, 0), (d_near[None], 0)],
        )
        z_got = swap(send, "zl")
        small_grad = scatter_axis(small_grad, "d0").astype(BF16)
        l_far, r_far, send, small_grad = tick(l_far, r_far, send, small_grad)
        l_send, r_send = near_part(l_own, l_core, l_far), near_part(r_own, r_core, r_far)
        l_near, r_near = swap(l_send, "d0"), swap(r_send, "d1")
        small_grad = scatter_axis(small_grad, "d1").astype(BF16)
        l_near, r_near, z_got, small_grad = tick(l_near, r_near, z_got, small_grad)
        send, kept = half_blocks(zh, kept, z_got)
        z_far = swap(send, "zh")
        q_send, q_kept = split_blocks(
            zl, 24,
            [(g_qkv[0], 0), (q_core, 0), (l_far, 0), (l_near[None], 0)],
            [(g_qkv[0], 4), (q_core, 4), (r_far, 0), (r_near[None], 0)],
        )
        q_got = swap(q_send, "zl")
        small_grad = scatter_axis(small_grad, "c").astype(BF16).reshape(4, -1)
        d_rows = finish(d_resid, local, (came, came_far), x_loc, vec)
        q_got, z_far, small_grad, d_rows = tick(q_got, z_far, small_grad, d_rows)
        q_send, q_kept = half_blocks(zh, q_kept, q_got)
        grads["q"] = q_kept + wide(swap(q_send, "zh"))
        small_total = wide(lax.dynamic_index_in_dim(small_grad, place, 0, keepdims=False))
        for at in range(1, 4):
            outgoing = lax.dynamic_index_in_dim(small_grad, (place + at) % 4, 0, keepdims=False)
            small_total = small_total + wide(lax.ppermute(outgoing, ("zh", "zl"), shift_perm(4, at)))
        small_grad = small_total
        both = kept + wide(z_far)
        grads["up"] = both[: both.shape[0] // 2]
        grads["down"] = unside(both[both.shape[0] // 2 :])
    else:
        came_far = swap((keep + wide(came[1])).astype(BF16), "zh")
        for name, arrays in (("up", g_up), ("down", g_down)):
            grads[name] = sum_z(whole_grid_sum(arrays[0]))
        grads["q"] = sum_z(whole_grid_sum(jnp.concatenate(g_qkv, axis=2)))
        for axis in AXES:
            small_grad = scatter_axis(small_grad, axis)
            small_grad = small_grad if axis == "zl" else small_grad.astype(BF16)
        d_rows = finish(d_resid, local, (came, came_far), x_loc, vec)
    joint = grads["q"]
    grads["qkv"] = jnp.concatenate([joint[:, :half], joint[:, LEFT : LEFT + half]], axis=1)
    grads["out"] = jnp.concatenate([joint[:, half:LEFT], joint[:, LEFT + half :]], axis=1)
    small_grad = small_grad.reshape(-1)
    grads["table"] = small_grad[: t_rows * HEADS].reshape(t_rows, HEADS)
    grads["vector"] = small_grad[t_rows * HEADS : t_rows * HEADS + v_len]
    rows_all = (IMA * (PAT_A + 1) + IMB * (PAT_B + 1)) * (devices // 4)
    states = (
        ("qkv", qkv_weight, qkv_momentum, qkv_average),
        ("out", out_weight, out_momentum, out_average),
        ("up", up_weight, up_momentum, up_average),
        ("down", down_weight, down_momentum, down_average),
        ("table", table_weight, table_momentum, table_average),
        ("vector", vector_weight, vector_momentum, vector_average),
    )
    updated = []
    for (name, *state), rate in zip(states, STEP_RATES):
        updated += nesterov(*state, grads[name], rate / math.sqrt(rows_all))
    return (*finals, *d_rows, *updated)


def solution(mesh):
    dp, seq = mesh.devices.shape
    split = Mesh(mesh.devices.reshape(dp // 4, 2, 2, seq // 2, 2), AXES)
    dp_axes = ("d0", "d1", "c")
    rows = P(dp_axes, ("zh", "zl"), None)
    classes = P(dp_axes, None)
    shard = P(AXES, None)
    vec = P(AXES)
    return jax.shard_map(
        body,
        mesh=split,
        in_specs=(
            rows, classes, rows, classes, P(dp_axes), P(dp_axes), P(), P(), rows, classes, rows, classes,
            *([shard] * 15), *([vec] * 3),
        ),
        out_specs=(rows, classes, rows, classes, rows, classes, rows, classes, *([shard] * 15), *([vec] * 3)),
        check_vma=False,
    )
```

```python
import functools
import math

import jax
import jax.numpy as jnp
from jax import lax
from jax.experimental import pallas as pl
from jax.experimental.pallas import tpu as pltpu
from jax.sharding import Mesh
from jax.sharding import PartitionSpec as P

F32 = jnp.float32
BF16 = jnp.bfloat16
D = 768
HEADS = 12
HEAD_DIM = 64
FF = 3072
IMA = 1
IMB = 2
SIDE_A = 24
SIDE_B = 14
PAT_A = 576
PAT_B = 196
SLOT_B = 224
BLK_A = 144
BLK_B = 56
REAL_B = 49
TABLE = 2304
EPS = 1e-06
NEG = -1e30
ROOT_HALF = 0.7071067811865476
ROOT_TAU = 0.3989422804014327
STEP_RATES = (0.04, 1.6, 0.08, 0.02, 3.0, 0.6)

QA = 160
QB = 64
NQ = QA + IMB * QB
KA = 640
KB = 256
NK = KA + IMB * KB
BLOCK = BLK_A + IMB * QB
GROUPS = BLK_A // SIDE_A
CHUNK = 256
STEP = 1024
ROWS = 48
LEFT = 3 * D // 2 + D // 2
REACH = 29
SPAN = 2 * SIDE_A - 1
STRIP = 768
VMEM = 56 << 20
AXES = ("d0", "d1", "c", "zh", "zl")


def lookup_kernel(table_ref, index_ref, out_ref):
    rows, lanes = index_ref.shape
    heads, entries = table_ref.shape

    def eight_rows(at, carry):
        start = pl.multiple_of(at * 8, 8)
        for col in range(lanes // 128):
            ids = index_ref[pl.ds(start, 8), col * 128 : (col + 1) * 128]
            low = ids & 127
            high = ids >> 7
            found = [jnp.zeros((8, 128), F32) for _ in range(heads)]
            for chunk in range(entries // 128):
                here = high == chunk
                for head in range(heads):
                    row = jnp.broadcast_to(
                        table_ref[head : head + 1, chunk * 128 : (chunk + 1) * 128], (8, 128)
                    )
                    got = jnp.take_along_axis(row, low, axis=1)
                    found[head] = jnp.where(here, got, found[head])
            for head in range(heads):
                out_ref[head, pl.ds(start, 8), col * 128 : (col + 1) * 128] = found[head]
        return carry

    lax.fori_loop(0, rows // 8, eight_rows, 0)


def lookup(table_t, ids):
    return pl.pallas_call(
        lookup_kernel,
        out_shape=jax.ShapeDtypeStruct((table_t.shape[0],) + ids.shape, F32),
        compiler_params=params(),
        cost_estimate=pl.CostEstimate(flops=20, bytes_accessed=2, transcendentals=0),
    )(table_t, ids)


def dot_last(left, right):
    return lax.dot_general(left, right, (((1,), (1,)), ((), ())), preferred_element_type=F32)


def dot_first(left, right):
    return lax.dot_general(left, right, (((0,), (0,)), ((), ())), preferred_element_type=F32)


def dot_plain(left, right):
    return jnp.dot(left, right, preferred_element_type=F32)


def unit_of(values):
    center = values - jnp.mean(values, axis=-1, keepdims=True)
    inv_std = lax.rsqrt(jnp.mean(center * center, axis=-1, keepdims=True) + EPS)
    return center * inv_std, inv_std


def norm_back(grad_in, unit_rows, inv_std, gain):
    d_unit = grad_in * gain
    return inv_std * (
        d_unit
        - jnp.mean(d_unit, axis=-1, keepdims=True)
        - unit_rows * jnp.mean(d_unit * unit_rows, axis=-1, keepdims=True)
    )


def col_sum(values):
    return jnp.sum(values, axis=0, keepdims=True)


class Piece:
    def __init__(self, blocks, rows, cols, order, other, col0, src=0, first=0, base=0):
        self.blocks, self.rows, self.cols = blocks, rows, cols
        self.order, self.other, self.col0 = order, other, col0
        self.src, self.first, self.base = src, first, base

    def part(self, ref, k):
        return ref.at[self.first + k, :, self.src : self.src + self.cols]

    def row(self, pos, k):
        if self.order is None:
            return 0
        near, far = k % 2, (k + self.base) // 2
        dy, dx = (near, far) if self.order == "x" else (far, near)
        y = 1 - pos[0] if dy else pos[0]
        x = 1 - pos[1] if dx else pos[1]
        c = 1 - pos[2] if self.other else pos[2]
        return pl.multiple_of(((y * 2 + x) * 2 + c) * self.rows, self.rows)


def copies_in(pos, pieces, refs, dest, sems):
    made = []
    for piece, ref in zip(pieces, refs):
        for k in range(piece.blocks):
            spot = dest.at[pl.ds(piece.row(pos, k), piece.rows), piece.col0 : piece.col0 + piece.cols]
            made.append(pltpu.make_async_copy(piece.part(ref, k), spot, sems.at[len(made)]))
    return made


def copies_out(pos, pieces, refs, source, sems):
    made = []
    for piece, ref in zip(pieces, refs):
        for k in range(piece.blocks):
            spot = source.at[pl.ds(piece.row(pos, k), piece.rows), piece.col0 : piece.col0 + piece.cols]
            made.append(pltpu.make_async_copy(spot, piece.part(ref, k), sems.at[len(made)]))
    return made


def piece_count(pieces):
    return sum(piece.blocks for piece in pieces)


def shift_perm(size, shift):
    return [(at, (at + shift) % size) for at in range(size)]


def swap(value, axis):
    return lax.ppermute(value, axis, [(0, 1), (1, 0)])


def hold(value, *after):
    return lax.optimization_barrier((value, *after))[0]


def small_grid():
    return lax.axis_size("d0") == 2 and lax.axis_size("d1") == 2 and lax.axis_size("c") == 2


def gather_axis(value, axis):
    size = lax.axis_size(axis)
    if size == 1:
        return value[None]
    if size > 4:
        return lax.all_gather(value, axis, axis=0)
    me = lax.axis_index(axis)
    pieces = [value] + [lax.ppermute(value, axis, shift_perm(size, s)) for s in range(1, size)]
    ordered = []
    for at in range(size):
        chosen = pieces[0]
        for s in range(1, size):
            chosen = jnp.where((me - at) % size == s, pieces[s], chosen)
        ordered.append(chosen)
    return jnp.stack(ordered)


def scatter_axis(value, axis):
    size = lax.axis_size(axis)
    if size == 1:
        return value[0].astype(F32)
    if size > 4:
        return lax.psum_scatter(value, axis, scatter_dimension=0).astype(F32)
    me = lax.axis_index(axis)
    total = lax.dynamic_index_in_dim(value, me, 0, keepdims=False).astype(F32)
    for s in range(1, size):
        outgoing = lax.dynamic_index_in_dim(value, (me + s) % size, 0, keepdims=False)
        total = total + lax.ppermute(outgoing.astype(BF16), axis, shift_perm(size, s)).astype(F32)
    return total


def halves_of(cols, order):
    if order == "split":
        return [("x", 0, cols // 2), ("y", cols // 2, cols)]
    return [(order, 0, cols)]


def gather_whole(block):
    rows, cols = block.shape
    for axis in ("c", "d1", "d0"):
        block = gather_axis(block, axis)
    return block.reshape(1, -1, cols)


def weight_pieces(turn, rows, cols, col0=0, src=0, pairs=False):
    if not small_grid():
        return [Piece(1, rows * lax.axis_size(AXES[:3]), cols, None, 0, col0, src)]
    if pairs:
        return [Piece(2, rows, cols, turn, other, col0, src, 0, far) for other in (0, 1) for far in (0, 2)]
    return [Piece(4, rows, cols, turn, other, col0, src) for other in (0, 1)]


def small_part(arrays, start):
    if not small_grid():
        tail = arrays[0][0, :, start:]
    else:
        tail = jnp.stack([each[..., start:] for each in arrays])
        tail = tail.reshape(2, 2, 2, *tail.shape[2:])
        for at, axis in enumerate(("c", "d0", "d1")):
            tail = jnp.where(lax.axis_index(axis) == 0, tail, jnp.flip(tail, at))
        tail = jnp.moveaxis(tail, 0, 2)
    return tail.reshape(lax.axis_size(AXES), -1)


def grad_pieces(rows, cols, order):
    if not small_grid():
        return [Piece(1, rows, stop - start, None, 0, start) for _, start, stop in halves_of(cols, order)]
    return [
        Piece(4, rows // 8, stop - start, turn, other, start)
        for turn, start, stop in halves_of(cols, order)
        for other in (0, 1)
    ]


def wide(value):
    return value.astype(F32)


def far_part(own, core):
    return (wide(own[2:]) + wide(core[2:])).astype(BF16)


def near_part(own, core, far):
    return (wide(own[1]) + wide(core[1]) + wide(far[1])).astype(BF16)


def side(rows):
    count = rows.shape[0] // 4
    return jnp.concatenate([rows[at * count : (at + 1) * count] for at in range(4)], axis=1)


def unside(wide_rows):
    width = wide_rows.shape[1] // 4
    return jnp.concatenate([wide_rows[:, at * width : (at + 1) * width] for at in range(4)], axis=0)


def beside(up, down):
    count = down.shape[1] // 4
    laid = jnp.concatenate([down[:, at * count : (at + 1) * count] for at in range(4)], axis=2)
    return jnp.concatenate([up, laid], axis=1)


def block_sum(own, core, far, near):
    return wide(own[0]) + wide(core[0]) + wide(far[0]) + wide(near)


def whole_grid_sum(whole):
    value = whole[0]
    sizes = [lax.axis_size(axis) for axis in AXES]
    value = value.reshape(*sizes[:3], -1, value.shape[-1])
    for axis in AXES[:3]:
        value = scatter_axis(value, axis)
        if axis != "c":
            value = value.astype(BF16)
    return value


def project_kernel(pieces, pos_ref, pair_ref, two_ref, xl_ref, vec_ref, *refs):
    w_refs = refs[: len(pieces)]
    q_ref, k_ref, v_ref, na_ref, nl_ref, xa_ref, w, sems = refs[len(pieces) :]
    copies = copies_in([pos_ref[at] for at in range(3)], pieces, w_refs, w, sems)
    for copy in copies:
        copy.start()
    for at in range(4):
        mine = pos_ref[3] % 2 == at % 2
        rows = jnp.where(mine, pair_ref[at // 2], two_ref[at // 2])
        xa_ref[at * BLK_A : (at + 1) * BLK_A] = rows[:BLK_A]
        for i in range(IMB):
            start = KA + i * KB + at * QB
            xa_ref[start : start + QB] = rows[BLK_A + i * QB : BLK_A + (i + 1) * QB]
    xa_ref[PAT_A : PAT_A + 16] = xl_ref[BLK_A:QA]
    xa_ref[PAT_A + 16 : KA] = jnp.zeros((KA - PAT_A - 16, D), BF16)
    gain, shift = vec_ref[0:1], vec_ref[1:2]
    nl_ref[...] = (unit_of(wide(xl_ref[...]))[0] * gain + shift).astype(BF16)

    @pl.loop(0, NK // 128)
    def _(at):
        rows = pl.ds(pl.multiple_of(at * 128, 128), 128)
        na_ref[rows] = (unit_of(wide(xa_ref[rows]))[0] * gain + shift).astype(BF16)

    for copy in copies:
        copy.wait()
    queries = dot_plain(nl_ref[...], w[:, :D]) + vec_ref[2:3]
    q_ref[...] = (queries * (1.0 / math.sqrt(HEAD_DIM))).astype(BF16)

    @pl.loop(0, NK // 384)
    def _(at):
        rows = pl.ds(pl.multiple_of(at * 384, 128), 384)
        k_ref[rows] = dot_plain(na_ref[rows], w[:, D : 2 * D]).astype(BF16)
        v_ref[rows] = (dot_plain(na_ref[rows], w[:, 2 * D :]) + vec_ref[3:4]).astype(BF16)


VSPEC = pl.BlockSpec(memory_space=pltpu.VMEM)
SSPEC = pl.BlockSpec(memory_space=pltpu.SMEM)
ANYSPEC = pl.BlockSpec(memory_space=pl.ANY)


def params(size=56):
    return pltpu.CompilerParams(vmem_limit_bytes=size << 20)


def cost(flops, moved):
    return pl.CostEstimate(flops=int(flops), bytes_accessed=int(moved), transcendentals=0)


def project(pos, x_pair, x_two, x_loc, vec, arrays, pieces):
    return pl.pallas_call(
        functools.partial(project_kernel, pieces),
        in_specs=[SSPEC] + [VSPEC] * 4 + [ANYSPEC] * len(arrays),
        out_specs=[VSPEC] * 6,
        out_shape=[
            jax.ShapeDtypeStruct((NQ, D), BF16),
            jax.ShapeDtypeStruct((NK, D), BF16),
            jax.ShapeDtypeStruct((NK, D), BF16),
            jax.ShapeDtypeStruct((NK, D), BF16),
            jax.ShapeDtypeStruct((NQ, D), BF16),
            jax.ShapeDtypeStruct((NK, D), BF16),
        ],
        scratch_shapes=[pltpu.VMEM((D, 3 * D), BF16), pltpu.SemaphoreType.DMA((piece_count(pieces),))],
        compiler_params=params(),
        cost_estimate=cost(2 * D * D * (NQ + 2 * NK), 12e6),
        name="project",
    )(pos, x_pair, x_two, x_loc, vec, *arrays)


def softmax_rows(scores):
    top = jnp.max(scores, axis=-1, keepdims=True)
    grown = jnp.exp(scores - top)
    return grown * (1.0 / jnp.sum(grown, axis=-1, keepdims=True))


def attend_kernel(cnt_ref, q_ref, k_ref, v_ref, col_ref, strip_ref, bias_ref, o_ref, pa_ref, pb_ref, sa, sb):
    lane = lax.broadcasted_iota(jnp.int32, (1, 128), 1)
    lane_a = lax.broadcasted_iota(jnp.int32, (1, KA), 1)
    lane_b = lax.broadcasted_iota(jnp.int32, (1, KB), 1)
    live_a = ((lane_a < PAT_A) & (lane_a < cnt_ref[0])) | (lane_a == PAT_A)
    spot = lane_b % QB
    live_b = [
        ((spot < REAL_B) & (lane_b // QB * REAL_B + spot < cnt_ref[1 + i])) | (lane_b == BLK_B)
        for i in range(IMB)
    ]
    for t in range(2):
        mine = (lane < HEAD_DIM) if t == 0 else (lane >= HEAD_DIM)
        queries = jnp.where(mine, q_ref[...], jnp.zeros((), BF16))
        sa[t] = dot_last(queries[:QA], k_ref[:KA])
        for i in range(IMB):
            q_at, k_at = QA + i * QB, KA + i * KB
            sb[t, i] = dot_last(queries[q_at : q_at + QB], k_ref[k_at : k_at + KB])
    for t in range(2):
        strip = strip_ref[t]
        for r in range(GROUPS + 1):
            start, count = r * SIDE_A, SIDE_A
            if r < GROUPS:
                off = (GROUPS - 1 - r) * SIDE_A
                bias = strip[:SIDE_A] if off == 0 else pltpu.roll(strip[:SIDE_A], STRIP - off, 1)
                bias = bias[:, :KA]
                bias = jnp.where(lane_a == PAT_A, col_ref[0, start : start + count, t : t + 1], bias)
            else:
                count = QA - start
                bias = jnp.concatenate([strip[SIDE_A:, :KA]] * 2, axis=0)
            probs = softmax_rows(jnp.where(live_a, sa[t, start : start + count] + bias, NEG))
            pa_ref[t, start : start + count] = probs
        for i in range(IMB):
            for r in range(2):
                rows = slice(r * 32, (r + 1) * 32)
                probs = softmax_rows(jnp.where(live_b[i], sb[t, i, rows] + bias_ref[t, rows], NEG))
                pb_ref[t, i, rows] = probs
    mixed = []
    for t in range(2):
        outs = [dot_plain(pa_ref[t].astype(BF16), v_ref[:KA])]
        for i in range(IMB):
            k_at = KA + i * KB
            outs.append(dot_plain(pb_ref[t, i].astype(BF16), v_ref[k_at : k_at + KB]))
        mixed.append(jnp.concatenate(outs, axis=0))
    o_ref[...] = jnp.where(lane < HEAD_DIM, mixed[0], mixed[1]).astype(BF16)


def attend(counts, queries, keys, values, cols, strip, bias_b):
    pairs = HEADS // 2
    return pl.pallas_call(
        attend_kernel,
        grid=(pairs,),
        in_specs=[
            SSPEC,
            pl.BlockSpec((NQ, 128), lambda p: (0, p)),
            pl.BlockSpec((NK, 128), lambda p: (0, p)),
            pl.BlockSpec((NK, 128), lambda p: (0, p)),
            pl.BlockSpec((1, QA, 128), lambda p: (p, 0, 0)),
        ]
        + [pl.BlockSpec((2, 32, STRIP), lambda p: (p, 0, 0)), pl.BlockSpec((2, QB, KB), lambda p: (p, 0, 0))],
        out_specs=[
            pl.BlockSpec((NQ, 128), lambda p: (0, p)),
            pl.BlockSpec((2, QA, KA), lambda p: (p, 0, 0)),
            pl.BlockSpec((2, IMB, QB, KB), lambda p: (p, 0, 0, 0)),
        ],
        out_shape=[
            jax.ShapeDtypeStruct((NQ, D), BF16),
            jax.ShapeDtypeStruct((HEADS, QA, KA), F32),
            jax.ShapeDtypeStruct((HEADS, IMB, QB, KB), F32),
        ],
        scratch_shapes=[pltpu.VMEM((2, QA, KA), F32), pltpu.VMEM((2, IMB, QB, KB), F32)],
        compiler_params=params(),
        cost_estimate=cost(4 * HEADS * 128 * (QA * KA + IMB * QB * KB), 30e6),
        name="attend",
    )(counts, queries, keys, values, cols, strip, bias_b)


def orders_b(odd):
    new_row = lax.broadcasted_iota(jnp.int32, (QB, QB), 0)
    old_row = lax.broadcasted_iota(jnp.int32, (QB, QB), 1)
    inside = new_row % 8
    slot = (new_row // 8 - odd) * 7 + 6 - inside
    order = (inside < 7) & (slot >= 0) & (slot < REAL_B) & (slot == old_row) & (new_row // 8 - odd >= 0)
    old_col = lax.broadcasted_iota(jnp.int32, (KB, KB), 0)
    new_col = lax.broadcasted_iota(jnp.int32, (KB, KB), 1)
    spread = (new_col < PAT_B) & (old_col == new_col // REAL_B * QB + new_col % REAL_B)
    return jnp.where(order, 1.0, 0.0).astype(BF16), jnp.where(spread, 1.0, 0.0).astype(BF16)


def strips_b(laid):
    pieces = []
    for r in range(4):
        off = (3 - r) * SIDE_B
        piece = laid[r * 16 : (r + 1) * 16]
        pieces.append(piece if off == 0 else pltpu.roll(piece, off, 1))
    return pieces


def fold_strip(strip, side):
    even = lax.broadcasted_iota(jnp.int32, (1, strip.shape[1]), 1) // side % 2 == 0
    return [
        pltpu.roll(part, 0, 1, stride=1, stride_axis=0)
        for part in (jnp.where(even, strip, 0.0), jnp.where(even, 0.0, strip))
    ]


def fold_strip_b(strip):
    even = lax.broadcasted_iota(jnp.int32, (1, KB), 1) // SIDE_B % 2 == 0
    return [
        (
            pltpu.roll(part[:8], 7, 1, stride=1, stride_axis=0),
            pltpu.roll(part[8:], 0, 1, stride=1, stride_axis=0),
        )
        for part in (jnp.where(even, strip, 0.0), jnp.where(even, 0.0, strip))
    ]


def row_weights(first):
    row = lax.broadcasted_iota(jnp.int32, (NQ, 1), 0)
    is_class = (row == BLK_A) | ((row >= QA) & ((row - QA) % QB == BLK_B))
    return jnp.where(is_class, first, 1.0)


def attend_back_kernel(place_ref, do_ref, q_ref, k_ref, v_ref, pa_ref, pb_ref, dq_ref, dk_ref, dv_ref, g_ref):
    lane = lax.broadcasted_iota(jnp.int32, (1, 128), 1)
    lane_a = lax.broadcasted_iota(jnp.int32, (1, KA), 1)
    low = lane < HEAD_DIM
    place = place_ref[0]
    odd = place % 2
    weight = row_weights(jnp.where(place == 0, 1.0, 0.0))
    new_row = lax.broadcasted_iota(jnp.int32, (BLK_A, QA), 0)
    old_row = lax.broadcasted_iota(jnp.int32, (BLK_A, QA), 1)
    turned = old_row == new_row // SIDE_A * SIDE_A + (SIDE_A - 1 - new_row % SIDE_A)
    turned = jnp.where(turned, 1.0, 0.0).astype(BF16)
    order, spread = orders_b(odd)
    pick_a = lax.broadcasted_iota(jnp.int32, (8, KA), 1) == PAT_A
    pick_a = jnp.where(pick_a, 1.0, 0.0).astype(BF16)
    pick_b = lax.broadcasted_iota(jnp.int32, (8, KB), 1) == BLK_B
    pick_b = jnp.where(pick_b, 1.0, 0.0).astype(BF16)
    lane_q = lax.broadcasted_iota(jnp.int32, (1, QA), 1)
    d_out = do_ref[...]
    d_out_w = (wide(d_out) * weight).astype(BF16)
    starts = {0: QA} | {QA + i * QB: QB for i in range(IMB)}
    q_turned = {at: jnp.transpose(wide(q_ref[at : at + size])).astype(BF16) for at, size in starts.items()}
    d_turned = {at: jnp.transpose(wide(d_out_w[at : at + size])).astype(BF16) for at, size in starts.items()}
    dq_parts, dk_parts, dv_parts = [], [], []
    for t in range(2):
        mine = low if t == 0 else jnp.logical_not(low)
        d_mine = jnp.where(mine, d_out, jnp.zeros((), BF16))

        def one(q_at, q_len, k_at, k_len, probs):
            d_probs = dot_last(d_mine[q_at : q_at + q_len], v_ref[k_at : k_at + k_len])
            delta = jnp.sum(probs * d_probs, axis=-1, keepdims=True)
            d_wide = probs * (d_probs - delta)
            d_low = d_wide.astype(BF16)
            d_query = dot_plain(d_low, k_ref[k_at : k_at + k_len])
            d_w = (wide(d_low) * weight[q_at : q_at + q_len]).astype(BF16)
            rows = slice(t * HEAD_DIM, (t + 1) * HEAD_DIM)
            d_key = dot_plain(q_turned[q_at][rows], d_w)
            d_value = dot_plain(d_turned[q_at][rows], probs.astype(BF16))
            return d_query, d_key, d_value, d_w

        d_query, d_key, d_value, d_w = one(0, QA, 0, KA, pa_ref[t])
        dqs, dks, dvs = [d_query], [d_key], [d_value]
        flipped = jnp.where(lane_a < PAT_A, dot_plain(turned, d_w), 0.0)
        flipped = jnp.concatenate([flipped, jnp.zeros((BLK_A, STRIP - KA), F32)], axis=1)
        strip = None
        for r in range(GROUPS):
            off = (GROUPS - 1 - r) * SIDE_A
            piece = flipped[r * SIDE_A : (r + 1) * SIDE_A]
            piece = piece if off == 0 else pltpu.roll(piece, off, 1)
            strip = piece if strip is None else strip + piece
        fold = [col_sum(part) for part in fold_strip(strip, SIDE_A)]
        row_a = wide(d_w[BLK_A : BLK_A + 16])[:1]
        col_a = jnp.where(lane_q < BLK_A, dot_last(pick_a, d_w)[:1], 0.0)
        moved, row_b, col_b = None, None, None
        for i in range(IMB):
            d_query, d_key, d_value, d_w = one(QA + i * QB, QB, KA + i * KB, KB, pb_ref[t, i])
            dqs.append(d_query)
            dks.append(d_key)
            dvs.append(d_value)
            laid = dot_plain(dot_plain(order, d_w).astype(BF16), spread)
            row = wide(d_w[BLK_B - 8 : BLK_B + 8])[8:9]
            col = jnp.where(lane_q[:, :QB] < BLK_B, dot_last(pick_b, d_w)[:1], 0.0)
            moved = laid if i == 0 else moved + laid
            row_b = row if i == 0 else row_b + row
            col_b = col if i == 0 else col_b + col
        strip = None
        for piece in strips_b(moved):
            strip = piece if strip is None else strip + piece
        fold_b = [col_sum(left + right) for left, right in fold_strip_b(strip)]
        g_ref[t, 0:1] = fold[0]
        g_ref[t, 1:2] = fold[1]
        g_ref[t, 2:3, 0:KB] = fold_b[0]
        g_ref[t, 2:3, KB : 2 * KB] = fold_b[1]
        g_ref[t, 2:3, 2 * KB :] = row_b
        g_ref[t, 3:4, 0:KA] = row_a
        g_ref[t, 3:4, KA:] = jnp.concatenate([col_b, jnp.zeros((1, 128 - QB), F32)], axis=1)
        g_ref[t, 4:5, 0:256] = jnp.concatenate([col_a, jnp.zeros((1, 256 - QA), F32)], axis=1)
        g_ref[t, 4:5, 256:] = jnp.zeros((1, STRIP - 256), F32)
        g_ref[t, 5:8] = jnp.zeros((3, STRIP), F32)
        dq_parts.append(jnp.concatenate(dqs, axis=0))
        dk_parts.append(jnp.concatenate(dks, axis=1))
        dv_parts.append(jnp.concatenate(dvs, axis=1))
    d_query = jnp.where(low, dq_parts[0], dq_parts[1]).astype(BF16)
    dq_ref[...] = (wide(d_query) * (1.0 / math.sqrt(HEAD_DIM))).astype(BF16)
    dk_ref[...] = jnp.transpose(jnp.concatenate(dk_parts, axis=0)).astype(BF16)
    dv_ref[...] = jnp.transpose(jnp.concatenate(dv_parts, axis=0)).astype(BF16)


def attend_back(place, part, d_mixed, queries, keys, values, probs_a, probs_b):
    pairs = HEADS // 4
    base = part * pairs
    return pl.pallas_call(
        attend_back_kernel,
        grid=(pairs,),
        in_specs=[
            SSPEC,
            pl.BlockSpec((NQ, 128), lambda p: (0, base + p)),
            pl.BlockSpec((NQ, 128), lambda p: (0, base + p)),
            pl.BlockSpec((NK, 128), lambda p: (0, base + p)),
            pl.BlockSpec((NK, 128), lambda p: (0, base + p)),
            pl.BlockSpec((2, QA, KA), lambda p: (base + p, 0, 0)),
            pl.BlockSpec((2, IMB, QB, KB), lambda p: (base + p, 0, 0, 0)),
        ],
        out_specs=[
            pl.BlockSpec((NQ, 128), lambda p: (0, p)),
            pl.BlockSpec((NK, 128), lambda p: (0, p)),
            pl.BlockSpec((NK, 128), lambda p: (0, p)),
            pl.BlockSpec((2, 8, STRIP), lambda p: (p, 0, 0)),
        ],
        out_shape=[
            jax.ShapeDtypeStruct((NQ, D // 2), BF16),
            jax.ShapeDtypeStruct((NK, D // 2), BF16),
            jax.ShapeDtypeStruct((NK, D // 2), BF16),
            jax.ShapeDtypeStruct((HEADS // 2, 8, STRIP), F32),
        ],
        compiler_params=params(24),
        cost_estimate=cost(6 * HEADS * 128 * (QA * KA + IMB * QB * KB), 15e6),
        name="attend_back",
    )(place, d_mixed, queries, keys, values, probs_a, probs_b)


def table_kernel(g0_ref, g1_ref, ids_ref, out_ref):
    rows = lax.broadcasted_iota(jnp.int32, (CHUNK, STRIP), 0)
    split = []
    for at in range(5):
        values = jnp.concatenate([g0_ref[:, at], g1_ref[:, at]], axis=0)
        top = values.astype(BF16)
        rest = values - wide(top)
        middle = rest.astype(BF16)
        bottom = (rest - wide(middle)).astype(BF16)
        pad = jnp.zeros((4, STRIP), F32)
        stacked = []
        for part in (top, middle, bottom):
            stacked += [wide(part), pad]
        split.append(jnp.concatenate(stacked, axis=0).astype(BF16))

    for step in range(TABLE // CHUNK):
        total = jnp.zeros((48, CHUNK), F32)
        for at in range(5):
            hot = jnp.where(rows + step * CHUNK == ids_ref[at : at + 1], 1.0, 0.0).astype(BF16)
            total = total + dot_last(split[at], hot)
        out_ref[:, step * CHUNK : (step + 1) * CHUNK] = total[:16] + total[16:32] + total[32:]


def table_grad(first, second, ids):
    return pl.pallas_call(
        table_kernel,
        in_specs=[VSPEC] * 3,
        out_specs=VSPEC,
        out_shape=jax.ShapeDtypeStruct((16, TABLE), F32),
        compiler_params=params(),
        cost_estimate=cost(2 * 48 * TABLE * 5 * STRIP, 2e6),
        name="table_grad",
    )(first, second, ids)


def flip_rows(count, size):
    new_row = lax.broadcasted_iota(jnp.int32, (count, count), 0)
    old_row = lax.broadcasted_iota(jnp.int32, (count, count), 1)
    turned = old_row == new_row // size * size + (size - 1 - new_row % size)
    return jnp.where(turned, 1.0, 0.0).astype(BF16)


def ids_kernel(place_ref, ia_ref, ib_ref, a_ref, b_ref, f_ref):
    place = place_ref[0]

    def through(matrix, ids):
        high = (ids // 64).astype(F32).astype(BF16)
        low = (ids % 64).astype(F32).astype(BF16)
        return 64.0 * dot_plain(matrix, high) + dot_plain(matrix, low)

    def column(ids, at):
        pick = lax.broadcasted_iota(jnp.int32, (8, ids.shape[1]), 1) == at
        pick = jnp.where(pick, 1.0, 0.0).astype(BF16)
        high = (ids // 64).astype(F32).astype(BF16)
        low = (ids % 64).astype(F32).astype(BF16)
        return (64.0 * dot_last(pick, high) + dot_last(pick, low))[:1].astype(jnp.int32)

    def fill(row, width):
        return jnp.concatenate([row, jnp.zeros((row.shape[0], width - row.shape[1]), jnp.int32)], axis=1)

    top = (GROUPS - 1) * SIDE_A
    for at in range(4):

        @pl.when(place == at)
        def _():
            rows_a = ia_ref[1 + BLK_A * at : 1 + BLK_A * (at + 1), :]
            last, first = rows_a[top:, 1 : 1 + top], rows_a[:SIDE_A, 1:]
            a_ref[:SIDE_A] = fill(jnp.concatenate([last, first], axis=1), STRIP)
            f_ref[4:5] = fill(column(rows_a, 0), STRIP)
            rows_b = jnp.concatenate(
                [ib_ref[1 + BLK_B * at : 1 + BLK_B * (at + 1), :], ib_ref[0:1, :], jnp.zeros((7, SLOT_B + 1), jnp.int32)],
                axis=0,
            )
            parts = []
            for k in range(4):
                parts += [rows_b[:, 1 + k * BLK_B : 1 + (k + 1) * BLK_B], rows_b[:, :1], jnp.zeros((QB, 7), jnp.int32)]
            b_ref[...] = jnp.concatenate(parts, axis=1)
            f_ref[3:4, KA:] = fill(column(rows_b, 0)[:, :BLK_B], 128)

    class_row = jnp.concatenate([ia_ref[0:1, 1:], ia_ref[0:1, :1]], axis=1)
    a_ref[SIDE_A : SIDE_A + 1] = fill(class_row, STRIP)
    a_ref[SIDE_A + 1 : SIDE_A + 2] = f_ref[4:5]
    a_ref[SIDE_A + 2 :] = jnp.zeros((6, STRIP), jnp.int32)
    f_ref[3:4, :KA] = fill(class_row, KA)
    f_ref[2:3, 2 * KB :] = b_ref[BLK_B : BLK_B + 1]
    f_ref[5:8] = jnp.zeros((3, STRIP), jnp.int32)
    turned = through(flip_rows(SIDE_A, SIDE_A), a_ref[:SIDE_A])
    lane = lax.broadcasted_iota(jnp.int32, (1, STRIP), 1)
    turned = jnp.where(lane < REACH * SIDE_A, turned, 0.0)
    for at, part in enumerate(fold_strip(turned, SIDE_A)):
        f_ref[at : at + 1] = jnp.max(part, axis=0, keepdims=True).astype(jnp.int32)
    order, spread = orders_b(place % 2)
    laid = through(order, b_ref[...]).astype(jnp.int32)
    high = (laid // 64).astype(F32).astype(BF16)
    low = (laid % 64).astype(F32).astype(BF16)
    laid = 64.0 * dot_plain(high, spread) + dot_plain(low, spread)
    strip = None
    for piece in strips_b(laid):
        strip = piece if strip is None else jnp.maximum(strip, piece)
    for at, (left, right) in enumerate(fold_strip_b(strip)):
        found = jnp.max(jnp.maximum(left, right), axis=0, keepdims=True)
        f_ref[2:3, at * KB : (at + 1) * KB] = found.astype(jnp.int32)


def all_ids(pos, index_a, index_b):
    return pl.pallas_call(
        ids_kernel,
        in_specs=[SSPEC, VSPEC, VSPEC],
        out_specs=[VSPEC] * 3,
        out_shape=[jax.ShapeDtypeStruct(shape, jnp.int32) for shape in ((32, STRIP), (QB, KB), (8, STRIP))],
        compiler_params=params(),
        cost_estimate=cost(1e8, 6e6),
        name="ids",
    )(pos[3:], index_a, index_b)


def feed_kernel(meta, pos_ref, cnt_ref, mixed_ref, x_ref, cot_ref, vec_ref, b1_ref, *refs):
    (p_out, p_up, p_down), (q_out, q_up, q_down) = meta
    refs = list(refs)

    def take(count):
        taken = refs[:count]
        del refs[:count]
        return taken

    wo_refs, wu_refs, wd_refs = take(len(p_out)), take(len(p_up)), take(len(p_down))
    fa_ref, fca_ref, fb_ref, fcb_ref, dres_ref, dmix_ref, gv_ref, gb_ref = take(8)
    go_refs, gu_refs, gd_refs = take(len(q_out)), take(len(q_up)), take(len(q_down))
    wo, wu, wd, go, gu, gd, norm, gelu, slope, d_hid, dsec, dsec_w, sem_o, sem_u, sem_d = refs
    pos = [pos_ref[at] for at in range(3)]
    loads = [copies_in(pos, *each) for each in ((p_out, wo_refs, wo, sem_o), (p_up, wu_refs, wu, sem_u), (p_down, wd_refs, wd, sem_d))]
    for group in loads:
        for copy in group:
            copy.start()

    def piece(at):
        return vec_ref[at : at + 1]

    place = pos_ref[3]
    weight = row_weights(jnp.where(place == 0, 1.0, 0.0))
    row = lax.broadcasted_iota(jnp.int32, (NQ, 1), 0)
    slot = (row - QA) % QB
    count_b = jnp.where(row < QA + QB, cnt_ref[1], cnt_ref[2])
    live_a = ((row < BLK_A) & (place * BLK_A + row < cnt_ref[0])) | (row == BLK_A)
    live_b = ((slot < REAL_B) & (place * REAL_B + slot < count_b)) | (slot == BLK_B)
    live = jnp.where(((row < QA) & live_a) | ((row >= QA) & live_b), 1.0, 0.0)

    for copy in loads[0]:
        copy.wait()
    branch = dot_plain(mixed_ref[...], wo[...]) + piece(4)
    resid = wide(x_ref[...]) + piece(5) * branch
    unit, inv_std = unit_of(resid)
    norm[...] = (unit * piece(6) + piece(7)).astype(BF16)
    for copy in loads[1]:
        copy.wait()

    @pl.loop(0, FF // STEP)
    def _(at):
        cols = pl.ds(pl.multiple_of(at * STEP, STEP), STEP)
        hidden = dot_plain(norm[...], wu[:, cols]) + b1_ref[pl.ds(at, 1), :]
        gate = 0.5 * (1.0 + lax.erf(hidden * ROOT_HALF))
        gelu[:, cols] = (hidden * gate).astype(BF16)
        slope[:, cols] = gate + hidden * ROOT_TAU * jnp.exp(-0.5 * hidden * hidden)

    for copy in loads[2]:
        copy.wait()
    second = dot_plain(gelu[...], wd[...]) + piece(8)
    final = resid + piece(9) * second
    fa_ref[0] = final[:BLK_A]
    fca_ref[...] = final[BLK_A : BLK_A + 1]
    d_final = wide(cot_ref[...]) * live
    for i in range(IMB):
        fb_ref[i] = final[QA + i * QB : QA + i * QB + BLK_B]
        fcb_ref[i : i + 1] = final[QA + i * QB + BLK_B : QA + i * QB + BLK_B + 1]
    gv_ref[5:6] = col_sum(d_final * second * weight)
    d_second = (piece(9) * d_final).astype(BF16)
    dsec[...] = d_second
    d_second_w = wide(d_second) * weight
    gv_ref[4:5] = col_sum(d_second_w)
    dsec_w[...] = d_second_w.astype(BF16)

    @pl.loop(0, FF // STEP)
    def _(at):
        cols = pl.ds(pl.multiple_of(at * STEP, STEP), STEP)
        d_gelu = dot_last(dsec[...], wd[cols, :])
        d_hid[:, cols] = (d_gelu * slope[:, cols]).astype(BF16)
        gd[cols, :] = dot_first(gelu[:, cols], dsec_w[...]).astype(BF16)

    stores = copies_out(pos, q_down, gd_refs, gd, sem_d)
    for copy in stores:
        copy.start()

    @pl.loop(0, FF // STEP)
    def _(at):
        cols = pl.ds(pl.multiple_of(at * STEP, STEP), STEP)
        d_hidden_w = wide(d_hid[:, cols]) * weight
        gb_ref[pl.ds(at, 1), :] = col_sum(d_hidden_w)
        gu[:, cols] = dot_first(norm[...], d_hidden_w.astype(BF16)).astype(BF16)

    more = copies_out(pos, q_up, gu_refs, gu, sem_u)
    for copy in more:
        copy.start()
    stores += more
    d_normed = dot_last(d_hid[...], wu[...])
    d_normed_w = d_normed * weight
    gv_ref[2:3] = col_sum(d_normed_w * unit)
    gv_ref[3:4] = col_sum(d_normed_w)
    d_resid = d_final + norm_back(d_normed, unit, inv_std, piece(6))
    dres_ref[...] = d_resid
    gv_ref[1:2] = col_sum(d_resid * branch * weight)
    d_branch = (piece(5) * d_resid).astype(BF16)
    d_branch_w = wide(d_branch) * weight
    gv_ref[0:1] = col_sum(d_branch_w)
    gv_ref[6:8] = jnp.zeros((2, D), F32)
    go[...] = dot_first(mixed_ref[...], d_branch_w.astype(BF16)).astype(BF16)
    last = copies_out(pos, q_out, go_refs, go, sem_o)
    for copy in last:
        copy.start()
    dmix_ref[...] = dot_last(d_branch, wo[...]).astype(BF16)
    for copy in stores + last:
        copy.wait()


def feed(pos, counts, mixed, x_loc, cot, vec, b1, weights, orders):
    (a_out, p_out), (a_up, p_up), (a_down, p_down) = weights
    q_out = grad_pieces(D, D, orders[0])
    q_up = grad_pieces(D, FF, orders[1])
    q_down = grad_pieces(FF, D, orders[2])
    grads = q_out + q_up + q_down
    shapes = [
        jax.ShapeDtypeStruct((IMA, BLK_A, D), F32),
        jax.ShapeDtypeStruct((IMA, D), F32),
        jax.ShapeDtypeStruct((IMB, BLK_B, D), F32),
        jax.ShapeDtypeStruct((IMB, D), F32),
        jax.ShapeDtypeStruct((NQ, D), F32),
        jax.ShapeDtypeStruct((NQ, D), BF16),
        jax.ShapeDtypeStruct((8, D), F32),
        jax.ShapeDtypeStruct((FF // STEP, STEP), F32),
    ]
    outs = pl.pallas_call(
        functools.partial(feed_kernel, ((p_out, p_up, p_down), (q_out, q_up, q_down))),
        in_specs=[SSPEC] * 2 + [VSPEC] * 5 + [ANYSPEC] * (len(a_out) + len(a_up) + len(a_down)),
        out_specs=[VSPEC] * 8 + [ANYSPEC] * len(grads),
        out_shape=shapes + [jax.ShapeDtypeStruct((p.blocks, p.rows, p.cols), BF16) for p in grads],
        scratch_shapes=[
            pltpu.VMEM((D, D), BF16),
            pltpu.VMEM((D, FF), BF16),
            pltpu.VMEM((FF, D), BF16),
            pltpu.VMEM((D, D), BF16),
            pltpu.VMEM((D, FF), BF16),
            pltpu.VMEM((FF, D), BF16),
            pltpu.VMEM((NQ, D), BF16),
            pltpu.VMEM((NQ, FF), BF16),
            pltpu.VMEM((NQ, FF), F32),
            pltpu.VMEM((NQ, FF), BF16),
            pltpu.VMEM((NQ, D), BF16),
            pltpu.VMEM((NQ, D), BF16),
            pltpu.SemaphoreType.DMA((max(piece_count(p_out), piece_count(q_out)),)),
            pltpu.SemaphoreType.DMA((max(piece_count(p_up), piece_count(q_up)),)),
            pltpu.SemaphoreType.DMA((max(piece_count(p_down), piece_count(q_down)),)),
        ],
        compiler_params=params(48),
        cost_estimate=cost(6 * NQ * D * (D + 2 * FF), 30e6),
        name="feed",
    )(pos, counts, mixed, x_loc, cot, vec, b1, *a_out, *a_up, *a_down)
    plain, rest = outs[:8], list(outs[8:])
    g_out = [rest.pop(0) for _ in q_out]
    g_up = [rest.pop(0) for _ in q_up]
    g_down = [rest.pop(0) for _ in q_down]
    return plain, g_out, g_up, g_down


def back_kernel(p_qkv, q_qkv, q_out, pos_ref, dq0_ref, dk0_ref, dv0_ref, dq1_ref, dk1_ref, dv1_ref, na_ref, nl_ref, xa_ref, xl_ref, *refs):
    refs = list(refs)

    def take(count):
        taken = refs[:count]
        del refs[:count]
        return taken

    w_refs, o_refs = take(len(p_qkv)), take(len(q_out))
    local_ref, keep_ref, send_ref, gv_ref = take(4)
    g_refs = take(2 if small_grid() else len(q_qkv))
    w, g, rows_all, sums, sem_w, sem_g, sem_o = refs
    pos = [pos_ref[at] for at in range(3)]
    place = pos_ref[3]
    loads = copies_in(pos, p_qkv, w_refs, w, sem_w)
    for copy in loads:
        copy.start()
    targets = [g_refs[at % 2] if small_grid() else g_refs[at] for at in range(len(q_qkv))]
    passed = []
    for piece, source, ref in zip(q_out, o_refs, targets):
        for k in range(piece.blocks):
            passed.append(pltpu.make_async_copy(source.at[k], piece.part(ref, k), sem_o.at[len(passed)]))
            passed[-1].start()
    weight = row_weights(jnp.where(place == 0, 1.0, 0.0))
    d_query = jnp.concatenate([dq0_ref[...], dq1_ref[...]], axis=1)
    d_query_w = wide(d_query) * weight
    gv_ref[2:3] = col_sum(d_query_w)
    g[:, :D] = dot_first(nl_ref[...], d_query_w.astype(BF16)).astype(BF16)

    half = D // 2
    for at, (dk_ref, dv_ref) in enumerate(((dk0_ref, dv0_ref), (dk1_ref, dv1_ref))):
        g[:, D + at * half : D + (at + 1) * half] = dot_first(na_ref[...], dk_ref[...]).astype(BF16)
        g[:, 2 * D + at * half : 2 * D + (at + 1) * half] = dot_first(na_ref[...], dv_ref[...]).astype(BF16)

    stores = copies_out(pos, q_qkv, targets, g, sem_g)
    for copy in stores:
        copy.start()
    for copy in loads:
        copy.wait()
    sums[...] = jnp.zeros((8, D), F32)

    @pl.loop(0, NK // 384)
    def _(at):
        rows = pl.ds(pl.multiple_of(at * 384, 128), 384)
        d_key = jnp.concatenate([dk0_ref[rows], dk1_ref[rows]], axis=1)
        d_value = jnp.concatenate([dv0_ref[rows], dv1_ref[rows]], axis=1)
        d_norm = dot_last(d_key, w[:, D : 2 * D]) + dot_last(d_value, w[:, 2 * D :])
        rows_all[rows] = d_norm
        unit = unit_of(wide(xa_ref[rows]))[0]
        sums[0:1] += col_sum(d_norm * unit)
        sums[1:2] += col_sum(d_norm)
        sums[2:3] += col_sum(wide(d_value))

    d_local = dot_last(d_query, w[:, :D])
    d_local_w = d_local * weight
    unit = unit_of(wide(xl_ref[...]))[0]
    gv_ref[0:1] = sums[0:1] + col_sum(d_local_w * unit)
    gv_ref[1:2] = sums[1:2] + col_sum(d_local_w)
    gv_ref[3:4] = sums[2:3]
    gv_ref[4:8] = jnp.zeros((4, D), F32)
    class_a = rows_all[PAT_A : PAT_A + 8][:1]
    class_b = [rows_all[KA + i * KB + BLK_B : KA + i * KB + BLK_B + 8][:1] for i in range(IMB)]
    row_b = lax.broadcasted_iota(jnp.int32, (QB, 1), 0)

    zh, zl = place // 2, place % 2

    def block_of(at):
        part_a = rows_all[pl.ds(pl.multiple_of(at * BLK_A, BLK_A), BLK_A)]
        parts = [part_a]
        for i in range(IMB):
            part = rows_all[pl.ds(pl.multiple_of(KA + i * KB + at * QB, QB), QB)]
            part = jnp.where(row_b == BLK_B, class_b[i], part)
            part = jnp.where(row_b == BLK_B + 1, class_a, part) if i == 0 else part
            parts.append(part)
        return parts

    for step in (0, 1):
        high = zh if step == 0 else 1 - zh
        send_ref[step] = jnp.concatenate(block_of(high * 2 + 1 - zl), axis=0).astype(BF16)
    keep_ref[...] = jnp.concatenate(block_of((1 - zh) * 2 + zl), axis=0)
    own = block_of(place)
    local_ref[:BLK_A] = own[0] + d_local[:BLK_A]
    local_ref[BLK_A : BLK_A + 16] = jnp.concatenate(
        [own[1][BLK_B + 1 : BLK_B + 2] + d_local[BLK_A : BLK_A + 1], jnp.zeros((15, D), F32)], axis=0
    )
    for i in range(IMB):
        at = QA + i * QB
        local_ref[at : at + QB] = own[1 + i] + d_local[at : at + QB]
    for copy in stores + passed:
        copy.wait()


def back(pos, first, second, normed_all, normed_loc, x_all, x_loc, arrays, pieces, g_out):
    q_qkv, q_out = grad_pieces(D, 3 * D, "split"), grad_pieces(D, D, "split")
    width = q_qkv[0].cols
    joint = [(1, D, 2 * D)] * 2
    if small_grid():
        joint = [(8, D // 8, 2 * D)] * 2
        for at in range(4):
            q_qkv[at].first = q_out[at].first = at // 2 * 4
    for piece in q_out:
        piece.src = width
    shapes = [((NQ, D), F32), ((BLOCK, D), F32), ((2, BLOCK, D), BF16), ((8, D), F32)]
    outs = pl.pallas_call(
        functools.partial(back_kernel, pieces, q_qkv, q_out),
        in_specs=[SSPEC] + [VSPEC] * 10 + [ANYSPEC] * len(arrays) + [VSPEC] * len(g_out),
        out_specs=[VSPEC] * 4 + [ANYSPEC] * 2,
        out_shape=[jax.ShapeDtypeStruct(*each) for each in shapes]
        + [jax.ShapeDtypeStruct(shape, BF16) for shape in joint],
        scratch_shapes=[
            pltpu.VMEM((D, 3 * D), BF16),
            pltpu.VMEM((D, 3 * D), BF16),
            pltpu.VMEM((NK, D), F32),
            pltpu.VMEM((8, D), F32),
            pltpu.SemaphoreType.DMA((piece_count(pieces),)),
            pltpu.SemaphoreType.DMA((piece_count(q_qkv),)),
            pltpu.SemaphoreType.DMA((piece_count(q_out),)),
        ],
        compiler_params=params(24),
        cost_estimate=cost(4 * D * D * (NQ + 2 * NK), 20e6),
        name="back",
    )(pos, *first, *second, normed_all, normed_loc, x_all, x_loc, *arrays, *g_out)
    return outs[:4], list(outs[4:])


def finish_kernel(dres_ref, local_ref, r1_ref, r2_ref, x_ref, vec_ref, ga_ref, gca_ref, gb_ref, gcb_ref):
    gain = vec_ref[0:1]

    def rows_of(at, count, got_at):
        grad = local_ref[at : at + count]
        grad = grad + wide(r1_ref[0, got_at : got_at + count]) + wide(r2_ref[got_at : got_at + count])
        unit, inv_std = unit_of(wide(x_ref[at : at + count]))
        return dres_ref[at : at + count] + norm_back(grad, unit, inv_std, gain)

    ga_ref[0] = rows_of(0, BLK_A, 0)
    for i in range(IMB):
        at = QA + i * QB
        rows = rows_of(at, QB, BLK_A + i * QB)
        gb_ref[i] = rows[:BLK_B]
        gcb_ref[i : i + 1] = rows[BLK_B : BLK_B + 1]
    grad = local_ref[BLK_A : BLK_A + 16]
    spot = BLK_A + 48
    grad = grad + wide(r1_ref[0, spot : spot + 16])[9:10] + wide(r2_ref[spot : spot + 16])[9:10]
    unit, inv_std = unit_of(wide(x_ref[BLK_A : BLK_A + 16]))
    rows = dres_ref[BLK_A : BLK_A + 16] + norm_back(grad, unit, inv_std, gain)
    gca_ref[...] = rows[:1]


def finish(d_resid, local, got, x_loc, vec):
    return pl.pallas_call(
        finish_kernel,
        in_specs=[VSPEC] * 6,
        out_specs=[VSPEC] * 4,
        out_shape=[
            jax.ShapeDtypeStruct((IMA, BLK_A, D), F32),
            jax.ShapeDtypeStruct((IMA, D), F32),
            jax.ShapeDtypeStruct((IMB, BLK_B, D), F32),
            jax.ShapeDtypeStruct((IMB, D), F32),
        ],
        compiler_params=params(),
        cost_estimate=cost(1e6, 6e6),
        name="finish",
    )(d_resid, local, *got, x_loc, vec)


def add_kernel(counts, *refs):
    ins, outs = refs[: sum(counts)], refs[sum(counts) :]
    at = 0
    for count, out in zip(counts, outs):
        total = wide(ins[at][...])
        for ref in ins[at + 1 : at + count]:
            total = total + wide(ref[...])
        out[...] = total.astype(BF16)
        at += count


def add_blocks(*groups):
    steps = 3
    specs, arrays, outs, shapes = [], [], [], []
    for group in groups:
        for array, first, count in group:
            rows, cols = array.shape[1:]
            specs.append(
                pl.BlockSpec((count, rows, cols // steps), lambda i, at=first // count: (at, 0, i))
            )
            arrays.append(array)
        outs.append(pl.BlockSpec((count, rows, cols // steps), lambda i: (0, 0, i)))
        shapes.append(jax.ShapeDtypeStruct((count, rows, cols), BF16))
    return pl.pallas_call(
        functools.partial(add_kernel, [len(group) for group in groups]),
        grid=(steps,),
        in_specs=specs,
        out_specs=outs,
        out_shape=shapes,
        compiler_params=params(),
        cost_estimate=cost(1, 1),
        name="add_blocks",
    )(*arrays)


def split_kernel(counts, zl_ref, *refs):
    ins, (send, kept) = refs[: sum(counts)], refs[sum(counts) :]
    first = zl_ref[0] == 0
    sums, at = [], 0
    for count in counts:
        total = wide(ins[at][0])
        for ref in ins[at + 1 : at + count]:
            total = total + wide(ref[0])
        sums.append(total)
        at += count
    groups = []
    for z in range(4):
        parts = []
        for total in sums:
            rows = total.shape[0] // 4
            part = total[z * rows : (z + 1) * rows]
            if rows > 24:
                part = jnp.concatenate([part[at : at + 24] for at in range(0, rows, 24)], axis=1)
            parts.append(part)
        axis = 1 if sums[0].shape == sums[1].shape else 0
        groups.append(jnp.concatenate(parts, axis=axis))
    for zh in range(2):
        one, two = groups[2 * zh], groups[2 * zh + 1]
        send[zh] = jnp.where(first, two, one).astype(BF16)
        kept[zh] = jnp.where(first, one, two)


def split_blocks(zl, rows, *groups):
    specs, arrays = [], []
    for group in groups:
        for array, first in group:
            specs.append(pl.BlockSpec((1,) + array.shape[1:], lambda i, at=first: (at, 0, 0)))
            arrays.append(array)
    shape = (2, rows, FF)
    return pl.pallas_call(
        functools.partial(split_kernel, [len(group) for group in groups]),
        grid=(1,),
        in_specs=[SSPEC] + specs,
        out_specs=[pl.BlockSpec(shape, lambda i: (0, 0, 0))] * 2,
        out_shape=[jax.ShapeDtypeStruct(shape, BF16), jax.ShapeDtypeStruct(shape, F32)],
        compiler_params=params(),
        cost_estimate=cost(1, 1),
        name="split_blocks",
    )(zl[None], *arrays)


def half_kernel(zh_ref, kept_ref, got_ref, send, keep):
    zh = zh_ref[0]
    send[...] = (kept_ref[1 - zh] + wide(got_ref[1 - zh])).astype(BF16)
    keep[...] = kept_ref[zh] + wide(got_ref[zh])


def half_blocks(zh, kept, got):
    return pl.pallas_call(
        half_kernel,
        in_specs=[SSPEC, VSPEC, VSPEC],
        out_specs=[VSPEC] * 2,
        out_shape=[jax.ShapeDtypeStruct(kept.shape[1:], BF16), jax.ShapeDtypeStruct(kept.shape[1:], F32)],
        compiler_params=params(),
        cost_estimate=cost(1, 1),
        name="half_blocks",
    )(zh[None], kept, got)


def pad_to(values, width):
    return jnp.pad(values, ((0, width - values.shape[0]),))


def nesterov(master, moment, average, grad_w, step_rate):
    moment_new = 0.5 * moment + grad_w
    master_new = master - step_rate * (grad_w + 0.5 * moment_new)
    return (master_new, moment_new, 0.5 * average + 0.5 * master_new)


def pair_up(value, other, axis):
    first = lax.axis_index(axis) == 0
    return jnp.stack([jnp.where(first, value, other), jnp.where(first, other, value)])


def across(mine, other):
    first = lax.axis_index("zl") == 0
    return jnp.stack([jnp.where(first, mine, other), jnp.where(first, other, mine)], axis=1)


def zl_parts(block):
    cut = block.reshape(2, 2, block.shape[0] // 4, block.shape[1])
    zl = lax.axis_index("zl")
    send = lax.dynamic_index_in_dim(cut, 1 - zl, 1, keepdims=False).astype(BF16)
    return send, lax.dynamic_index_in_dim(cut, zl, 1, keepdims=False)


def zh_parts(kept, got):
    zh = lax.axis_index("zh")
    both = kept + wide(got)
    send = lax.dynamic_index_in_dim(both, 1 - zh, 0, keepdims=False).astype(BF16)
    return send, lax.dynamic_index_in_dim(both, zh, 0, keepdims=False)


def sum_z(block):
    send, kept = zl_parts(block)
    send, kept = zh_parts(kept, swap(send, "zl"))
    return kept + wide(swap(send, "zh"))


def tick(*values):
    return lax.optimization_barrier(values)


def pack_kernel(xa_ref, xca_ref, xb_ref, xcb_ref, ca_ref, cca_ref, cb_ref, ccb_ref, x_ref, cot_ref, send_ref):
    def lay(rows_a, class_a, rows_b, class_b):
        zero = jnp.zeros((16, D), F32)
        parts = [wide(rows_a[0]), wide(class_a[...]), zero[: QA - BLK_A - 1]]
        for i in range(IMB):
            parts += [wide(rows_b[i]), wide(class_b[i : i + 1]), zero[: QB - BLK_B - 1]]
        return jnp.concatenate(parts, axis=0).astype(BF16)

    rows = lay(xa_ref, xca_ref, xb_ref, xcb_ref)
    x_ref[...] = rows
    send_ref[:BLK_A] = rows[:BLK_A]
    send_ref[BLK_A:] = rows[QA:]
    cot_ref[...] = lay(ca_ref, cca_ref, cb_ref, ccb_ref)


def pack(*rows):
    return pl.pallas_call(
        pack_kernel,
        in_specs=[VSPEC] * 8,
        out_specs=[VSPEC] * 3,
        out_shape=[jax.ShapeDtypeStruct((count, D), BF16) for count in (NQ, NQ, BLOCK)],
        compiler_params=params(),
        cost_estimate=cost(1e6, 2e6),
        name="pack",
    )(*rows)


LEFT = 3 * D // 2 + D // 2


def body(
    patches_a, class_a, patches_b, class_b, count_a, count_b, index_a, index_b,
    cot_a, cot_class_a, cot_b, cot_class_b,
    qkv_weight, qkv_momentum, qkv_average, out_weight, out_momentum, out_average,
    up_weight, up_momentum, up_average, down_weight, down_momentum, down_average,
    table_weight, table_momentum, table_average, vector_weight, vector_momentum, vector_average,
):
    zh, zl = lax.axis_index("zh"), lax.axis_index("zl")
    place = zh * 2 + zl
    devices = lax.axis_size(AXES)
    n0, n1, nc = [lax.axis_size(axis) for axis in AXES[:3]]
    pos = jnp.stack([lax.axis_index("d0"), lax.axis_index("d1"), lax.axis_index("c"), place]).astype(jnp.int32)
    counts = jnp.concatenate([count_a, count_b, jnp.zeros((1,), jnp.int32)])

    grid = small_grid()
    t_rows, v_len = table_weight.shape[0], vector_weight.shape[0]
    small = jnp.concatenate([table_weight.reshape(-1), vector_weight])
    small = pad_to(small, qkv_weight.shape[0] * 128).reshape(-1, 128)
    half, part = 3 * D // 2, D // 2
    qkv = jnp.concatenate(
        [qkv_weight[:, :half], out_weight[:, :part], qkv_weight[:, half:], out_weight[:, part:], small], axis=1
    ).astype(BF16)

    q_one = swap(qkv, "zh")
    up, down = up_weight.astype(BF16), down_weight.astype(BF16)
    x_loc, cot, message = pack(patches_a, class_a, patches_b, class_b, cot_a, cot_class_a, cot_b, cot_class_b)
    q_one, up, down, x_loc, cot, message = tick(q_one, up, down, x_loc, cot, message)

    q_pair, up = tick(pair_up(qkv, q_one, "zh"), up)
    q_two, u_one = swap(q_pair, "zl"), swap(up, "zh")
    q_two, u_one = tick(q_two, u_one)

    q_block = across(q_pair, q_two).reshape(-1, qkv.shape[1])
    left, right = q_block[:, :LEFT], q_block[:, LEFT:]
    u_pair = pair_up(up, u_one, "zh")
    left, right, u_pair, down, index_a, index_b = tick(left, right, u_pair, down, index_a, index_b)
    if grid:
        l_one, r_one = swap(left, "d0"), swap(right, "d1")
    u_two, d_one = swap(u_pair, "zl"), swap(down, "zh")
    ids = all_ids(pos, index_a, index_b)
    if grid:
        l_one, r_one, u_two, d_one, ids = tick(l_one, r_one, u_two, d_one, ids)
        l_two, r_two = jnp.stack([left, l_one]), jnp.stack([right, r_one])
    else:
        u_two, d_one, ids = tick(u_two, d_one, ids)
        l_two, r_two = left, right
    d_pair = pair_up(down, d_one, "zh")
    l_two, r_two, d_pair, message = tick(l_two, r_two, d_pair, message)
    if grid:
        l_far, r_far = swap(l_two, "d1"), swap(r_two, "d0")
    d_two, x_one = swap(d_pair, "zl"), swap(message, "zh")
    u_block = across(u_pair, u_two).reshape(-1, FF)
    if grid:
        l_far, r_far, d_two, x_one, u_block = tick(l_far, r_far, d_two, x_one, u_block)
        l_four, r_four = jnp.concatenate([l_two, l_far]), jnp.concatenate([r_two, r_far])
    else:
        d_two, x_one, u_block = tick(d_two, x_one, u_block)
        l_four, r_four = left, right
    d_block = across(d_pair, d_two).reshape(-1, D)
    x_pair = pair_up(message, x_one, "zh")
    l_four, r_four, u_block, d_block, x_pair = tick(l_four, r_four, u_block, d_block, x_pair)
    if grid:
        rights = [r_four, swap(r_four, "c")]
        lefts = [l_four, swap(l_four, "c")]
        u_near, d_near = swap(u_block, "d0"), swap(d_block, "d1")
    else:
        lefts, rights = [gather_whole(left)], [gather_whole(right)]
    x_two = swap(x_pair, "zl")
    rows = q_block.shape[0]
    qkv_w = (
        lefts + rights,
        weight_pieces("x", rows, half) + weight_pieces("y", rows, half, half),
    )
    out_w = (
        lefts + rights,
        weight_pieces("x", rows, part, 0, half) + weight_pieces("y", rows, part, part, half),
    )

    small = wide(small_part(rights, LEFT))
    table_t = jnp.transpose(small[:, : t_rows * HEADS].reshape(TABLE, HEADS))
    vector = small[:, t_rows * HEADS : t_rows * HEADS + v_len].reshape(-1)
    vec = jnp.pad(vector[: 10 * D].reshape(10, D), ((0, 6), (0, 0)))
    b1 = vector[10 * D :].reshape(FF // STEP, STEP)
    ids_a, ids_b, ids_fold = ids
    strip = lookup(table_t, ids_a)
    cols = jnp.transpose(strip[:, SIDE_A + 1, :QA].reshape(HEADS // 2, 2, QA), (0, 2, 1))
    cols = jnp.pad(cols, ((0, 0), (0, 0), (0, 126)))

    if grid:
        u_near, d_near, strip, cols = tick(u_near, d_near, strip, cols)
        u_pair, d_pair, table_t = tick(jnp.stack([u_block, u_near]), jnp.stack([d_block, d_near]), table_t)
        u_far, d_far = swap(u_pair, "d1"), swap(d_pair, "d0")
        ups, downs = [u_pair, None, swap(u_pair, "c"), None], [d_pair, None, swap(d_pair, "c"), None]
    bias_b = lookup(table_t, ids_b)
    if grid:
        x_two, bias_b = tick(x_two, bias_b)
    queries, keys, values, normed_all, normed_loc, x_all = project(pos, x_pair, x_two, x_loc, vec, *qkv_w)
    mixed, probs_a, probs_b = attend(counts, queries, keys, values, cols, strip, bias_b)
    if grid:
        ups[2], downs[2], u_far, d_far, mixed = tick(ups[2], downs[2], u_far, d_far, mixed)
        ups[1], downs[1] = u_far, d_far
        ups[3], downs[3] = swap(u_far, "c"), swap(d_far, "c")
    else:
        ups, downs = [gather_whole(u_block)], [gather_whole(d_block)]
    up_w = (ups, weight_pieces("x", rows, FF, pairs=True))
    down_w = (downs, weight_pieces("y", d_block.shape[0], D, pairs=True))
    plain, g_out, g_up, g_down = feed(
        pos, counts, mixed, x_loc, cot, vec, b1, (out_w, up_w, down_w), ("split", "x", "y"),
    )
    finals, (d_resid, d_mixed, gv_feed, gb_feed) = plain[:4], plain[4:]
    att = (queries, keys, values, probs_a, probs_b)
    grads = {}
    if grid:
        d_mixed, g_up, g_down, g_out = tick(d_mixed, g_up, g_down, g_out)
        u_core, d_core = swap(g_up[1], "c"), swap(g_down[1], "c")
        first = attend_back(pos[3:], 0, d_mixed, *att)
        u_core, d_core, first = tick(u_core, d_core, first)
        u_send, d_send, d_mixed, first = tick(
            far_part(g_up[0], u_core), far_part(g_down[0], d_core), d_mixed, first
        )
        u_far, d_far = swap(u_send, "d1"), swap(d_send, "d0")
    else:
        first = attend_back(pos[3:], 0, d_mixed, *att)
    second = attend_back(pos[3:], 1, d_mixed, *att)
    (local, keep, send, gv_back), g_qkv = back(
        pos, first[:3], second[:3], normed_all, normed_loc, x_all, x_loc, *qkv_w, g_out
    )
    folded = (first[3], second[3])
    if grid:
        u_far, d_far, send, g_qkv, gv_back, folded, keep = tick(u_far, d_far, send, g_qkv, gv_back, folded, keep)
        came = swap(send, "zl")
        q_core = swap(g_qkv[1], "c")
        u_send, d_send = near_part(g_up[0], u_core, u_far), near_part(g_down[0], d_core, d_far)
        u_near, d_near = swap(u_send, "d0"), swap(d_send, "d1")
        q_core, u_send, d_send = tick(q_core, u_send, d_send)
        l_own, r_own, l_core, r_core = g_qkv[0][:4], g_qkv[0][4:], q_core[:4], q_core[4:]
        l_send, r_send, folded, gv_back = tick(far_part(l_own, l_core), far_part(r_own, r_core), folded, gv_back)
        l_far, r_far = swap(l_send, "d1"), swap(r_send, "d0")
    else:
        came = swap(send, "zl")

    gt = gt_first = table_grad(*folded, ids_fold)
    gv = jnp.concatenate([gv_back[:4].reshape(-1), gv_feed[:6].reshape(-1), gb_feed.reshape(-1)])
    gt = jnp.transpose(gt[:HEADS]).reshape(devices, t_rows * HEADS)
    small_grad = jnp.concatenate([gt, gv.reshape(devices, v_len)], axis=1)
    small_len = (small_grad.shape[1] + 2047) // 2048 * 2048
    small_grad = jnp.pad(small_grad, ((0, 0), (0, small_len - small_grad.shape[1])))
    small_grad = small_grad.astype(BF16).reshape(n0, n1, nc, 2, 2, -1, 128)

    if grid:
        came, gt_first = tick(came, gt_first)
        came_send = (keep + wide(came[1])).astype(BF16)
        came_far = swap(came_send, "zh")
        u_near, d_near, came_send, small_grad = tick(u_near, d_near, came_send, small_grad)
        send, kept = split_blocks(
            zl, 48,
            [(g_up[0], 0), (u_core, 0), (u_far, 0), (u_near[None], 0)],
            [(g_down[0], 0), (d_core, 0), (d_far, 0), (d_near[None], 0)],
        )
        z_got = swap(send, "zl")
        small_grad = scatter_axis(small_grad, "d0").astype(BF16)
        l_far, r_far, send, small_grad = tick(l_far, r_far, send, small_grad)
        l_send, r_send = near_part(l_own, l_core, l_far), near_part(r_own, r_core, r_far)
        l_near, r_near = swap(l_send, "d0"), swap(r_send, "d1")
        small_grad = scatter_axis(small_grad, "d1").astype(BF16)
        l_near, r_near, z_got, small_grad = tick(l_near, r_near, z_got, small_grad)
        send, kept = half_blocks(zh, kept, z_got)
        z_far = swap(send, "zh")
        q_send, q_kept = split_blocks(
            zl, 24,
            [(g_qkv[0], 0), (q_core, 0), (l_far, 0), (l_near[None], 0)],
            [(g_qkv[0], 4), (q_core, 4), (r_far, 0), (r_near[None], 0)],
        )
        q_got = swap(q_send, "zl")
        small_grad = scatter_axis(small_grad, "c").astype(BF16).reshape(4, -1)
        d_rows = finish(d_resid, local, (came, came_far), x_loc, vec)
        q_got, z_far, small_grad, d_rows = tick(q_got, z_far, small_grad, d_rows)
        q_send, q_kept = half_blocks(zh, q_kept, q_got)
        grads["q"] = q_kept + wide(swap(q_send, "zh"))
        small_total = wide(lax.dynamic_index_in_dim(small_grad, place, 0, keepdims=False))
        for at in range(1, 4):
            outgoing = lax.dynamic_index_in_dim(small_grad, (place + at) % 4, 0, keepdims=False)
            small_total = small_total + wide(lax.ppermute(outgoing, ("zh", "zl"), shift_perm(4, at)))
        small_grad = small_total
        both = kept + wide(z_far)
        grads["up"] = both[: both.shape[0] // 2]
        grads["down"] = unside(both[both.shape[0] // 2 :])
    else:
        came_far = swap((keep + wide(came[1])).astype(BF16), "zh")
        for name, arrays in (("up", g_up), ("down", g_down)):
            grads[name] = sum_z(whole_grid_sum(arrays[0]))
        grads["q"] = sum_z(whole_grid_sum(jnp.concatenate(g_qkv, axis=2)))
        for axis in AXES:
            small_grad = scatter_axis(small_grad, axis)
            small_grad = small_grad if axis == "zl" else small_grad.astype(BF16)
        d_rows = finish(d_resid, local, (came, came_far), x_loc, vec)
    joint = grads["q"]
    grads["qkv"] = jnp.concatenate([joint[:, :half], joint[:, LEFT : LEFT + half]], axis=1)
    grads["out"] = jnp.concatenate([joint[:, half:LEFT], joint[:, LEFT + half :]], axis=1)
    small_grad = small_grad.reshape(-1)
    grads["table"] = small_grad[: t_rows * HEADS].reshape(t_rows, HEADS)
    grads["vector"] = small_grad[t_rows * HEADS : t_rows * HEADS + v_len]
    rows_all = (IMA * (PAT_A + 1) + IMB * (PAT_B + 1)) * (devices // 4)
    states = (
        ("qkv", qkv_weight, qkv_momentum, qkv_average),
        ("out", out_weight, out_momentum, out_average),
        ("up", up_weight, up_momentum, up_average),
        ("down", down_weight, down_momentum, down_average),
        ("table", table_weight, table_momentum, table_average),
        ("vector", vector_weight, vector_momentum, vector_average),
    )
    updated = []
    for (name, *state), rate in zip(states, STEP_RATES):
        updated += nesterov(*state, grads[name], rate / math.sqrt(rows_all))
    return (*finals, *d_rows, *updated)


def solution(mesh):
    dp, seq = mesh.devices.shape
    split = Mesh(mesh.devices.reshape(dp // 4, 2, 2, seq // 2, 2), AXES)
    dp_axes = ("d0", "d1", "c")
    rows = P(dp_axes, ("zh", "zl"), None)
    classes = P(dp_axes, None)
    shard = P(AXES, None)
    vec = P(AXES)
    return jax.shard_map(
        body,
        mesh=split,
        in_specs=(
            rows, classes, rows, classes, P(dp_axes), P(dp_axes), P(), P(), rows, classes, rows, classes,
            *([shard] * 15), *([vec] * 3),
        ),
        out_specs=(rows, classes, rows, classes, rows, classes, rows, classes, *([shard] * 15), *([vec] * 3)),
        check_vma=False,
    )
```

```python
import functools
import math

import jax
import jax.numpy as jnp
from jax import lax
from jax.experimental import pallas as pl
from jax.experimental.pallas import tpu as pltpu
from jax.sharding import Mesh
from jax.sharding import PartitionSpec as P

F32 = jnp.float32
BF16 = jnp.bfloat16
D = 768
HEADS = 12
HEAD_DIM = 64
FF = 3072
IMA = 1
IMB = 2
SIDE_A = 24
SIDE_B = 14
PAT_A = 576
PAT_B = 196
SLOT_B = 224
BLK_A = 144
BLK_B = 56
REAL_B = 49
TABLE = 2304
EPS = 1e-06
NEG = -1e30
ROOT_HALF = 0.7071067811865476
ROOT_TAU = 0.3989422804014327
STEP_RATES = (0.04, 1.6, 0.08, 0.02, 3.0, 0.6)

QA = 160
QB = 64
NQ = QA + IMB * QB
KA = 640
KB = 256
NK = KA + IMB * KB
BLOCK = BLK_A + IMB * QB
GROUPS = BLK_A // SIDE_A
CHUNK = 256
STEP = 1024
ROWS = 48
LEFT = 3 * D // 2 + D // 2
REACH = 29
SPAN = 2 * SIDE_A - 1
STRIP = 768
VMEM = 56 << 20
AXES = ("d0", "d1", "c", "zh", "zl")


def lookup_kernel(table_ref, index_ref, out_ref):
    rows, lanes = index_ref.shape
    heads, entries = table_ref.shape

    def eight_rows(at, carry):
        start = pl.multiple_of(at * 8, 8)
        for col in range(lanes // 128):
            ids = index_ref[pl.ds(start, 8), col * 128 : (col + 1) * 128]
            low = ids & 127
            high = ids >> 7
            found = [jnp.zeros((8, 128), F32) for _ in range(heads)]
            for chunk in range(entries // 128):
                here = high == chunk
                for head in range(heads):
                    row = jnp.broadcast_to(
                        table_ref[head : head + 1, chunk * 128 : (chunk + 1) * 128], (8, 128)
                    )
                    got = jnp.take_along_axis(row, low, axis=1)
                    found[head] = jnp.where(here, got, found[head])
            for head in range(heads):
                out_ref[head, pl.ds(start, 8), col * 128 : (col + 1) * 128] = found[head]
        return carry

    lax.fori_loop(0, rows // 8, eight_rows, 0)


def lookup(table_t, ids):
    return pl.pallas_call(
        lookup_kernel,
        out_shape=jax.ShapeDtypeStruct((table_t.shape[0],) + ids.shape, F32),
        compiler_params=params(48),
        cost_estimate=pl.CostEstimate(flops=20, bytes_accessed=2, transcendentals=0),
    )(table_t, ids)


def dot_last(left, right):
    return lax.dot_general(left, right, (((1,), (1,)), ((), ())), preferred_element_type=F32)


def dot_first(left, right):
    return lax.dot_general(left, right, (((0,), (0,)), ((), ())), preferred_element_type=F32)


def dot_plain(left, right):
    return jnp.dot(left, right, preferred_element_type=F32)


def unit_of(values):
    center = values - jnp.mean(values, axis=-1, keepdims=True)
    inv_std = lax.rsqrt(jnp.mean(center * center, axis=-1, keepdims=True) + EPS)
    return center * inv_std, inv_std


def norm_back(grad_in, unit_rows, inv_std, gain):
    d_unit = grad_in * gain
    return inv_std * (
        d_unit
        - jnp.mean(d_unit, axis=-1, keepdims=True)
        - unit_rows * jnp.mean(d_unit * unit_rows, axis=-1, keepdims=True)
    )


def col_sum(values):
    return jnp.sum(values, axis=0, keepdims=True)


class Piece:
    def __init__(self, blocks, rows, cols, order, other, col0, src=0, first=0, base=0):
        self.blocks, self.rows, self.cols = blocks, rows, cols
        self.order, self.other, self.col0 = order, other, col0
        self.src, self.first, self.base = src, first, base

    def part(self, ref, k):
        return ref.at[self.first + k, :, self.src : self.src + self.cols]

    def row(self, pos, k):
        if self.order is None:
            return 0
        near, far = k % 2, (k + self.base) // 2
        dy, dx = (near, far) if self.order == "x" else (far, near)
        y = 1 - pos[0] if dy else pos[0]
        x = 1 - pos[1] if dx else pos[1]
        c = 1 - pos[2] if self.other else pos[2]
        return pl.multiple_of(((y * 2 + x) * 2 + c) * self.rows, self.rows)


def copies_in(pos, pieces, refs, dest, sems):
    made = []
    for piece, ref in zip(pieces, refs):
        for k in range(piece.blocks):
            spot = dest.at[pl.ds(piece.row(pos, k), piece.rows), piece.col0 : piece.col0 + piece.cols]
            made.append(pltpu.make_async_copy(piece.part(ref, k), spot, sems.at[len(made)]))
    return made


def copies_out(pos, pieces, refs, source, sems):
    made = []
    for piece, ref in zip(pieces, refs):
        for k in range(piece.blocks):
            spot = source.at[pl.ds(piece.row(pos, k), piece.rows), piece.col0 : piece.col0 + piece.cols]
            made.append(pltpu.make_async_copy(spot, piece.part(ref, k), sems.at[len(made)]))
    return made


def piece_count(pieces):
    return sum(piece.blocks for piece in pieces)


def shift_perm(size, shift):
    return [(at, (at + shift) % size) for at in range(size)]


def swap(value, axis):
    return lax.ppermute(value, axis, [(0, 1), (1, 0)])


def hold(value, *after):
    return lax.optimization_barrier((value, *after))[0]


def small_grid():
    return lax.axis_size("d0") == 2 and lax.axis_size("d1") == 2 and lax.axis_size("c") == 2


def gather_axis(value, axis):
    size = lax.axis_size(axis)
    if size == 1:
        return value[None]
    if size > 4:
        return lax.all_gather(value, axis, axis=0)
    me = lax.axis_index(axis)
    pieces = [value] + [lax.ppermute(value, axis, shift_perm(size, s)) for s in range(1, size)]
    ordered = []
    for at in range(size):
        chosen = pieces[0]
        for s in range(1, size):
            chosen = jnp.where((me - at) % size == s, pieces[s], chosen)
        ordered.append(chosen)
    return jnp.stack(ordered)


def scatter_axis(value, axis):
    size = lax.axis_size(axis)
    if size == 1:
        return value[0].astype(F32)
    if size > 4:
        return lax.psum_scatter(value, axis, scatter_dimension=0).astype(F32)
    me = lax.axis_index(axis)
    total = lax.dynamic_index_in_dim(value, me, 0, keepdims=False).astype(F32)
    for s in range(1, size):
        outgoing = lax.dynamic_index_in_dim(value, (me + s) % size, 0, keepdims=False)
        total = total + lax.ppermute(outgoing.astype(BF16), axis, shift_perm(size, s)).astype(F32)
    return total


def halves_of(cols, order):
    if order == "split":
        return [("x", 0, cols // 2), ("y", cols // 2, cols)]
    return [(order, 0, cols)]


def gather_whole(block):
    rows, cols = block.shape
    for axis in ("c", "d1", "d0"):
        block = gather_axis(block, axis)
    return block.reshape(1, -1, cols)


def weight_pieces(turn, rows, cols, col0=0, src=0, pairs=False):
    if not small_grid():
        return [Piece(1, rows * lax.axis_size(AXES[:3]), cols, None, 0, col0, src)]
    if pairs:
        return [Piece(2, rows, cols, turn, other, col0, src, 0, far) for other in (0, 1) for far in (0, 2)]
    return [Piece(4, rows, cols, turn, other, col0, src) for other in (0, 1)]


def small_part(arrays, start):
    if not small_grid():
        tail = arrays[0][0, :, start:]
    else:
        tail = jnp.stack([each[..., start:] for each in arrays])
        tail = tail.reshape(2, 2, 2, *tail.shape[2:])
        for at, axis in enumerate(("c", "d0", "d1")):
            tail = jnp.where(lax.axis_index(axis) == 0, tail, jnp.flip(tail, at))
        tail = jnp.moveaxis(tail, 0, 2)
    return tail.reshape(lax.axis_size(AXES), -1)


def grad_pieces(rows, cols, order):
    if not small_grid():
        return [Piece(1, rows, stop - start, None, 0, start) for _, start, stop in halves_of(cols, order)]
    return [
        Piece(4, rows // 8, stop - start, turn, other, start)
        for turn, start, stop in halves_of(cols, order)
        for other in (0, 1)
    ]


def wide(value):
    return value.astype(F32)


def far_part(own, core):
    return (wide(own[2:]) + wide(core[2:])).astype(BF16)


def near_part(own, core, far):
    return (wide(own[1]) + wide(core[1]) + wide(far[1])).astype(BF16)


def side(rows):
    count = rows.shape[0] // 4
    return jnp.concatenate([rows[at * count : (at + 1) * count] for at in range(4)], axis=1)


def unside(wide_rows):
    width = wide_rows.shape[1] // 4
    return jnp.concatenate([wide_rows[:, at * width : (at + 1) * width] for at in range(4)], axis=0)


def beside(up, down):
    count = down.shape[1] // 4
    laid = jnp.concatenate([down[:, at * count : (at + 1) * count] for at in range(4)], axis=2)
    return jnp.concatenate([up, laid], axis=1)


def block_sum(own, core, far, near):
    return wide(own[0]) + wide(core[0]) + wide(far[0]) + wide(near)


def whole_grid_sum(whole):
    value = whole[0]
    sizes = [lax.axis_size(axis) for axis in AXES]
    value = value.reshape(*sizes[:3], -1, value.shape[-1])
    for axis in AXES[:3]:
        value = scatter_axis(value, axis)
        if axis != "c":
            value = value.astype(BF16)
    return value


def project_kernel(pieces, pos_ref, pair_ref, two_ref, xl_ref, vec_ref, *refs):
    w_refs = refs[: len(pieces)]
    q_ref, k_ref, v_ref, na_ref, nl_ref, xa_ref, w, sems = refs[len(pieces) :]
    copies = copies_in([pos_ref[at] for at in range(3)], pieces, w_refs, w, sems)
    for copy in copies:
        copy.start()
    for at in range(4):
        mine = pos_ref[3] % 2 == at % 2
        rows = jnp.where(mine, pair_ref[at // 2], two_ref[at // 2])
        xa_ref[at * BLK_A : (at + 1) * BLK_A] = rows[:BLK_A]
        for i in range(IMB):
            start = KA + i * KB + at * QB
            xa_ref[start : start + QB] = rows[BLK_A + i * QB : BLK_A + (i + 1) * QB]
    xa_ref[PAT_A : PAT_A + 16] = xl_ref[BLK_A:QA]
    xa_ref[PAT_A + 16 : KA] = jnp.zeros((KA - PAT_A - 16, D), BF16)
    gain, shift = vec_ref[0:1], vec_ref[1:2]
    nl_ref[...] = (unit_of(wide(xl_ref[...]))[0] * gain + shift).astype(BF16)

    @pl.loop(0, NK // 128)
    def _(at):
        rows = pl.ds(pl.multiple_of(at * 128, 128), 128)
        na_ref[rows] = (unit_of(wide(xa_ref[rows]))[0] * gain + shift).astype(BF16)

    for copy in copies:
        copy.wait()
    queries = dot_plain(nl_ref[...], w[:, :D]) + vec_ref[2:3]
    q_ref[...] = (queries * (1.0 / math.sqrt(HEAD_DIM))).astype(BF16)

    @pl.loop(0, NK // 384)
    def _(at):
        rows = pl.ds(pl.multiple_of(at * 384, 128), 384)
        k_ref[rows] = dot_plain(na_ref[rows], w[:, D : 2 * D]).astype(BF16)
        v_ref[rows] = (dot_plain(na_ref[rows], w[:, 2 * D :]) + vec_ref[3:4]).astype(BF16)


VSPEC = pl.BlockSpec(memory_space=pltpu.VMEM)
SSPEC = pl.BlockSpec(memory_space=pltpu.SMEM)
ANYSPEC = pl.BlockSpec(memory_space=pl.ANY)


def params(size=56):
    return pltpu.CompilerParams(vmem_limit_bytes=size << 20)


def cost(flops, moved):
    return pl.CostEstimate(flops=int(flops), bytes_accessed=int(moved), transcendentals=0)


def project(pos, x_pair, x_two, x_loc, vec, arrays, pieces):
    return pl.pallas_call(
        functools.partial(project_kernel, pieces),
        in_specs=[SSPEC] + [VSPEC] * 4 + [ANYSPEC] * len(arrays),
        out_specs=[VSPEC] * 6,
        out_shape=[
            jax.ShapeDtypeStruct((NQ, D), BF16),
            jax.ShapeDtypeStruct((NK, D), BF16),
            jax.ShapeDtypeStruct((NK, D), BF16),
            jax.ShapeDtypeStruct((NK, D), BF16),
            jax.ShapeDtypeStruct((NQ, D), BF16),
            jax.ShapeDtypeStruct((NK, D), BF16),
        ],
        scratch_shapes=[pltpu.VMEM((D, 3 * D), BF16), pltpu.SemaphoreType.DMA((piece_count(pieces),))],
        compiler_params=params(),
        cost_estimate=cost(2 * D * D * (NQ + 2 * NK), 12e6),
        name="project",
    )(pos, x_pair, x_two, x_loc, vec, *arrays)


def softmax_rows(scores):
    top = jnp.max(scores, axis=-1, keepdims=True)
    grown = jnp.exp(scores - top)
    return grown * (1.0 / jnp.sum(grown, axis=-1, keepdims=True))


def attend_kernel(cnt_ref, q_ref, k_ref, v_ref, col_ref, strip_ref, bias_ref, o_ref, pa_ref, pb_ref, sa, sb):
    lane = lax.broadcasted_iota(jnp.int32, (1, 128), 1)
    lane_a = lax.broadcasted_iota(jnp.int32, (1, KA), 1)
    lane_b = lax.broadcasted_iota(jnp.int32, (1, KB), 1)
    live_a = ((lane_a < PAT_A) & (lane_a < cnt_ref[0])) | (lane_a == PAT_A)
    spot = lane_b % QB
    live_b = [
        ((spot < REAL_B) & (lane_b // QB * REAL_B + spot < cnt_ref[1 + i])) | (lane_b == BLK_B)
        for i in range(IMB)
    ]
    for t in range(2):
        mine = (lane < HEAD_DIM) if t == 0 else (lane >= HEAD_DIM)
        queries = jnp.where(mine, q_ref[...], jnp.zeros((), BF16))
        sa[t] = dot_last(queries[:QA], k_ref[:KA])
        for i in range(IMB):
            q_at, k_at = QA + i * QB, KA + i * KB
            sb[t, i] = dot_last(queries[q_at : q_at + QB], k_ref[k_at : k_at + KB])
    for t in range(2):
        strip = strip_ref[t]
        for r in range(GROUPS + 1):
            start, count = r * SIDE_A, SIDE_A
            if r < GROUPS:
                off = (GROUPS - 1 - r) * SIDE_A
                bias = strip[:SIDE_A] if off == 0 else pltpu.roll(strip[:SIDE_A], STRIP - off, 1)
                bias = bias[:, :KA]
                bias = jnp.where(lane_a == PAT_A, col_ref[0, start : start + count, t : t + 1], bias)
            else:
                count = QA - start
                bias = jnp.concatenate([strip[SIDE_A:, :KA]] * 2, axis=0)
            probs = softmax_rows(jnp.where(live_a, sa[t, start : start + count] + bias, NEG))
            pa_ref[t, start : start + count] = probs
        for i in range(IMB):
            for r in range(2):
                rows = slice(r * 32, (r + 1) * 32)
                probs = softmax_rows(jnp.where(live_b[i], sb[t, i, rows] + bias_ref[t, rows], NEG))
                pb_ref[t, i, rows] = probs
    mixed = []
    for t in range(2):
        outs = [dot_plain(pa_ref[t].astype(BF16), v_ref[:KA])]
        for i in range(IMB):
            k_at = KA + i * KB
            outs.append(dot_plain(pb_ref[t, i].astype(BF16), v_ref[k_at : k_at + KB]))
        mixed.append(jnp.concatenate(outs, axis=0))
    o_ref[...] = jnp.where(lane < HEAD_DIM, mixed[0], mixed[1]).astype(BF16)


def attend(counts, queries, keys, values, cols, strip, bias_b):
    pairs = HEADS // 2
    return pl.pallas_call(
        attend_kernel,
        grid=(pairs,),
        in_specs=[
            SSPEC,
            pl.BlockSpec((NQ, 128), lambda p: (0, p)),
            pl.BlockSpec((NK, 128), lambda p: (0, p)),
            pl.BlockSpec((NK, 128), lambda p: (0, p)),
            pl.BlockSpec((1, QA, 128), lambda p: (p, 0, 0)),
        ]
        + [pl.BlockSpec((2, 32, STRIP), lambda p: (p, 0, 0)), pl.BlockSpec((2, QB, KB), lambda p: (p, 0, 0))],
        out_specs=[
            pl.BlockSpec((NQ, 128), lambda p: (0, p)),
            pl.BlockSpec((2, QA, KA), lambda p: (p, 0, 0)),
            pl.BlockSpec((2, IMB, QB, KB), lambda p: (p, 0, 0, 0)),
        ],
        out_shape=[
            jax.ShapeDtypeStruct((NQ, D), BF16),
            jax.ShapeDtypeStruct((HEADS, QA, KA), F32),
            jax.ShapeDtypeStruct((HEADS, IMB, QB, KB), F32),
        ],
        scratch_shapes=[pltpu.VMEM((2, QA, KA), F32), pltpu.VMEM((2, IMB, QB, KB), F32)],
        compiler_params=params(),
        cost_estimate=cost(4 * HEADS * 128 * (QA * KA + IMB * QB * KB), 30e6),
        name="attend",
    )(counts, queries, keys, values, cols, strip, bias_b)


def orders_b(odd):
    new_row = lax.broadcasted_iota(jnp.int32, (QB, QB), 0)
    old_row = lax.broadcasted_iota(jnp.int32, (QB, QB), 1)
    inside = new_row % 8
    slot = (new_row // 8 - odd) * 7 + 6 - inside
    order = (inside < 7) & (slot >= 0) & (slot < REAL_B) & (slot == old_row) & (new_row // 8 - odd >= 0)
    old_col = lax.broadcasted_iota(jnp.int32, (KB, KB), 0)
    new_col = lax.broadcasted_iota(jnp.int32, (KB, KB), 1)
    spread = (new_col < PAT_B) & (old_col == new_col // REAL_B * QB + new_col % REAL_B)
    return jnp.where(order, 1.0, 0.0).astype(BF16), jnp.where(spread, 1.0, 0.0).astype(BF16)


def strips_b(laid):
    pieces = []
    for r in range(4):
        off = (3 - r) * SIDE_B
        piece = laid[r * 16 : (r + 1) * 16]
        pieces.append(piece if off == 0 else pltpu.roll(piece, off, 1))
    return pieces


def fold_strip(strip, side):
    even = lax.broadcasted_iota(jnp.int32, (1, strip.shape[1]), 1) // side % 2 == 0
    return [
        pltpu.roll(part, 0, 1, stride=1, stride_axis=0)
        for part in (jnp.where(even, strip, 0.0), jnp.where(even, 0.0, strip))
    ]


def fold_strip_b(strip):
    even = lax.broadcasted_iota(jnp.int32, (1, KB), 1) // SIDE_B % 2 == 0
    return [
        (
            pltpu.roll(part[:8], 7, 1, stride=1, stride_axis=0),
            pltpu.roll(part[8:], 0, 1, stride=1, stride_axis=0),
        )
        for part in (jnp.where(even, strip, 0.0), jnp.where(even, 0.0, strip))
    ]


def row_weights(first):
    row = lax.broadcasted_iota(jnp.int32, (NQ, 1), 0)
    is_class = (row == BLK_A) | ((row >= QA) & ((row - QA) % QB == BLK_B))
    return jnp.where(is_class, first, 1.0)


def attend_back_kernel(place_ref, do_ref, q_ref, k_ref, v_ref, pa_ref, pb_ref, dq_ref, dk_ref, dv_ref, g_ref):
    lane = lax.broadcasted_iota(jnp.int32, (1, 128), 1)
    lane_a = lax.broadcasted_iota(jnp.int32, (1, KA), 1)
    low = lane < HEAD_DIM
    place = place_ref[0]
    odd = place % 2
    weight = row_weights(jnp.where(place == 0, 1.0, 0.0))
    new_row = lax.broadcasted_iota(jnp.int32, (BLK_A, QA), 0)
    old_row = lax.broadcasted_iota(jnp.int32, (BLK_A, QA), 1)
    turned = old_row == new_row // SIDE_A * SIDE_A + (SIDE_A - 1 - new_row % SIDE_A)
    turned = jnp.where(turned, 1.0, 0.0).astype(BF16)
    order, spread = orders_b(odd)
    pick_a = lax.broadcasted_iota(jnp.int32, (8, KA), 1) == PAT_A
    pick_a = jnp.where(pick_a, 1.0, 0.0).astype(BF16)
    pick_b = lax.broadcasted_iota(jnp.int32, (8, KB), 1) == BLK_B
    pick_b = jnp.where(pick_b, 1.0, 0.0).astype(BF16)
    lane_q = lax.broadcasted_iota(jnp.int32, (1, QA), 1)
    d_out = do_ref[...]
    d_out_w = (wide(d_out) * weight).astype(BF16)
    starts = {0: QA} | {QA + i * QB: QB for i in range(IMB)}
    q_turned = {at: jnp.transpose(wide(q_ref[at : at + size])).astype(BF16) for at, size in starts.items()}
    d_turned = {at: jnp.transpose(wide(d_out_w[at : at + size])).astype(BF16) for at, size in starts.items()}
    dq_parts, dk_parts, dv_parts = [], [], []
    for t in range(2):
        mine = low if t == 0 else jnp.logical_not(low)
        d_mine = jnp.where(mine, d_out, jnp.zeros((), BF16))

        def one(q_at, q_len, k_at, k_len, probs):
            d_probs = dot_last(d_mine[q_at : q_at + q_len], v_ref[k_at : k_at + k_len])
            delta = jnp.sum(probs * d_probs, axis=-1, keepdims=True)
            d_wide = probs * (d_probs - delta)
            d_low = d_wide.astype(BF16)
            d_query = dot_plain(d_low, k_ref[k_at : k_at + k_len])
            d_w = (wide(d_low) * weight[q_at : q_at + q_len]).astype(BF16)
            rows = slice(t * HEAD_DIM, (t + 1) * HEAD_DIM)
            d_key = dot_plain(q_turned[q_at][rows], d_w)
            d_value = dot_plain(d_turned[q_at][rows], probs.astype(BF16))
            return d_query, d_key, d_value, d_w

        d_query, d_key, d_value, d_w = one(0, QA, 0, KA, pa_ref[t])
        dqs, dks, dvs = [d_query], [d_key], [d_value]
        flipped = jnp.where(lane_a < PAT_A, dot_plain(turned, d_w), 0.0)
        flipped = jnp.concatenate([flipped, jnp.zeros((BLK_A, STRIP - KA), F32)], axis=1)
        strip = None
        for r in range(GROUPS):
            off = (GROUPS - 1 - r) * SIDE_A
            piece = flipped[r * SIDE_A : (r + 1) * SIDE_A]
            piece = piece if off == 0 else pltpu.roll(piece, off, 1)
            strip = piece if strip is None else strip + piece
        fold = [col_sum(part) for part in fold_strip(strip, SIDE_A)]
        row_a = wide(d_w[BLK_A : BLK_A + 16])[:1]
        col_a = jnp.where(lane_q < BLK_A, dot_last(pick_a, d_w)[:1], 0.0)
        moved, row_b, col_b = None, None, None
        for i in range(IMB):
            d_query, d_key, d_value, d_w = one(QA + i * QB, QB, KA + i * KB, KB, pb_ref[t, i])
            dqs.append(d_query)
            dks.append(d_key)
            dvs.append(d_value)
            laid = dot_plain(dot_plain(order, d_w).astype(BF16), spread)
            row = wide(d_w[BLK_B - 8 : BLK_B + 8])[8:9]
            col = jnp.where(lane_q[:, :QB] < BLK_B, dot_last(pick_b, d_w)[:1], 0.0)
            moved = laid if i == 0 else moved + laid
            row_b = row if i == 0 else row_b + row
            col_b = col if i == 0 else col_b + col
        strip = None
        for piece in strips_b(moved):
            strip = piece if strip is None else strip + piece
        fold_b = [col_sum(left + right) for left, right in fold_strip_b(strip)]
        g_ref[t, 0:1] = fold[0]
        g_ref[t, 1:2] = fold[1]
        g_ref[t, 2:3, 0:KB] = fold_b[0]
        g_ref[t, 2:3, KB : 2 * KB] = fold_b[1]
        g_ref[t, 2:3, 2 * KB :] = row_b
        g_ref[t, 3:4, 0:KA] = row_a
        g_ref[t, 3:4, KA:] = jnp.concatenate([col_b, jnp.zeros((1, 128 - QB), F32)], axis=1)
        g_ref[t, 4:5, 0:256] = jnp.concatenate([col_a, jnp.zeros((1, 256 - QA), F32)], axis=1)
        g_ref[t, 4:5, 256:] = jnp.zeros((1, STRIP - 256), F32)
        g_ref[t, 5:8] = jnp.zeros((3, STRIP), F32)
        dq_parts.append(jnp.concatenate(dqs, axis=0))
        dk_parts.append(jnp.concatenate(dks, axis=1))
        dv_parts.append(jnp.concatenate(dvs, axis=1))
    d_query = jnp.where(low, dq_parts[0], dq_parts[1]).astype(BF16)
    dq_ref[...] = (wide(d_query) * (1.0 / math.sqrt(HEAD_DIM))).astype(BF16)
    dk_ref[...] = jnp.transpose(jnp.concatenate(dk_parts, axis=0)).astype(BF16)
    dv_ref[...] = jnp.transpose(jnp.concatenate(dv_parts, axis=0)).astype(BF16)


def attend_back(place, part, d_mixed, queries, keys, values, probs_a, probs_b):
    pairs = HEADS // 4
    base = part * pairs
    return pl.pallas_call(
        attend_back_kernel,
        grid=(pairs,),
        in_specs=[
            SSPEC,
            pl.BlockSpec((NQ, 128), lambda p: (0, base + p)),
            pl.BlockSpec((NQ, 128), lambda p: (0, base + p)),
            pl.BlockSpec((NK, 128), lambda p: (0, base + p)),
            pl.BlockSpec((NK, 128), lambda p: (0, base + p)),
            pl.BlockSpec((2, QA, KA), lambda p: (base + p, 0, 0)),
            pl.BlockSpec((2, IMB, QB, KB), lambda p: (base + p, 0, 0, 0)),
        ],
        out_specs=[
            pl.BlockSpec((NQ, 128), lambda p: (0, p)),
            pl.BlockSpec((NK, 128), lambda p: (0, p)),
            pl.BlockSpec((NK, 128), lambda p: (0, p)),
            pl.BlockSpec((2, 8, STRIP), lambda p: (p, 0, 0)),
        ],
        out_shape=[
            jax.ShapeDtypeStruct((NQ, D // 2), BF16),
            jax.ShapeDtypeStruct((NK, D // 2), BF16),
            jax.ShapeDtypeStruct((NK, D // 2), BF16),
            jax.ShapeDtypeStruct((HEADS // 2, 8, STRIP), F32),
        ],
        compiler_params=params(24),
        cost_estimate=cost(6 * HEADS * 128 * (QA * KA + IMB * QB * KB), 15e6),
        name="attend_back",
    )(place, d_mixed, queries, keys, values, probs_a, probs_b)


def table_kernel(g0_ref, g1_ref, ids_ref, out_ref):
    rows = lax.broadcasted_iota(jnp.int32, (CHUNK, STRIP), 0)
    split = []
    for at in range(5):
        values = jnp.concatenate([g0_ref[:, at], g1_ref[:, at]], axis=0)
        top = values.astype(BF16)
        rest = values - wide(top)
        middle = rest.astype(BF16)
        bottom = (rest - wide(middle)).astype(BF16)
        pad = jnp.zeros((4, STRIP), F32)
        stacked = []
        for part in (top, middle, bottom):
            stacked += [wide(part), pad]
        split.append(jnp.concatenate(stacked, axis=0).astype(BF16))

    for step in range(TABLE // CHUNK):
        total = jnp.zeros((48, CHUNK), F32)
        for at in range(5):
            hot = jnp.where(rows + step * CHUNK == ids_ref[at : at + 1], 1.0, 0.0).astype(BF16)
            total = total + dot_last(split[at], hot)
        out_ref[:, step * CHUNK : (step + 1) * CHUNK] = total[:16] + total[16:32] + total[32:]


def table_grad(first, second, ids):
    return pl.pallas_call(
        table_kernel,
        in_specs=[VSPEC] * 3,
        out_specs=VSPEC,
        out_shape=jax.ShapeDtypeStruct((16, TABLE), F32),
        compiler_params=params(),
        cost_estimate=cost(2 * 48 * TABLE * 5 * STRIP, 2e6),
        name="table_grad",
    )(first, second, ids)


def flip_rows(count, size):
    new_row = lax.broadcasted_iota(jnp.int32, (count, count), 0)
    old_row = lax.broadcasted_iota(jnp.int32, (count, count), 1)
    turned = old_row == new_row // size * size + (size - 1 - new_row % size)
    return jnp.where(turned, 1.0, 0.0).astype(BF16)


def ids_kernel(place_ref, ia_ref, ib_ref, a_ref, b_ref, f_ref):
    place = place_ref[0]

    def through(matrix, ids):
        high = (ids // 64).astype(F32).astype(BF16)
        low = (ids % 64).astype(F32).astype(BF16)
        return 64.0 * dot_plain(matrix, high) + dot_plain(matrix, low)

    def column(ids, at):
        pick = lax.broadcasted_iota(jnp.int32, (8, ids.shape[1]), 1) == at
        pick = jnp.where(pick, 1.0, 0.0).astype(BF16)
        high = (ids // 64).astype(F32).astype(BF16)
        low = (ids % 64).astype(F32).astype(BF16)
        return (64.0 * dot_last(pick, high) + dot_last(pick, low))[:1].astype(jnp.int32)

    def fill(row, width):
        return jnp.concatenate([row, jnp.zeros((row.shape[0], width - row.shape[1]), jnp.int32)], axis=1)

    top = (GROUPS - 1) * SIDE_A
    for at in range(4):

        @pl.when(place == at)
        def _():
            rows_a = ia_ref[1 + BLK_A * at : 1 + BLK_A * (at + 1), :]
            last, first = rows_a[top:, 1 : 1 + top], rows_a[:SIDE_A, 1:]
            a_ref[:SIDE_A] = fill(jnp.concatenate([last, first], axis=1), STRIP)
            f_ref[4:5] = fill(column(rows_a, 0), STRIP)
            rows_b = jnp.concatenate(
                [ib_ref[1 + BLK_B * at : 1 + BLK_B * (at + 1), :], ib_ref[0:1, :], jnp.zeros((7, SLOT_B + 1), jnp.int32)],
                axis=0,
            )
            parts = []
            for k in range(4):
                parts += [rows_b[:, 1 + k * BLK_B : 1 + (k + 1) * BLK_B], rows_b[:, :1], jnp.zeros((QB, 7), jnp.int32)]
            b_ref[...] = jnp.concatenate(parts, axis=1)
            f_ref[3:4, KA:] = fill(column(rows_b, 0)[:, :BLK_B], 128)

    class_row = jnp.concatenate([ia_ref[0:1, 1:], ia_ref[0:1, :1]], axis=1)
    a_ref[SIDE_A : SIDE_A + 1] = fill(class_row, STRIP)
    a_ref[SIDE_A + 1 : SIDE_A + 2] = f_ref[4:5]
    a_ref[SIDE_A + 2 :] = jnp.zeros((6, STRIP), jnp.int32)
    f_ref[3:4, :KA] = fill(class_row, KA)
    f_ref[2:3, 2 * KB :] = b_ref[BLK_B : BLK_B + 1]
    f_ref[5:8] = jnp.zeros((3, STRIP), jnp.int32)
    turned = through(flip_rows(SIDE_A, SIDE_A), a_ref[:SIDE_A])
    lane = lax.broadcasted_iota(jnp.int32, (1, STRIP), 1)
    turned = jnp.where(lane < REACH * SIDE_A, turned, 0.0)
    for at, part in enumerate(fold_strip(turned, SIDE_A)):
        f_ref[at : at + 1] = jnp.max(part, axis=0, keepdims=True).astype(jnp.int32)
    order, spread = orders_b(place % 2)
    laid = through(order, b_ref[...]).astype(jnp.int32)
    high = (laid // 64).astype(F32).astype(BF16)
    low = (laid % 64).astype(F32).astype(BF16)
    laid = 64.0 * dot_plain(high, spread) + dot_plain(low, spread)
    strip = None
    for piece in strips_b(laid):
        strip = piece if strip is None else jnp.maximum(strip, piece)
    for at, (left, right) in enumerate(fold_strip_b(strip)):
        found = jnp.max(jnp.maximum(left, right), axis=0, keepdims=True)
        f_ref[2:3, at * KB : (at + 1) * KB] = found.astype(jnp.int32)


def all_ids(pos, index_a, index_b):
    return pl.pallas_call(
        ids_kernel,
        in_specs=[SSPEC, VSPEC, VSPEC],
        out_specs=[VSPEC] * 3,
        out_shape=[jax.ShapeDtypeStruct(shape, jnp.int32) for shape in ((32, STRIP), (QB, KB), (8, STRIP))],
        compiler_params=params(),
        cost_estimate=cost(1e8, 6e6),
        name="ids",
    )(pos[3:], index_a, index_b)


def feed_kernel(meta, pos_ref, cnt_ref, mixed_ref, x_ref, cot_ref, vec_ref, b1_ref, *refs):
    (p_out, p_up, p_down), (q_out, q_up, q_down) = meta
    refs = list(refs)

    def take(count):
        taken = refs[:count]
        del refs[:count]
        return taken

    wo_refs, wu_refs, wd_refs = take(len(p_out)), take(len(p_up)), take(len(p_down))
    fa_ref, fca_ref, fb_ref, fcb_ref, dres_ref, dmix_ref, gv_ref, gb_ref = take(8)
    go_refs, gu_refs, gd_refs = take(len(q_out)), take(len(q_up)), take(len(q_down))
    wo, wu, wd, go, gu, gd, norm, gelu, slope, d_hid, dsec, dsec_w, sem_o, sem_u, sem_d = refs
    pos = [pos_ref[at] for at in range(3)]
    loads = [copies_in(pos, *each) for each in ((p_out, wo_refs, wo, sem_o), (p_up, wu_refs, wu, sem_u), (p_down, wd_refs, wd, sem_d))]
    for group in loads:
        for copy in group:
            copy.start()

    def piece(at):
        return vec_ref[at : at + 1]

    place = pos_ref[3]
    weight = row_weights(jnp.where(place == 0, 1.0, 0.0))
    row = lax.broadcasted_iota(jnp.int32, (NQ, 1), 0)
    slot = (row - QA) % QB
    count_b = jnp.where(row < QA + QB, cnt_ref[1], cnt_ref[2])
    live_a = ((row < BLK_A) & (place * BLK_A + row < cnt_ref[0])) | (row == BLK_A)
    live_b = ((slot < REAL_B) & (place * REAL_B + slot < count_b)) | (slot == BLK_B)
    live = jnp.where(((row < QA) & live_a) | ((row >= QA) & live_b), 1.0, 0.0)

    for copy in loads[0]:
        copy.wait()
    branch = dot_plain(mixed_ref[...], wo[...]) + piece(4)
    resid = wide(x_ref[...]) + piece(5) * branch
    unit, inv_std = unit_of(resid)
    norm[...] = (unit * piece(6) + piece(7)).astype(BF16)
    for copy in loads[1]:
        copy.wait()

    @pl.loop(0, FF // STEP)
    def _(at):
        cols = pl.ds(pl.multiple_of(at * STEP, STEP), STEP)
        hidden = dot_plain(norm[...], wu[:, cols]) + b1_ref[pl.ds(at, 1), :]
        gate = 0.5 * (1.0 + lax.erf(hidden * ROOT_HALF))
        gelu[:, cols] = (hidden * gate).astype(BF16)
        slope[:, cols] = gate + hidden * ROOT_TAU * jnp.exp(-0.5 * hidden * hidden)

    for copy in loads[2]:
        copy.wait()
    second = dot_plain(gelu[...], wd[...]) + piece(8)
    final = resid + piece(9) * second
    fa_ref[0] = final[:BLK_A]
    fca_ref[...] = final[BLK_A : BLK_A + 1]
    d_final = wide(cot_ref[...]) * live
    for i in range(IMB):
        fb_ref[i] = final[QA + i * QB : QA + i * QB + BLK_B]
        fcb_ref[i : i + 1] = final[QA + i * QB + BLK_B : QA + i * QB + BLK_B + 1]
    gv_ref[5:6] = col_sum(d_final * second * weight)
    d_second = (piece(9) * d_final).astype(BF16)
    dsec[...] = d_second
    d_second_w = wide(d_second) * weight
    gv_ref[4:5] = col_sum(d_second_w)
    dsec_w[...] = d_second_w.astype(BF16)

    @pl.loop(0, FF // STEP)
    def _(at):
        cols = pl.ds(pl.multiple_of(at * STEP, STEP), STEP)
        d_gelu = dot_last(dsec[...], wd[cols, :])
        d_hid[:, cols] = (d_gelu * slope[:, cols]).astype(BF16)
        gd[cols, :] = dot_first(gelu[:, cols], dsec_w[...]).astype(BF16)

    stores = copies_out(pos, q_down, gd_refs, gd, sem_d)
    for copy in stores:
        copy.start()

    @pl.loop(0, FF // STEP)
    def _(at):
        cols = pl.ds(pl.multiple_of(at * STEP, STEP), STEP)
        d_hidden_w = wide(d_hid[:, cols]) * weight
        gb_ref[pl.ds(at, 1), :] = col_sum(d_hidden_w)
        gu[:, cols] = dot_first(norm[...], d_hidden_w.astype(BF16)).astype(BF16)

    more = copies_out(pos, q_up, gu_refs, gu, sem_u)
    for copy in more:
        copy.start()
    stores += more
    d_normed = dot_last(d_hid[...], wu[...])
    d_normed_w = d_normed * weight
    gv_ref[2:3] = col_sum(d_normed_w * unit)
    gv_ref[3:4] = col_sum(d_normed_w)
    d_resid = d_final + norm_back(d_normed, unit, inv_std, piece(6))
    dres_ref[...] = d_resid
    gv_ref[1:2] = col_sum(d_resid * branch * weight)
    d_branch = (piece(5) * d_resid).astype(BF16)
    d_branch_w = wide(d_branch) * weight
    gv_ref[0:1] = col_sum(d_branch_w)
    gv_ref[6:8] = jnp.zeros((2, D), F32)
    go[...] = dot_first(mixed_ref[...], d_branch_w.astype(BF16)).astype(BF16)
    last = copies_out(pos, q_out, go_refs, go, sem_o)
    for copy in last:
        copy.start()
    dmix_ref[...] = dot_last(d_branch, wo[...]).astype(BF16)
    for copy in stores + last:
        copy.wait()


def feed(pos, counts, mixed, x_loc, cot, vec, b1, weights, orders):
    (a_out, p_out), (a_up, p_up), (a_down, p_down) = weights
    q_out = grad_pieces(D, D, orders[0])
    q_up = grad_pieces(D, FF, orders[1])
    q_down = grad_pieces(FF, D, orders[2])
    grads = q_out + q_up + q_down
    shapes = [
        jax.ShapeDtypeStruct((IMA, BLK_A, D), F32),
        jax.ShapeDtypeStruct((IMA, D), F32),
        jax.ShapeDtypeStruct((IMB, BLK_B, D), F32),
        jax.ShapeDtypeStruct((IMB, D), F32),
        jax.ShapeDtypeStruct((NQ, D), F32),
        jax.ShapeDtypeStruct((NQ, D), BF16),
        jax.ShapeDtypeStruct((8, D), F32),
        jax.ShapeDtypeStruct((FF // STEP, STEP), F32),
    ]
    outs = pl.pallas_call(
        functools.partial(feed_kernel, ((p_out, p_up, p_down), (q_out, q_up, q_down))),
        in_specs=[SSPEC] * 2 + [VSPEC] * 5 + [ANYSPEC] * (len(a_out) + len(a_up) + len(a_down)),
        out_specs=[VSPEC] * 8 + [ANYSPEC] * len(grads),
        out_shape=shapes + [jax.ShapeDtypeStruct((p.blocks, p.rows, p.cols), BF16) for p in grads],
        scratch_shapes=[
            pltpu.VMEM((D, D), BF16),
            pltpu.VMEM((D, FF), BF16),
            pltpu.VMEM((FF, D), BF16),
            pltpu.VMEM((D, D), BF16),
            pltpu.VMEM((D, FF), BF16),
            pltpu.VMEM((FF, D), BF16),
            pltpu.VMEM((NQ, D), BF16),
            pltpu.VMEM((NQ, FF), BF16),
            pltpu.VMEM((NQ, FF), F32),
            pltpu.VMEM((NQ, FF), BF16),
            pltpu.VMEM((NQ, D), BF16),
            pltpu.VMEM((NQ, D), BF16),
            pltpu.SemaphoreType.DMA((max(piece_count(p_out), piece_count(q_out)),)),
            pltpu.SemaphoreType.DMA((max(piece_count(p_up), piece_count(q_up)),)),
            pltpu.SemaphoreType.DMA((max(piece_count(p_down), piece_count(q_down)),)),
        ],
        compiler_params=params(48),
        cost_estimate=cost(6 * NQ * D * (D + 2 * FF), 30e6),
        name="feed",
    )(pos, counts, mixed, x_loc, cot, vec, b1, *a_out, *a_up, *a_down)
    plain, rest = outs[:8], list(outs[8:])
    g_out = [rest.pop(0) for _ in q_out]
    g_up = [rest.pop(0) for _ in q_up]
    g_down = [rest.pop(0) for _ in q_down]
    return plain, g_out, g_up, g_down


def back_kernel(p_qkv, q_qkv, q_out, pos_ref, dq0_ref, dk0_ref, dv0_ref, dq1_ref, dk1_ref, dv1_ref, na_ref, nl_ref, xa_ref, xl_ref, *refs):
    refs = list(refs)

    def take(count):
        taken = refs[:count]
        del refs[:count]
        return taken

    w_refs, o_refs = take(len(p_qkv)), take(len(q_out))
    local_ref, keep_ref, send_ref, gv_ref = take(4)
    g_refs = take(2 if small_grid() else len(q_qkv))
    w, g, rows_all, sums, sem_w, sem_g, sem_o = refs
    pos = [pos_ref[at] for at in range(3)]
    place = pos_ref[3]
    loads = copies_in(pos, p_qkv, w_refs, w, sem_w)
    for copy in loads:
        copy.start()
    targets = [g_refs[at % 2] if small_grid() else g_refs[at] for at in range(len(q_qkv))]
    passed = []
    for piece, source, ref in zip(q_out, o_refs, targets):
        for k in range(piece.blocks):
            passed.append(pltpu.make_async_copy(source.at[k], piece.part(ref, k), sem_o.at[len(passed)]))
            passed[-1].start()
    weight = row_weights(jnp.where(place == 0, 1.0, 0.0))
    d_query = jnp.concatenate([dq0_ref[...], dq1_ref[...]], axis=1)
    d_query_w = wide(d_query) * weight
    gv_ref[2:3] = col_sum(d_query_w)
    g[:, :D] = dot_first(nl_ref[...], d_query_w.astype(BF16)).astype(BF16)

    half = D // 2
    for at, (dk_ref, dv_ref) in enumerate(((dk0_ref, dv0_ref), (dk1_ref, dv1_ref))):
        g[:, D + at * half : D + (at + 1) * half] = dot_first(na_ref[...], dk_ref[...]).astype(BF16)
        g[:, 2 * D + at * half : 2 * D + (at + 1) * half] = dot_first(na_ref[...], dv_ref[...]).astype(BF16)

    stores = copies_out(pos, q_qkv, targets, g, sem_g)
    for copy in stores:
        copy.start()
    for copy in loads:
        copy.wait()
    sums[...] = jnp.zeros((8, D), F32)

    @pl.loop(0, NK // 384)
    def _(at):
        rows = pl.ds(pl.multiple_of(at * 384, 128), 384)
        d_key = jnp.concatenate([dk0_ref[rows], dk1_ref[rows]], axis=1)
        d_value = jnp.concatenate([dv0_ref[rows], dv1_ref[rows]], axis=1)
        d_norm = dot_last(d_key, w[:, D : 2 * D]) + dot_last(d_value, w[:, 2 * D :])
        rows_all[rows] = d_norm
        unit = unit_of(wide(xa_ref[rows]))[0]
        sums[0:1] += col_sum(d_norm * unit)
        sums[1:2] += col_sum(d_norm)
        sums[2:3] += col_sum(wide(d_value))

    d_local = dot_last(d_query, w[:, :D])
    d_local_w = d_local * weight
    unit = unit_of(wide(xl_ref[...]))[0]
    gv_ref[0:1] = sums[0:1] + col_sum(d_local_w * unit)
    gv_ref[1:2] = sums[1:2] + col_sum(d_local_w)
    gv_ref[3:4] = sums[2:3]
    gv_ref[4:8] = jnp.zeros((4, D), F32)
    class_a = rows_all[PAT_A : PAT_A + 8][:1]
    class_b = [rows_all[KA + i * KB + BLK_B : KA + i * KB + BLK_B + 8][:1] for i in range(IMB)]
    row_b = lax.broadcasted_iota(jnp.int32, (QB, 1), 0)

    zh, zl = place // 2, place % 2

    def block_of(at):
        part_a = rows_all[pl.ds(pl.multiple_of(at * BLK_A, BLK_A), BLK_A)]
        parts = [part_a]
        for i in range(IMB):
            part = rows_all[pl.ds(pl.multiple_of(KA + i * KB + at * QB, QB), QB)]
            part = jnp.where(row_b == BLK_B, class_b[i], part)
            part = jnp.where(row_b == BLK_B + 1, class_a, part) if i == 0 else part
            parts.append(part)
        return parts

    for step in (0, 1):
        high = zh if step == 0 else 1 - zh
        send_ref[step] = jnp.concatenate(block_of(high * 2 + 1 - zl), axis=0).astype(BF16)
    keep_ref[...] = jnp.concatenate(block_of((1 - zh) * 2 + zl), axis=0)
    own = block_of(place)
    local_ref[:BLK_A] = own[0] + d_local[:BLK_A]
    local_ref[BLK_A : BLK_A + 16] = jnp.concatenate(
        [own[1][BLK_B + 1 : BLK_B + 2] + d_local[BLK_A : BLK_A + 1], jnp.zeros((15, D), F32)], axis=0
    )
    for i in range(IMB):
        at = QA + i * QB
        local_ref[at : at + QB] = own[1 + i] + d_local[at : at + QB]
    for copy in stores + passed:
        copy.wait()


def back(pos, first, second, normed_all, normed_loc, x_all, x_loc, arrays, pieces, g_out):
    q_qkv, q_out = grad_pieces(D, 3 * D, "split"), grad_pieces(D, D, "split")
    width = q_qkv[0].cols
    joint = [(1, D, 2 * D)] * 2
    if small_grid():
        joint = [(8, D // 8, 2 * D)] * 2
        for at in range(4):
            q_qkv[at].first = q_out[at].first = at // 2 * 4
    for piece in q_out:
        piece.src = width
    shapes = [((NQ, D), F32), ((BLOCK, D), F32), ((2, BLOCK, D), BF16), ((8, D), F32)]
    outs = pl.pallas_call(
        functools.partial(back_kernel, pieces, q_qkv, q_out),
        in_specs=[SSPEC] + [VSPEC] * 10 + [ANYSPEC] * len(arrays) + [VSPEC] * len(g_out),
        out_specs=[VSPEC] * 4 + [ANYSPEC] * 2,
        out_shape=[jax.ShapeDtypeStruct(*each) for each in shapes]
        + [jax.ShapeDtypeStruct(shape, BF16) for shape in joint],
        scratch_shapes=[
            pltpu.VMEM((D, 3 * D), BF16),
            pltpu.VMEM((D, 3 * D), BF16),
            pltpu.VMEM((NK, D), F32),
            pltpu.VMEM((8, D), F32),
            pltpu.SemaphoreType.DMA((piece_count(pieces),)),
            pltpu.SemaphoreType.DMA((piece_count(q_qkv),)),
            pltpu.SemaphoreType.DMA((piece_count(q_out),)),
        ],
        compiler_params=params(24),
        cost_estimate=cost(4 * D * D * (NQ + 2 * NK), 20e6),
        name="back",
    )(pos, *first, *second, normed_all, normed_loc, x_all, x_loc, *arrays, *g_out)
    return outs[:4], list(outs[4:])


def finish_kernel(dres_ref, local_ref, r1_ref, r2_ref, x_ref, vec_ref, ga_ref, gca_ref, gb_ref, gcb_ref):
    gain = vec_ref[0:1]

    def rows_of(at, count, got_at):
        grad = local_ref[at : at + count]
        grad = grad + wide(r1_ref[0, got_at : got_at + count]) + wide(r2_ref[got_at : got_at + count])
        unit, inv_std = unit_of(wide(x_ref[at : at + count]))
        return dres_ref[at : at + count] + norm_back(grad, unit, inv_std, gain)

    ga_ref[0] = rows_of(0, BLK_A, 0)
    for i in range(IMB):
        at = QA + i * QB
        rows = rows_of(at, QB, BLK_A + i * QB)
        gb_ref[i] = rows[:BLK_B]
        gcb_ref[i : i + 1] = rows[BLK_B : BLK_B + 1]
    grad = local_ref[BLK_A : BLK_A + 16]
    spot = BLK_A + 48
    grad = grad + wide(r1_ref[0, spot : spot + 16])[9:10] + wide(r2_ref[spot : spot + 16])[9:10]
    unit, inv_std = unit_of(wide(x_ref[BLK_A : BLK_A + 16]))
    rows = dres_ref[BLK_A : BLK_A + 16] + norm_back(grad, unit, inv_std, gain)
    gca_ref[...] = rows[:1]


def finish(d_resid, local, got, x_loc, vec):
    return pl.pallas_call(
        finish_kernel,
        in_specs=[VSPEC] * 6,
        out_specs=[VSPEC] * 4,
        out_shape=[
            jax.ShapeDtypeStruct((IMA, BLK_A, D), F32),
            jax.ShapeDtypeStruct((IMA, D), F32),
            jax.ShapeDtypeStruct((IMB, BLK_B, D), F32),
            jax.ShapeDtypeStruct((IMB, D), F32),
        ],
        compiler_params=params(),
        cost_estimate=cost(1e6, 6e6),
        name="finish",
    )(d_resid, local, *got, x_loc, vec)


def add_kernel(counts, *refs):
    ins, outs = refs[: sum(counts)], refs[sum(counts) :]
    at = 0
    for count, out in zip(counts, outs):
        total = wide(ins[at][...])
        for ref in ins[at + 1 : at + count]:
            total = total + wide(ref[...])
        out[...] = total.astype(BF16)
        at += count


def add_blocks(*groups):
    steps = 3
    specs, arrays, outs, shapes = [], [], [], []
    for group in groups:
        for array, first, count in group:
            rows, cols = array.shape[1:]
            specs.append(
                pl.BlockSpec((count, rows, cols // steps), lambda i, at=first // count: (at, 0, i))
            )
            arrays.append(array)
        outs.append(pl.BlockSpec((count, rows, cols // steps), lambda i: (0, 0, i)))
        shapes.append(jax.ShapeDtypeStruct((count, rows, cols), BF16))
    return pl.pallas_call(
        functools.partial(add_kernel, [len(group) for group in groups]),
        grid=(steps,),
        in_specs=specs,
        out_specs=outs,
        out_shape=shapes,
        compiler_params=params(),
        cost_estimate=cost(1, 1),
        name="add_blocks",
    )(*arrays)


def split_kernel(counts, zl_ref, *refs):
    ins, (send, kept) = refs[: sum(counts)], refs[sum(counts) :]
    first = zl_ref[0] == 0
    sums, at = [], 0
    for count in counts:
        total = wide(ins[at][0])
        for ref in ins[at + 1 : at + count]:
            total = total + wide(ref[0])
        sums.append(total)
        at += count
    groups = []
    for z in range(4):
        parts = []
        for total in sums:
            rows = total.shape[0] // 4
            part = total[z * rows : (z + 1) * rows]
            if rows > 24:
                part = jnp.concatenate([part[at : at + 24] for at in range(0, rows, 24)], axis=1)
            parts.append(part)
        axis = 1 if sums[0].shape == sums[1].shape else 0
        groups.append(jnp.concatenate(parts, axis=axis))
    for zh in range(2):
        one, two = groups[2 * zh], groups[2 * zh + 1]
        send[zh] = jnp.where(first, two, one).astype(BF16)
        kept[zh] = jnp.where(first, one, two)


def split_blocks(zl, rows, *groups):
    specs, arrays = [], []
    for group in groups:
        for array, first in group:
            specs.append(pl.BlockSpec((1,) + array.shape[1:], lambda i, at=first: (at, 0, 0)))
            arrays.append(array)
    shape = (2, rows, FF)
    return pl.pallas_call(
        functools.partial(split_kernel, [len(group) for group in groups]),
        grid=(1,),
        in_specs=[SSPEC] + specs,
        out_specs=[pl.BlockSpec(shape, lambda i: (0, 0, 0))] * 2,
        out_shape=[jax.ShapeDtypeStruct(shape, BF16), jax.ShapeDtypeStruct(shape, F32)],
        compiler_params=params(),
        cost_estimate=cost(1, 1),
        name="split_blocks",
    )(zl[None], *arrays)


def half_kernel(zh_ref, kept_ref, got_ref, send, keep):
    zh = zh_ref[0]
    send[...] = (kept_ref[1 - zh] + wide(got_ref[1 - zh])).astype(BF16)
    keep[...] = kept_ref[zh] + wide(got_ref[zh])


def half_blocks(zh, kept, got):
    return pl.pallas_call(
        half_kernel,
        in_specs=[SSPEC, VSPEC, VSPEC],
        out_specs=[VSPEC] * 2,
        out_shape=[jax.ShapeDtypeStruct(kept.shape[1:], BF16), jax.ShapeDtypeStruct(kept.shape[1:], F32)],
        compiler_params=params(),
        cost_estimate=cost(1, 1),
        name="half_blocks",
    )(zh[None], kept, got)


def pad_to(values, width):
    return jnp.pad(values, ((0, width - values.shape[0]),))


def nesterov(master, moment, average, grad_w, step_rate):
    moment_new = 0.5 * moment + grad_w
    master_new = master - step_rate * (grad_w + 0.5 * moment_new)
    return (master_new, moment_new, 0.5 * average + 0.5 * master_new)


def pair_up(value, other, axis):
    first = lax.axis_index(axis) == 0
    return jnp.stack([jnp.where(first, value, other), jnp.where(first, other, value)])


def across(mine, other):
    first = lax.axis_index("zl") == 0
    return jnp.stack([jnp.where(first, mine, other), jnp.where(first, other, mine)], axis=1)


def zl_parts(block):
    cut = block.reshape(2, 2, block.shape[0] // 4, block.shape[1])
    zl = lax.axis_index("zl")
    send = lax.dynamic_index_in_dim(cut, 1 - zl, 1, keepdims=False).astype(BF16)
    return send, lax.dynamic_index_in_dim(cut, zl, 1, keepdims=False)


def zh_parts(kept, got):
    zh = lax.axis_index("zh")
    both = kept + wide(got)
    send = lax.dynamic_index_in_dim(both, 1 - zh, 0, keepdims=False).astype(BF16)
    return send, lax.dynamic_index_in_dim(both, zh, 0, keepdims=False)


def sum_z(block):
    send, kept = zl_parts(block)
    send, kept = zh_parts(kept, swap(send, "zl"))
    return kept + wide(swap(send, "zh"))


def tick(*values):
    return lax.optimization_barrier(values)


def pack_kernel(xa_ref, xca_ref, xb_ref, xcb_ref, ca_ref, cca_ref, cb_ref, ccb_ref, x_ref, cot_ref, send_ref):
    def lay(rows_a, class_a, rows_b, class_b):
        zero = jnp.zeros((16, D), F32)
        parts = [wide(rows_a[0]), wide(class_a[...]), zero[: QA - BLK_A - 1]]
        for i in range(IMB):
            parts += [wide(rows_b[i]), wide(class_b[i : i + 1]), zero[: QB - BLK_B - 1]]
        return jnp.concatenate(parts, axis=0).astype(BF16)

    rows = lay(xa_ref, xca_ref, xb_ref, xcb_ref)
    x_ref[...] = rows
    send_ref[:BLK_A] = rows[:BLK_A]
    send_ref[BLK_A:] = rows[QA:]
    cot_ref[...] = lay(ca_ref, cca_ref, cb_ref, ccb_ref)


def pack(*rows):
    return pl.pallas_call(
        pack_kernel,
        in_specs=[VSPEC] * 8,
        out_specs=[VSPEC] * 3,
        out_shape=[jax.ShapeDtypeStruct((count, D), BF16) for count in (NQ, NQ, BLOCK)],
        compiler_params=params(),
        cost_estimate=cost(1e6, 2e6),
        name="pack",
    )(*rows)


LEFT = 3 * D // 2 + D // 2


def body(
    patches_a, class_a, patches_b, class_b, count_a, count_b, index_a, index_b,
    cot_a, cot_class_a, cot_b, cot_class_b,
    qkv_weight, qkv_momentum, qkv_average, out_weight, out_momentum, out_average,
    up_weight, up_momentum, up_average, down_weight, down_momentum, down_average,
    table_weight, table_momentum, table_average, vector_weight, vector_momentum, vector_average,
):
    zh, zl = lax.axis_index("zh"), lax.axis_index("zl")
    place = zh * 2 + zl
    devices = lax.axis_size(AXES)
    n0, n1, nc = [lax.axis_size(axis) for axis in AXES[:3]]
    pos = jnp.stack([lax.axis_index("d0"), lax.axis_index("d1"), lax.axis_index("c"), place]).astype(jnp.int32)
    counts = jnp.concatenate([count_a, count_b, jnp.zeros((1,), jnp.int32)])

    grid = small_grid()
    t_rows, v_len = table_weight.shape[0], vector_weight.shape[0]
    small = jnp.concatenate([table_weight.reshape(-1), vector_weight])
    small = pad_to(small, qkv_weight.shape[0] * 128).reshape(-1, 128)
    half, part = 3 * D // 2, D // 2
    qkv = jnp.concatenate(
        [qkv_weight[:, :half], out_weight[:, :part], qkv_weight[:, half:], out_weight[:, part:], small], axis=1
    ).astype(BF16)

    q_one = swap(qkv, "zh")
    up, down = up_weight.astype(BF16), down_weight.astype(BF16)
    x_loc, cot, message = pack(patches_a, class_a, patches_b, class_b, cot_a, cot_class_a, cot_b, cot_class_b)
    q_one, up, down, x_loc, cot, message = tick(q_one, up, down, x_loc, cot, message)

    q_pair, up = tick(pair_up(qkv, q_one, "zh"), up)
    q_two, u_one = swap(q_pair, "zl"), swap(up, "zh")
    q_two, u_one = tick(q_two, u_one)

    q_block = across(q_pair, q_two).reshape(-1, qkv.shape[1])
    left, right = q_block[:, :LEFT], q_block[:, LEFT:]
    u_pair = pair_up(up, u_one, "zh")
    left, right, u_pair, down, index_a, index_b = tick(left, right, u_pair, down, index_a, index_b)
    if grid:
        l_one, r_one = swap(left, "d0"), swap(right, "d1")
    u_two, d_one = swap(u_pair, "zl"), swap(down, "zh")
    ids = all_ids(pos, index_a, index_b)
    if grid:
        l_one, r_one, u_two, d_one, ids = tick(l_one, r_one, u_two, d_one, ids)
        l_two, r_two = jnp.stack([left, l_one]), jnp.stack([right, r_one])
    else:
        u_two, d_one, ids = tick(u_two, d_one, ids)
        l_two, r_two = left, right
    d_pair = pair_up(down, d_one, "zh")
    l_two, r_two, d_pair, message = tick(l_two, r_two, d_pair, message)
    if grid:
        l_far, r_far = swap(l_two, "d1"), swap(r_two, "d0")
    d_two, x_one = swap(d_pair, "zl"), swap(message, "zh")
    u_block = across(u_pair, u_two).reshape(-1, FF)
    if grid:
        l_far, r_far, d_two, x_one, u_block = tick(l_far, r_far, d_two, x_one, u_block)
        l_four, r_four = jnp.concatenate([l_two, l_far]), jnp.concatenate([r_two, r_far])
    else:
        d_two, x_one, u_block = tick(d_two, x_one, u_block)
        l_four, r_four = left, right
    d_block = across(d_pair, d_two).reshape(-1, D)
    x_pair = pair_up(message, x_one, "zh")
    l_four, r_four, u_block, d_block, x_pair = tick(l_four, r_four, u_block, d_block, x_pair)
    if grid:
        rights = [r_four, swap(r_four, "c")]
        lefts = [l_four, swap(l_four, "c")]
        u_near, d_near = swap(u_block, "d0"), swap(d_block, "d1")
    else:
        lefts, rights = [gather_whole(left)], [gather_whole(right)]
    x_two = swap(x_pair, "zl")
    rows = q_block.shape[0]
    qkv_w = (
        lefts + rights,
        weight_pieces("x", rows, half) + weight_pieces("y", rows, half, half),
    )
    out_w = (
        lefts + rights,
        weight_pieces("x", rows, part, 0, half) + weight_pieces("y", rows, part, part, half),
    )

    small = wide(small_part(rights, LEFT))
    table_t = jnp.transpose(small[:, : t_rows * HEADS].reshape(TABLE, HEADS))
    vector = small[:, t_rows * HEADS : t_rows * HEADS + v_len].reshape(-1)
    vec = jnp.pad(vector[: 10 * D].reshape(10, D), ((0, 6), (0, 0)))
    b1 = vector[10 * D :].reshape(FF // STEP, STEP)
    ids_a, ids_b, ids_fold = ids
    strip = lookup(table_t, ids_a)
    cols = jnp.transpose(strip[:, SIDE_A + 1, :QA].reshape(HEADS // 2, 2, QA), (0, 2, 1))
    cols = jnp.pad(cols, ((0, 0), (0, 0), (0, 126)))

    if grid:
        u_near, d_near, strip, cols = tick(u_near, d_near, strip, cols)
        u_pair, d_pair, table_t = tick(jnp.stack([u_block, u_near]), jnp.stack([d_block, d_near]), table_t)
        u_far, d_far = swap(u_pair, "d1"), swap(d_pair, "d0")
        ups, downs = [u_pair, None, swap(u_pair, "c"), None], [d_pair, None, swap(d_pair, "c"), None]
    bias_b = lookup(table_t, ids_b)
    if grid:
        x_two, bias_b = tick(x_two, bias_b)
    queries, keys, values, normed_all, normed_loc, x_all = project(pos, x_pair, x_two, x_loc, vec, *qkv_w)
    mixed, probs_a, probs_b = attend(counts, queries, keys, values, cols, strip, bias_b)
    if grid:
        ups[2], downs[2], u_far, d_far, mixed = tick(ups[2], downs[2], u_far, d_far, mixed)
        ups[1], downs[1] = u_far, d_far
        ups[3], downs[3] = swap(u_far, "c"), swap(d_far, "c")
    else:
        ups, downs = [gather_whole(u_block)], [gather_whole(d_block)]
    up_w = (ups, weight_pieces("x", rows, FF, pairs=True))
    down_w = (downs, weight_pieces("y", d_block.shape[0], D, pairs=True))
    plain, g_out, g_up, g_down = feed(
        pos, counts, mixed, x_loc, cot, vec, b1, (out_w, up_w, down_w), ("split", "x", "y"),
    )
    finals, (d_resid, d_mixed, gv_feed, gb_feed) = plain[:4], plain[4:]
    att = (queries, keys, values, probs_a, probs_b)
    grads = {}
    if grid:
        d_mixed, g_up, g_down, g_out = tick(d_mixed, g_up, g_down, g_out)
        u_core, d_core = swap(g_up[1], "c"), swap(g_down[1], "c")
        first = attend_back(pos[3:], 0, d_mixed, *att)
        u_core, d_core, first = tick(u_core, d_core, first)
        u_send, d_send, d_mixed, first = tick(
            far_part(g_up[0], u_core), far_part(g_down[0], d_core), d_mixed, first
        )
        u_far, d_far = swap(u_send, "d1"), swap(d_send, "d0")
    else:
        first = attend_back(pos[3:], 0, d_mixed, *att)
    second = attend_back(pos[3:], 1, d_mixed, *att)
    (local, keep, send, gv_back), g_qkv = back(
        pos, first[:3], second[:3], normed_all, normed_loc, x_all, x_loc, *qkv_w, g_out
    )
    folded = (first[3], second[3])
    if grid:
        u_far, d_far, send, g_qkv, gv_back, folded, keep = tick(u_far, d_far, send, g_qkv, gv_back, folded, keep)
        came = swap(send, "zl")
        q_core = swap(g_qkv[1], "c")
        u_send, d_send = near_part(g_up[0], u_core, u_far), near_part(g_down[0], d_core, d_far)
        u_near, d_near = swap(u_send, "d0"), swap(d_send, "d1")
        q_core, u_send, d_send = tick(q_core, u_send, d_send)
        l_own, r_own, l_core, r_core = g_qkv[0][:4], g_qkv[0][4:], q_core[:4], q_core[4:]
        l_send, r_send, folded, gv_back = tick(far_part(l_own, l_core), far_part(r_own, r_core), folded, gv_back)
        l_far, r_far = swap(l_send, "d1"), swap(r_send, "d0")
    else:
        came = swap(send, "zl")

    gt = gt_first = table_grad(*folded, ids_fold)
    gv = jnp.concatenate([gv_back[:4].reshape(-1), gv_feed[:6].reshape(-1), gb_feed.reshape(-1)])
    gt = jnp.transpose(gt[:HEADS]).reshape(devices, t_rows * HEADS)
    small_grad = jnp.concatenate([gt, gv.reshape(devices, v_len)], axis=1)
    small_len = (small_grad.shape[1] + 2047) // 2048 * 2048
    small_grad = jnp.pad(small_grad, ((0, 0), (0, small_len - small_grad.shape[1])))
    small_grad = small_grad.astype(BF16).reshape(n0, n1, nc, 2, 2, -1, 128)

    if grid:
        came, gt_first = tick(came, gt_first)
        came_send = (keep + wide(came[1])).astype(BF16)
        came_far = swap(came_send, "zh")
        u_near, d_near, came_send, small_grad = tick(u_near, d_near, came_send, small_grad)
        send, kept = split_blocks(
            zl, 48,
            [(g_up[0], 0), (u_core, 0), (u_far, 0), (u_near[None], 0)],
            [(g_down[0], 0), (d_core, 0), (d_far, 0), (d_near[None], 0)],
        )
        z_got = swap(send, "zl")
        small_grad = scatter_axis(small_grad, "d0").astype(BF16)
        l_far, r_far, send, small_grad = tick(l_far, r_far, send, small_grad)
        l_send, r_send = near_part(l_own, l_core, l_far), near_part(r_own, r_core, r_far)
        l_near, r_near = swap(l_send, "d0"), swap(r_send, "d1")
        small_grad = scatter_axis(small_grad, "d1").astype(BF16)
        l_near, r_near, z_got, small_grad = tick(l_near, r_near, z_got, small_grad)
        send, kept = half_blocks(zh, kept, z_got)
        z_far = swap(send, "zh")
        q_send, q_kept = split_blocks(
            zl, 24,
            [(g_qkv[0], 0), (q_core, 0), (l_far, 0), (l_near[None], 0)],
            [(g_qkv[0], 4), (q_core, 4), (r_far, 0), (r_near[None], 0)],
        )
        q_got = swap(q_send, "zl")
        small_grad = scatter_axis(small_grad, "c").astype(BF16).reshape(4, -1)
        d_rows = finish(d_resid, local, (came, came_far), x_loc, vec)
        q_got, z_far, small_grad, d_rows = tick(q_got, z_far, small_grad, d_rows)
        q_send, q_kept = half_blocks(zh, q_kept, q_got)
        grads["q"] = q_kept + wide(swap(q_send, "zh"))
        small_total = wide(lax.dynamic_index_in_dim(small_grad, place, 0, keepdims=False))
        for at in range(1, 4):
            outgoing = lax.dynamic_index_in_dim(small_grad, (place + at) % 4, 0, keepdims=False)
            small_total = small_total + wide(lax.ppermute(outgoing, ("zh", "zl"), shift_perm(4, at)))
        small_grad = small_total
        both = kept + wide(z_far)
        grads["up"] = both[: both.shape[0] // 2]
        grads["down"] = unside(both[both.shape[0] // 2 :])
    else:
        came_far = swap((keep + wide(came[1])).astype(BF16), "zh")
        for name, arrays in (("up", g_up), ("down", g_down)):
            grads[name] = sum_z(whole_grid_sum(arrays[0]))
        grads["q"] = sum_z(whole_grid_sum(jnp.concatenate(g_qkv, axis=2)))
        for axis in AXES:
            small_grad = scatter_axis(small_grad, axis)
            small_grad = small_grad if axis == "zl" else small_grad.astype(BF16)
        d_rows = finish(d_resid, local, (came, came_far), x_loc, vec)
    joint = grads["q"]
    grads["qkv"] = jnp.concatenate([joint[:, :half], joint[:, LEFT : LEFT + half]], axis=1)
    grads["out"] = jnp.concatenate([joint[:, half:LEFT], joint[:, LEFT + half :]], axis=1)
    small_grad = small_grad.reshape(-1)
    grads["table"] = small_grad[: t_rows * HEADS].reshape(t_rows, HEADS)
    grads["vector"] = small_grad[t_rows * HEADS : t_rows * HEADS + v_len]
    rows_all = (IMA * (PAT_A + 1) + IMB * (PAT_B + 1)) * (devices // 4)
    states = (
        ("qkv", qkv_weight, qkv_momentum, qkv_average),
        ("out", out_weight, out_momentum, out_average),
        ("up", up_weight, up_momentum, up_average),
        ("down", down_weight, down_momentum, down_average),
        ("table", table_weight, table_momentum, table_average),
        ("vector", vector_weight, vector_momentum, vector_average),
    )
    updated = []
    for (name, *state), rate in zip(states, STEP_RATES):
        updated += nesterov(*state, grads[name], rate / math.sqrt(rows_all))
    return (*finals, *d_rows, *updated)


def solution(mesh):
    dp, seq = mesh.devices.shape
    split = Mesh(mesh.devices.reshape(dp // 4, 2, 2, seq // 2, 2), AXES)
    dp_axes = ("d0", "d1", "c")
    rows = P(dp_axes, ("zh", "zl"), None)
    classes = P(dp_axes, None)
    shard = P(AXES, None)
    vec = P(AXES)
    return jax.shard_map(
        body,
        mesh=split,
        in_specs=(
            rows, classes, rows, classes, P(dp_axes), P(dp_axes), P(), P(), rows, classes, rows, classes,
            *([shard] * 15), *([vec] * 3),
        ),
        out_specs=(rows, classes, rows, classes, rows, classes, rows, classes, *([shard] * 15), *([vec] * 3)),
        check_vma=False,
    )
```
